32 devices in a mesh: seq: 4 (over y, x), batch: 8 (over z, core).
Axes of the slice: x: 2, y: 2, z: 4, core: 2. Of those that a mesh axis runs over, the one named last changes fastest.
Arguments:
- inputs: bfloat16 [8, 1024, 768], P('batch', 'seq'), may hold values from -6 to 6
- norm_gain: float32 [2, 2, 768], replicated, may hold values from 0.25 to 1.75
- norm_bias: float32 [2, 2, 768], replicated, may hold values from -3 to 3
- w_in: bfloat16 [2, 768, 3072], replicated, may hold values from -0.21875 to 0.21875
- b_in: float32 [2, 3072], replicated, may hold values from -4 to 4
- w_out: bfloat16 [2, 3072, 768], replicated, may hold values from -0.109375 to 0.109375
- b_out: float32 [2, 768], replicated, may hold values from -3 to 3
- cotangent: float32 [8, 1024, 768], P('batch', 'seq'), may hold values from -6 to 6
Outputs:
- outputs: float32 [8, 1024, 768], P('batch', 'seq')
- input_grad: float32 [8, 1024, 768], P('batch', 'seq')
- norm_gain_grad: float32 [2, 2, 768], replicated
- norm_bias_grad: float32 [2, 2, 768], replicated
- w_in_grad: float32 [2, 768, 3072], P(None, None, ('seq', 'batch'))
- b_in_grad: float32 [2, 3072], replicated
- w_out_grad: float32 [2, 3072, 768], P(None, ('seq', 'batch'))
- b_out_grad: float32 [2, 768], replicated
The draws below stay inside these ranges and needn't reach their ends.
All inputs are finite; a program needn't handle non-finite values.
Results may differ from the reference program's by a relative error of at most 0.01.
Values may be sent and summed in bfloat16 or wider, within the bound.
No kernel may reach another device: no remote copies, remote signals or barrier semaphores. Data moves between devices by JAX's collectives and lax.ppermute only.
A program may use at most 192 MiB of HBM per device.

```python
import math
import jax
import jax.numpy as jnp
from jax import lax

D = 768
FF = 3072
LAYERS = 2
LEN = 1024
SEQS = 8


def block_levels(own_key, dims, shards, smallest, top_value):
    factor_of = 1.0
    for dim, blocks in shards:
        draws = jax.random.uniform(jax.random.fold_in(jax.random.fold_in(own_key, 6), dim), (blocks,), jnp.float32, smallest / len(shards), top_value / len(shards))
        factor_of = factor_of * jnp.repeat(jnp.exp(draws), dims[dim] // blocks).reshape((-1,) + (1,) * (len(dims) - 1 - dim))
    return factor_of


def noise(rng, dims, spread, bound, shards=(), kind=jnp.bfloat16):
    factor_of = block_levels(rng, dims, shards, -0.22, 0.18) if shards else 1.0
    array = jax.random.normal(rng, dims, jnp.float32) * spread * factor_of
    return jnp.minimum(jnp.maximum(array, -bound), bound).astype(kind)


def setup_inputs(seed: int = 0) -> dict:
    streams_of = jax.random.split(jax.random.key(seed), 9)
    return {
        "inputs": noise(streams_of[0], (SEQS, LEN, D), 1.0, 6.0, ((0, 8), (1, 4))),
        "norm_gain": jnp.clip(1.0 + 0.15 * jax.random.normal(streams_of[1], (LAYERS, 2, D), jnp.float32), 0.25, 1.75),
        "norm_bias": noise(streams_of[2], (LAYERS, 2, D), 0.3, 3.0, (), jnp.float32),
        "w_in": noise(streams_of[3], (LAYERS, D, FF), D ** -0.5, 0.21875),
        "b_in": noise(streams_of[4], (LAYERS, FF), 0.5, 4.0, (), jnp.float32),
        "w_out": noise(streams_of[5], (LAYERS, FF, D), FF ** -0.5, 0.109375),
        "b_out": noise(streams_of[6], (LAYERS, D), 0.3, 3.0, (), jnp.float32),
        "cotangent": noise(streams_of[7], (SEQS, LEN, D), 1.0, 6.0, ((0, 8), (1, 4)), jnp.float32),
    }


eps_norm = 1e-05
highest_prec = lax.Precision.HIGHEST

@jax.custom_vjp
def low(v):
    return lax.optimization_barrier(v.astype(jnp.bfloat16)).astype(jnp.float32)

@jax.custom_vjp
def low_back(v):
    return v

def low_keep(v):
    return (low(v), None)

def low_pass(kept, grad):
    return (grad,)

def back_keep(v):
    return (v, None)

def back_low(kept, grad):
    return (low(grad),)
low.defvjp(low_keep, low_pass)
low_back.defvjp(back_keep, back_low)

def dft_tables(modulus):
    ids = jnp.arange(modulus, dtype=jnp.int32)
    product = ids[:, None] * ids[None, :] % modulus
    angles = product.astype(jnp.float32) * (2.0 * math.pi / modulus)
    return (low(jnp.cos(angles)), low(jnp.sin(angles)))

def matmul(left, right):
    return jnp.dot(left, right, precision=highest_prec, preferred_element_type=jnp.float32)

def layer_norm(values, gain_vec, bias_vec):
    centered = values - lax.optimization_barrier(jnp.mean(values, axis=-1, keepdims=True))
    variance = lax.optimization_barrier(jnp.mean(centered * centered, axis=-1, keepdims=True))
    return centered * lax.rsqrt(variance + eps_norm) * gain_vec + bias_vec

def fnet_layer(state, gains, biases, weight_in, bias_in, weight_out, bias_out, tables):
    cos_seq, sin_seq, cos_hid, sin_hid, dft_scale = tables
    flat_in = low(state)
    spec_cos = low(low_back(matmul(flat_in, cos_hid) * dft_scale))
    spec_sin = low(low_back(matmul(flat_in, sin_hid) * dft_scale))
    mixed = low_back(matmul(cos_seq, spec_cos) - matmul(sin_seq, spec_sin))
    hidden = layer_norm(state + mixed, gains[0], biases[0])
    pre_act = low_back(matmul(low(hidden), weight_in) + bias_in)
    activation = low(jax.nn.gelu(pre_act))
    branch = low_back(matmul(activation, weight_out) + bias_out)
    return layer_norm(hidden + branch, gains[1], biases[1])

def reference(inputs, norm_gain, norm_bias, w_in, b_in, w_out, b_out, cotangent):
    length = inputs.shape[1]
    width = inputs.shape[2]
    cos_seq, sin_seq = dft_tables(length)
    cos_hid, sin_hid = dft_tables(width)
    tables = (cos_seq, sin_seq, cos_hid, sin_hid, 1.0 / math.sqrt(length * width))
    params = (norm_gain, norm_bias, w_in.astype(jnp.float32), b_in, w_out.astype(jnp.float32), b_out)

    def forward(state, weights):
        gains, biases, weight_in, bias_in, weight_out, bias_out = weights
        for layer_id in range(weight_in.shape[0]):
            state = fnet_layer(state, gains[layer_id], biases[layer_id], weight_in[layer_id], bias_in[layer_id], weight_out[layer_id], bias_out[layer_id], tables)
        return state

    def one_sequence(totals, item):
        sequence, seq_cot = item
        result, pull = jax.vjp(forward, sequence.astype(jnp.float32), params)
        input_grad, weight_grads = pull(seq_cot.astype(jnp.float32))
        return (jax.tree.map(jnp.add, totals, weight_grads), (result, input_grad))
    zeros = jax.tree.map(jnp.zeros_like, params)
    totals, (results, input_grads) = lax.scan(one_sequence, zeros, (inputs, cotangent))
    return (results, input_grads, totals[0], totals[1], totals[2], totals[3], totals[4], totals[5])
```

```python
import math

import jax
import jax.numpy as jnp
import numpy as np
from jax import lax
from jax.sharding import PartitionSpec as P

eps_norm = 1e-05
bf16 = jnp.bfloat16
f32 = jnp.float32


def np_tables(modulus):
    ids = np.arange(modulus, dtype=np.int64)
    product = (ids[:, None] * ids[None, :]) % modulus
    angles = product.astype(np.float32) * np.float32(2.0 * math.pi / modulus)
    return np.cos(angles).astype(bf16), np.sin(angles).astype(bf16)


def seq_tables(length, seq_count):
    rows = length // seq_count
    cos_t, sin_t = np_tables(length)
    out = np.zeros((seq_count, 2 * rows, length), dtype=bf16)
    for s in range(seq_count):
        own = slice(s * rows, (s + 1) * rows)
        for m in range(seq_count):
            src = slice((s ^ m) * rows, ((s ^ m) + 1) * rows)
            dst = slice(m * rows, (m + 1) * rows)
            out[s, :rows, dst] = cos_t[own, src]
            out[s, rows:, dst] = sin_t[own, src]
    return out


def xor_send(value, axis, mask):
    size = lax.axis_size(axis)
    return lax.ppermute(value, axis, [(i, i ^ mask) for i in range(size)])


def gather_blocks(block):
    return [block] + [xor_send(block, "seq", m) for m in range(1, lax.axis_size("seq"))]


def layer_norm(values, gain_vec, bias_vec):
    centered = values - jnp.mean(values, axis=-1, keepdims=True)
    inv_std = lax.rsqrt(jnp.mean(centered * centered, axis=-1, keepdims=True) + eps_norm)
    normed = centered * inv_std
    return (normed * gain_vec + bias_vec, normed, inv_std)


def norm_back(upstream, normed, inv_std, gain_vec):
    gain_grad = jnp.sum(upstream * normed, axis=0)
    bias_grad = jnp.sum(upstream, axis=0)
    scaled = upstream * gain_vec
    inner = (
        scaled
        - jnp.mean(scaled, axis=-1, keepdims=True)
        - normed * jnp.mean(scaled * normed, axis=-1, keepdims=True)
    )
    return (inv_std * inner, gain_grad, bias_grad)


def gelu_both(z):
    k = math.sqrt(2.0 / math.pi)
    z2 = z * z
    t = jnp.tanh(k * z * (1.0 + 0.044715 * z2))
    half = 0.5 * (1.0 + t)
    slope = half + 0.5 * z * (1.0 - t * t) * (k * (1.0 + 3 * 0.044715 * z2))
    return z * half, slope


def dot(a, b, dims=((1,), (0,))):
    return lax.dot_general(a, b, (dims, ((), ())), preferred_element_type=f32)


def exchange_sum(part, axis_name, bit, dim, out_dtype):
    mine = (lax.axis_index(axis_name) >> bit) & 1
    keep = lax.dynamic_index_in_dim(part, mine, dim, keepdims=False)
    give = lax.dynamic_index_in_dim(part, 1 - mine, dim, keepdims=False)
    got = xor_send(give, axis_name, 1 << bit)
    return (keep.astype(f32) + got.astype(f32)).astype(out_dtype)


def scatter_sum(grad, flip):
    seq_bits = lax.axis_size("seq").bit_length() - 1
    batch_bits = lax.axis_size("batch").bit_length() - 1
    slots = seq_bits + batch_bits
    part = grad.reshape((2,) * slots + (-1, grad.shape[-1]))
    order = [("batch", 0)]
    seq_order = list(range(seq_bits))
    if flip:
        seq_order.reverse()
    order += [("seq", b) for b in seq_order]
    order += [("batch", b) for b in range(1, batch_bits)]
    dims = [("seq", b) for b in reversed(range(seq_bits))] + [("batch", b) for b in reversed(range(batch_bits))]
    for n, (axis_name, bit) in enumerate(order):
        dim = dims.index((axis_name, bit))
        dims.pop(dim)
        part = exchange_sum(part, axis_name, bit, dim, f32 if n == slots - 1 else bf16)
    return part


def all_sum(vec):
    for axis_name in ("batch", "seq"):
        for bit in range(lax.axis_size(axis_name).bit_length() - 1):
            vec = vec + xor_send(vec, axis_name, 1 << bit)
    return vec


def body(tables, hid_tables, inputs, norm_gain, norm_bias, w_in, b_in, w_out, b_out, cotangent):
    seq_count = lax.axis_size("seq")
    rows = inputs.shape[1]
    width = inputs.shape[2]
    length = rows * seq_count
    layers = w_in.shape[0]
    table = lax.dynamic_index_in_dim(jnp.asarray(tables), lax.axis_index("seq"), 0, keepdims=False)
    cos_hid, sin_hid = (jnp.asarray(t) for t in hid_tables)
    dft_scale = 1.0 / math.sqrt(length * width)

    def mix(block):
        pieces = jnp.concatenate(gather_blocks(block), axis=0)
        spec = (dot(table, pieces) * dft_scale).astype(bf16)
        return dot(spec[:rows], cos_hid) - dot(spec[rows:], sin_hid)

    state = inputs[0].astype(f32)
    stored = []
    for layer_id in range(layers):
        mixed = mix(state.astype(bf16))
        hidden, normed_mix, inv_mix = layer_norm(state + mixed, norm_gain[layer_id, 0], norm_bias[layer_id, 0])
        hidden_low = hidden.astype(bf16)
        act, slope = gelu_both(dot(hidden_low, w_in[layer_id]) + b_in[layer_id])
        act_low, slope = act.astype(bf16), slope.astype(bf16)
        branch = dot(act_low, w_out[layer_id]) + b_out[layer_id]
        state, normed_ff, inv_ff = layer_norm(hidden + branch, norm_gain[layer_id, 1], norm_bias[layer_id, 1])
        stored.append((hidden_low, slope, act_low, normed_mix, inv_mix, normed_ff, inv_ff))
    upstream = cotangent[0]
    win_out, wout_out, small_out = [None] * layers, [None] * layers, [None] * layers
    for layer_id in reversed(range(layers)):
        hidden_low, slope, act_low, normed_mix, inv_mix, normed_ff, inv_ff = stored[layer_id]
        resid_ff, gain_ff, bias_ff = norm_back(upstream, normed_ff, inv_ff, norm_gain[layer_id, 1])
        branch_grad = resid_ff.astype(bf16)
        bout = jnp.sum(branch_grad.astype(f32), axis=0)
        wout = dot(act_low, branch_grad, ((0,), (0,))).astype(bf16)
        pre_grad = (dot(branch_grad, w_out[layer_id], ((1,), (1,))) * slope.astype(f32)).astype(bf16)
        win = dot(pre_grad, hidden_low, ((0,), (0,))).astype(bf16)
        bin_ = jnp.sum(pre_grad.astype(f32), axis=0)
        hidden_grad = resid_ff + dot(pre_grad, w_in[layer_id], ((1,), (1,)))
        resid_mix, gain_mix, bias_mix = norm_back(hidden_grad, normed_mix, inv_mix, norm_gain[layer_id, 0])
        wout_out[layer_id] = scatter_sum(wout, False)
        win_out[layer_id] = scatter_sum(win, True).T
        small_out[layer_id] = all_sum(jnp.concatenate([gain_mix, gain_ff, bias_mix, bias_ff, bout, bin_]))
        upstream = resid_mix + mix(resid_mix.astype(bf16))
    small = jnp.stack(small_out)
    gains = small[:, : 2 * width].reshape(layers, 2, width)
    biases = small[:, 2 * width : 4 * width].reshape(layers, 2, width)
    bout = small[:, 4 * width : 5 * width]
    bin_ = small[:, 5 * width :]
    return (state[None], upstream[None], gains, biases, jnp.stack(win_out), bin_, jnp.stack(wout_out), bout)


def solution(mesh):
    def run(inputs, norm_gain, norm_bias, w_in, b_in, w_out, b_out, cotangent):
        tables = seq_tables(inputs.shape[1], mesh.shape["seq"])
        hid_tables = np_tables(inputs.shape[2])

        def inner(*args):
            return body(tables, hid_tables, *args)

        return jax.shard_map(
            inner,
            mesh=mesh,
            in_specs=(P("batch", "seq", None), P(), P(), P(), P(), P(), P(), P("batch", "seq", None)),
            out_specs=(
                P("batch", "seq", None),
                P("batch", "seq", None),
                P(),
                P(),
                P(None, None, ("seq", "batch")),
                P(),
                P(None, ("seq", "batch"), None),
                P(),
            ),
            check_vma=False,
        )(inputs, norm_gain, norm_bias, w_in, b_in, w_out, b_out, cotangent)

    return run
```

```python
import math

import jax
import jax.numpy as jnp
import numpy as np
from jax import lax
from jax.sharding import PartitionSpec as P

eps_norm = 1e-05
bf16 = jnp.bfloat16
f32 = jnp.float32


def parity_of(index):
    return bin(index).count("1") & 1


def np_tables(modulus):
    ids = np.arange(modulus, dtype=np.int64)
    product = (ids[:, None] * ids[None, :]) % modulus
    angles = product.astype(np.float32) * np.float32(2.0 * math.pi / modulus)
    return np.cos(angles).astype(bf16), np.sin(angles).astype(bf16)


def seq_tables(length, seq_count):
    rows = length // seq_count
    cos_t, sin_t = np_tables(length)
    ids = [
        np.concatenate([np.arange(t * rows, (t + 1) * rows) for t in range(seq_count) if parity_of(t) == c])
        for c in (0, 1)
    ]
    out = []
    for c in (0, 1):
        cols = np.concatenate([ids[c], ids[1 - c]])
        out.append(np.concatenate([t[ids[c]][:, cols] for t in (cos_t, sin_t)], axis=0))
    return np.stack(out)


class Place:
    def __init__(self):
        self.seq_count = lax.axis_size("seq")
        self.batch_count = lax.axis_size("batch")
        self.s = lax.axis_index("seq")
        self.core = lax.axis_index("batch") & 1
        bits = self.s
        for shift in (4, 2, 1):
            bits = bits ^ (bits >> shift)
        self.parity = bits & 1
        self.home = self.core == self.parity

    def send(self, value, pairs):
        n = self.batch_count
        full = [
            (s0 * n + 2 * z + c0, s1 * n + 2 * z + c1)
            for (s0, c0), (s1, c1) in pairs
            for z in range(n // 2)
        ]
        return lax.ppermute(value, ("seq", "batch"), full)

    def swap(self, value):
        return xor_send(value, "batch", 1)

    def collect(self, block):
        odd = [m for m in range(1, self.seq_count) if parity_of(m)]
        even = [m for m in range(1, self.seq_count) if not parity_of(m)]
        size = block.shape[0]
        buffer = jnp.zeros((size * self.seq_count // 2, block.shape[1]), block.dtype)

        def put(buffer, piece, block_id):
            return lax.dynamic_update_slice(buffer, piece, ((block_id >> 1) * size, 0))

        for n, mask in enumerate(odd):
            pairs = [((t, 1 - parity_of(t)), (t ^ mask, parity_of(t))) for t in range(self.seq_count)]
            ids = self.s ^ mask
            piece = None
            if n < len(even):
                pairs += [((t, parity_of(t)), (t ^ even[n], parity_of(t))) for t in range(self.seq_count)]
                ids = jnp.where(self.home, self.s ^ even[n], ids)
                piece = self.send(block, pairs)
            else:
                ids = jnp.where(self.home, self.s, ids)
                piece = jnp.where(self.home, block, self.send(block, pairs))
            buffer = put(buffer, piece, ids)
        return buffer

    def give_back(self, rows, size):
        local = lax.dynamic_slice(rows, ((self.s >> 1) * size, 0), (size, rows.shape[1]))
        pairs = [((t, 1 - parity_of(t)), (t ^ 1, parity_of(t))) for t in range(self.seq_count)]
        got = self.send(local.astype(bf16), pairs)
        return jnp.where(self.home, local, got.astype(f32))


def xor_send(value, axis, mask):
    size = lax.axis_size(axis)
    return lax.ppermute(value, axis, [(i, i ^ mask) for i in range(size)])


def layer_norm(values, gain_vec, bias_vec):
    centered = values - jnp.mean(values, axis=-1, keepdims=True)
    inv_std = lax.rsqrt(jnp.mean(centered * centered, axis=-1, keepdims=True) + eps_norm)
    normed = centered * inv_std
    return (normed * gain_vec + bias_vec, normed, inv_std)


def norm_back(upstream, normed, inv_std, gain_vec):
    gain_grad = jnp.sum(upstream * normed, axis=0)
    bias_grad = jnp.sum(upstream, axis=0)
    scaled = upstream * gain_vec
    inner = (
        scaled
        - jnp.mean(scaled, axis=-1, keepdims=True)
        - normed * jnp.mean(scaled * normed, axis=-1, keepdims=True)
    )
    return (inv_std * inner, gain_grad, bias_grad)


def gelu_both(z):
    k = math.sqrt(2.0 / math.pi)
    z2 = z * z
    t = jnp.tanh(k * z * (1.0 + 0.044715 * z2))
    half = 0.5 * (1.0 + t)
    slope = half + 0.5 * z * (1.0 - t * t) * (k * (1.0 + 3 * 0.044715 * z2))
    return z * half, slope


def dot(a, b, dims=((1,), (0,))):
    return lax.dot_general(a, b, (dims, ((), ())), preferred_element_type=f32)


def exchange_sum(part, axis_name, bit, dim, out_dtype):
    mine = (lax.axis_index(axis_name) >> bit) & 1
    keep = lax.dynamic_index_in_dim(part, mine, dim, keepdims=False)
    give = lax.dynamic_index_in_dim(part, 1 - mine, dim, keepdims=False)
    got = xor_send(give, axis_name, 1 << bit)
    return (keep.astype(f32) + got.astype(f32)).astype(out_dtype)


def slot_grad(place, left, right, mask):
    batch_bits = place.batch_count.bit_length() - 1
    span = left.shape[1] // place.seq_count

    def one(slot):
        cut = lax.dynamic_slice(left, (0, slot * span), (left.shape[0], span))
        return dot(cut, right, ((0,), (0,))).astype(bf16)

    part = jnp.stack([one(place.s), one(place.s ^ mask)])
    part = part.reshape((2,) + (2,) * batch_bits + (-1, right.shape[1]))
    part = exchange_sum(part, "batch", 0, batch_bits, bf16)
    part = (part[0].astype(f32) + xor_send(part[1], "seq", mask).astype(f32)).astype(bf16)
    for bit in range(1, batch_bits):
        part = exchange_sum(part, "batch", bit, batch_bits - 1 - bit, f32 if bit == batch_bits - 1 else bf16)
    return part


def all_sum(vec):
    vec = vec + xor_send(vec, "batch", 1)
    vec = vec + xor_send(vec, "seq", 1)
    for bit in range(1, lax.axis_size("batch").bit_length() - 1):
        vec = vec + xor_send(vec, "batch", 1 << bit)
    return vec


def body(tables, hid_tables, inputs, norm_gain, norm_bias, w_in, b_in, w_out, b_out, cotangent):
    place = Place()
    size = inputs.shape[1]
    width = inputs.shape[2]
    length = size * place.seq_count
    rows = length // 2
    layers = w_in.shape[0]
    table = lax.dynamic_index_in_dim(jnp.asarray(tables), place.core, 0, keepdims=False)
    cos_hid, sin_hid = (jnp.asarray(t) for t in hid_tables)
    dft_scale = 1.0 / math.sqrt(length * width)

    def mix(block):
        pieces = jnp.concatenate([block, place.swap(block)], axis=0)
        spec = (dot(table, pieces) * dft_scale).astype(bf16)
        return dot(spec[:rows], cos_hid) - dot(spec[rows:], sin_hid)

    state = place.collect(inputs[0]).astype(f32)
    stored = []
    for layer_id in range(layers):
        mixed = mix(state.astype(bf16))
        hidden, normed_mix, inv_mix = layer_norm(state + mixed, norm_gain[layer_id, 0], norm_bias[layer_id, 0])
        hidden_low = hidden.astype(bf16)
        act, slope = gelu_both(dot(hidden_low, w_in[layer_id]) + b_in[layer_id])
        act_low, slope = act.astype(bf16), slope.astype(bf16)
        branch = dot(act_low, w_out[layer_id]) + b_out[layer_id]
        state, normed_ff, inv_ff = layer_norm(hidden + branch, norm_gain[layer_id, 1], norm_bias[layer_id, 1])
        stored.append((hidden_low, slope, act_low, normed_mix, inv_mix, normed_ff, inv_ff))
    outputs = place.give_back(state, size)
    upstream = place.collect(cotangent[0].astype(bf16)).astype(f32)
    win_out, wout_out, small_out = [None] * layers, [None] * layers, [None] * layers
    for layer_id in reversed(range(layers)):
        hidden_low, slope, act_low, normed_mix, inv_mix, normed_ff, inv_ff = stored[layer_id]
        resid_ff, gain_ff, bias_ff = norm_back(upstream, normed_ff, inv_ff, norm_gain[layer_id, 1])
        branch_grad = resid_ff.astype(bf16)
        bout = jnp.sum(branch_grad.astype(f32), axis=0)
        pre_grad = (dot(branch_grad, w_out[layer_id], ((1,), (1,))) * slope.astype(f32)).astype(bf16)
        bin_ = jnp.sum(pre_grad.astype(f32), axis=0)
        hidden_grad = resid_ff + dot(pre_grad, w_in[layer_id], ((1,), (1,)))
        resid_mix, gain_mix, bias_mix = norm_back(hidden_grad, normed_mix, inv_mix, norm_gain[layer_id, 0])
        wout_out[layer_id] = slot_grad(place, act_low, branch_grad, 1)
        win_out[layer_id] = slot_grad(place, pre_grad, hidden_low, 2).T
        small_out[layer_id] = all_sum(jnp.concatenate([gain_mix, gain_ff, bias_mix, bias_ff, bout, bin_]))
        upstream = resid_mix + mix(resid_mix.astype(bf16))
    small = jnp.stack(small_out)
    gains = small[:, : 2 * width].reshape(layers, 2, width)
    biases = small[:, 2 * width : 4 * width].reshape(layers, 2, width)
    bout = small[:, 4 * width : 5 * width]
    bin_ = small[:, 5 * width :]
    input_grad = place.give_back(upstream, size)
    return (outputs[None], input_grad[None], gains, biases, jnp.stack(win_out), bin_, jnp.stack(wout_out), bout)


def solution(mesh):
    def run(inputs, norm_gain, norm_bias, w_in, b_in, w_out, b_out, cotangent):
        tables = seq_tables(inputs.shape[1], mesh.shape["seq"])
        hid_tables = np_tables(inputs.shape[2])

        def inner(*args):
            return body(tables, hid_tables, *args)

        return jax.shard_map(
            inner,
            mesh=mesh,
            in_specs=(P("batch", "seq", None), P(), P(), P(), P(), P(), P(), P("batch", "seq", None)),
            out_specs=(
                P("batch", "seq", None),
                P("batch", "seq", None),
                P(),
                P(),
                P(None, None, ("seq", "batch")),
                P(),
                P(None, ("seq", "batch"), None),
                P(),
            ),
            check_vma=False,
        )(inputs, norm_gain, norm_bias, w_in, b_in, w_out, b_out, cotangent)

    return run
```

```python
import functools
import math

import jax
import jax.numpy as jnp
import numpy as np
from jax import lax
from jax.experimental import pallas as pl
from jax.experimental.pallas import tpu as pltpu
from jax.sharding import PartitionSpec as P

eps_norm = 1e-05
bf16 = jnp.bfloat16
f32 = jnp.float32


def parity_of(index):
    return bin(index).count("1") & 1


def np_tables(modulus):
    ids = np.arange(modulus, dtype=np.int64)
    product = (ids[:, None] * ids[None, :]) % modulus
    angles = product.astype(np.float32) * np.float32(2.0 * math.pi / modulus)
    return np.cos(angles).astype(bf16), np.sin(angles).astype(bf16)


def seq_tables(length, seq_count):
    rows = length // seq_count
    cos_t, sin_t = np_tables(length)
    ids = [
        np.concatenate([np.arange(t * rows, (t + 1) * rows) for t in range(seq_count) if parity_of(t) == c])
        for c in (0, 1)
    ]
    out = []
    for c in (0, 1):
        cols = np.concatenate([ids[c], ids[1 - c]])
        out.append(np.concatenate([t[ids[c]][:, cols] for t in (cos_t, sin_t)], axis=0))
    return np.stack(out)


class Place:
    def __init__(self):
        self.seq_count = lax.axis_size("seq")
        self.batch_count = lax.axis_size("batch")

    @property
    def s(self):
        return lax.axis_index("seq")

    @property
    def core(self):
        return lax.axis_index("batch") & 1

    @property
    def home(self):
        bits = self.s
        for shift in (4, 2, 1):
            bits = bits ^ (bits >> shift)
        return self.core == (bits & 1)

    def send(self, value, pairs):
        n = self.batch_count
        full = [
            (s0 * n + 2 * z + c0, s1 * n + 2 * z + c1)
            for (s0, c0), (s1, c1) in pairs
            for z in range(n // 2)
        ]
        return lax.ppermute(value, ("seq", "batch"), full)

    def swap(self, value):
        return xor_send(value, "batch", 1)

    @property
    def z(self):
        return lax.axis_index("batch") >> 1

    def row(self, size, mask=0):
        return pl.ds(pl.multiple_of(((self.s ^ mask) >> 1) * size, size), size)

    def send_back(self, low):
        pairs = [((t, 1 - parity_of(t)), (t ^ 1, parity_of(t))) for t in range(self.seq_count)]
        return self.send(low, pairs)

    def collect(self, block):
        odd = [m for m in range(1, self.seq_count) if parity_of(m)]
        even = [m for m in range(1, self.seq_count) if not parity_of(m)]
        size = block.shape[0]
        buffer = jnp.zeros((size * self.seq_count // 2, block.shape[1]), block.dtype)

        def put(buffer, piece, block_id):
            return lax.dynamic_update_slice(buffer, piece, ((block_id >> 1) * size, 0))

        for n, mask in enumerate(odd):
            pairs = [((t, 1 - parity_of(t)), (t ^ mask, parity_of(t))) for t in range(self.seq_count)]
            ids = self.s ^ mask
            piece = None
            if n < len(even):
                pairs += [((t, parity_of(t)), (t ^ even[n], parity_of(t))) for t in range(self.seq_count)]
                ids = jnp.where(self.home, self.s ^ even[n], ids)
                piece = self.send(block, pairs)
            else:
                ids = jnp.where(self.home, self.s, ids)
                piece = jnp.where(self.home, block, self.send(block, pairs))
            buffer = put(buffer, piece, ids)
        return buffer

    def give_back(self, rows, size):
        local = lax.dynamic_slice(rows, ((self.s >> 1) * size, 0), (size, rows.shape[1]))
        pairs = [((t, 1 - parity_of(t)), (t ^ 1, parity_of(t))) for t in range(self.seq_count)]
        got = self.send(local.astype(bf16), pairs)
        return jnp.where(self.home, local, got.astype(f32))


def xor_send(value, axis, mask):
    size = lax.axis_size(axis)
    return lax.ppermute(value, axis, [(i, i ^ mask) for i in range(size)])


def dot(a, b, dims=((1,), (0,))):
    return lax.dot_general(a, b, (dims, ((), ())), preferred_element_type=f32)


def dot_t(a, b):
    return dot(a, b, ((1,), (1,)))


def gelu_both(z):
    k = math.sqrt(2.0 / math.pi)
    z2 = z * z
    t = jnp.tanh(z * (k + (k * 0.044715) * z2))
    half = 0.5 + 0.5 * t
    act = z * half
    slope = half + act * (1.0 - half) * (2.0 * k + (6.0 * k * 0.044715) * z2)
    return act, slope


def row_loop(rows, step, fn, init=0):
    def one(i, carry):
        return fn(pl.ds(pl.multiple_of(i * step, step), step), carry)

    return lax.fori_loop(0, rows // step, one, init)


def mean_of(v):
    return jnp.mean(v, axis=-1, keepdims=True)


def norm_fwd(v):
    centered = v - mean_of(v)
    inv = lax.rsqrt(mean_of(centered * centered) + eps_norm)
    return centered * inv, inv


def norm_bwd(up, normed, inv, gain):
    scaled = up * gain
    return inv * (scaled - mean_of(scaled) - normed * mean_of(scaled * normed))


def wide(inv):
    return jnp.broadcast_to(inv, (inv.shape[0], 128))


def mix_phase(table, hid, pieces, spec, rows, scale, each):
    width = hid.shape[1]
    for part in range(2):
        cut = pl.ds(part * rows, rows)
        value, start = None, 0
        for piece in pieces:
            term = dot(table[cut, start : start + piece.shape[0]], piece[...])
            value = term if value is None else value + term
            start += piece.shape[0]
        spec[cut, :] = (value * scale).astype(bf16)
    mixed = dot(spec[pl.ds(0, rows), :], hid[pl.ds(0, width), :])
    mixed += dot(spec[pl.ds(rows, rows), :], hid[pl.ds(width, width), :])
    each(mixed)


STEP = 128


def fwd_compute(layer, rows, scale, refs):
    r = refs
    def after_mix(mixed):
        r["hidden"][...] = mixed
    mix_phase(r["table"], r["hid"], r["pieces"], r["spec"], rows, scale, after_mix)
    gain0, bias0 = r["gain"][layer, 0:1, :], r["bias"][layer, 0:1, :]
    gain1, bias1 = r["gain"][layer, 1:2, :], r["bias"][layer, 1:2, :]

    def first(cut, carry):
        normed, inv = norm_fwd(r["state"][cut, :].astype(f32) + r["hidden"][cut, :])
        r["norm0"][cut, :] = normed
        r["inv0"][cut, :] = wide(inv)
        hidden = normed * gain0 + bias0
        r["hidden"][cut, :] = hidden
        r["hidden_low"][cut, :] = hidden.astype(bf16)
        return carry

    row_loop(rows, STEP, first)
    r["after_first"]()
    r["wait_in"]()
    ff = r["w_in"].shape[1]
    chunk = r["chunk"]
    for j in range(ff // chunk):
        cut = pl.ds(j * chunk, chunk)
        z = dot(r["hidden_low"][...], r["w_in"][:, cut]) + r["b_in"][layer : layer + 1, cut]
        act, slope = gelu_both(z)
        act = act.astype(bf16)
        r["act"][:, cut] = act
        r["slope"][:, cut] = slope.astype(bf16)
        if j == 0:
            r["wait_out"]()
            r["norm1"][...] = dot(act, r["w_out"][cut, :])
        else:
            r["norm1"][...] += dot(act, r["w_out"][cut, :])
    r["after_ff"]()
    b_out = r["b_out"][layer : layer + 1, :]

    def second(cut, carry):
        normed, inv = norm_fwd(r["hidden"][cut, :] + (r["norm1"][cut, :] + b_out))
        r["norm1"][cut, :] = normed
        r["inv1"][cut, :] = wide(inv)
        r["put_state"](cut, normed * gain1 + bias1)
        return carry

    row_loop(rows, STEP, second)


def zero_sums(rows8):
    return tuple(jnp.zeros((8, n), f32) for n in rows8)


def fold(v):
    return jnp.sum(v.reshape(v.shape[0] // 8, 8, v.shape[1]), axis=0)


def last_norm_back(layer, rows, refs, upstream):
    r = refs
    gain1 = r["gain"][layer, 1:2, :]
    width = r["resid"].shape[1]

    def back(cut, sums):
        up, normed = upstream(cut), r["norm1"][cut, :]
        resid = norm_bwd(up, normed, r["inv1"][cut, :1], gain1)
        low = resid.astype(bf16)
        r["resid"][cut, :] = resid
        r["branch_low"][cut, :] = low
        return (sums[0] + fold(up * normed), sums[1] + fold(up), sums[2] + fold(low.astype(f32)))

    sums = row_loop(rows, STEP, back, zero_sums((width,) * 3))
    for slot, value in zip((1, 3, 4), sums):
        r["small"][slot : slot + 1, :] = jnp.sum(value, axis=0, keepdims=True)


def ff_back_in(rows, refs):
    r = refs
    ff = r["pre_low"].shape[1]
    chunk = r["chunk"]
    width = r["small"].shape[1]
    for j in range(ff // chunk):
        cut = pl.ds(j * chunk, chunk)
        act_grad = dot_t(r["branch_low"][...], r["w_out"][cut, :])
        low = (act_grad * r["slope"][:, cut].astype(f32)).astype(bf16)
        r["pre_low"][:, cut] = low
        sums = jnp.sum(low.astype(f32), axis=0, keepdims=True)
        for n in range(chunk // width):
            slot = 5 + j * (chunk // width) + n
            r["small"][slot : slot + 1, :] = sums[:, n * width : (n + 1) * width]


def ff_back_out(layer, rows, refs):
    r = refs
    width = r["resid"].shape[1]
    r["resid"][...] = r["resid_in"][...] + dot_t(r["pre_low"][...], r["w_in"][...])
    gain0 = r["gain"][layer, 0:1, :]

    def back(cut, sums):
        up, normed = r["resid"][cut, :], r["norm0"][cut, :]
        resid = norm_bwd(up, normed, r["inv0"][cut, :1], gain0)
        r["resid"][cut, :] = resid
        r["put_mix"](cut, resid.astype(bf16))
        return (sums[0] + fold(up * normed), sums[1] + fold(up))

    sums = row_loop(rows, STEP, back, zero_sums((width,) * 2))
    for slot, value in zip((0, 2), sums):
        r["small"][slot : slot + 1, :] = jnp.sum(value, axis=0, keepdims=True)
def layer_norm(values, gain_vec, bias_vec):
    centered = values - jnp.mean(values, axis=-1, keepdims=True)
    inv_std = lax.rsqrt(jnp.mean(centered * centered, axis=-1, keepdims=True) + eps_norm)
    normed = centered * inv_std
    return (normed * gain_vec + bias_vec, normed, inv_std)


def norm_back(upstream, normed, inv_std, gain_vec):
    gain_grad = jnp.sum(upstream * normed, axis=0)
    bias_grad = jnp.sum(upstream, axis=0)
    scaled = upstream * gain_vec
    inner = (
        scaled
        - jnp.mean(scaled, axis=-1, keepdims=True)
        - normed * jnp.mean(scaled * normed, axis=-1, keepdims=True)
    )
    return (inv_std * inner, gain_grad, bias_grad)


def exchange_sum(part, axis_name, bit, dim, out_dtype):
    mine = (lax.axis_index(axis_name) >> bit) & 1
    keep = lax.dynamic_index_in_dim(part, mine, dim, keepdims=False)
    give = lax.dynamic_index_in_dim(part, 1 - mine, dim, keepdims=False)
    got = xor_send(give, axis_name, 1 << bit)
    return (keep.astype(f32) + got.astype(f32)).astype(out_dtype)


def slot_grad(place, left, right, mask):
    batch_bits = place.batch_count.bit_length() - 1
    span = left.shape[1] // place.seq_count

    def one(slot):
        cut = lax.dynamic_slice(left, (0, slot * span), (left.shape[0], span))
        return dot(cut, right, ((0,), (0,))).astype(bf16)

    part = jnp.stack([one(place.s), one(place.s ^ mask)])
    part = part.reshape((2,) + (2,) * batch_bits + (-1, right.shape[1]))
    part = exchange_sum(part, "batch", 0, batch_bits, bf16)
    part = (part[0].astype(f32) + xor_send(part[1], "seq", mask).astype(f32)).astype(bf16)
    for bit in range(1, batch_bits):
        part = exchange_sum(part, "batch", bit, batch_bits - 1 - bit, f32 if bit == batch_bits - 1 else bf16)
    return part


def all_sum(vec):
    vec = vec + xor_send(vec, "batch", 1)
    vec = vec + xor_send(vec, "seq", 1)
    for bit in range(1, lax.axis_size("batch").bit_length() - 1):
        vec = vec + xor_send(vec, "batch", 1 << bit)
    return vec


def plain_body(table, hid_table, inputs, norm_gain, norm_bias, w_in, b_in, w_out, b_out, cotangent):
    place = Place()
    size = inputs.shape[1]
    width = inputs.shape[2]
    length = size * place.seq_count
    rows = length // 2
    layers = w_in.shape[0]
    dft_scale = 1.0 / math.sqrt(length * width)

    def mix(block):
        pieces = jnp.concatenate([block, place.swap(block)], axis=0)
        spec = (dot(table, pieces) * dft_scale).astype(bf16)
        return dot(spec[:rows], hid_table[:width]) + dot(spec[rows:], hid_table[width:])

    state = place.collect(inputs[0]).astype(f32)
    stored = []
    for layer_id in range(layers):
        mixed = mix(state.astype(bf16))
        hidden, normed_mix, inv_mix = layer_norm(state + mixed, norm_gain[layer_id, 0], norm_bias[layer_id, 0])
        hidden_low = hidden.astype(bf16)
        act, slope = gelu_both(dot(hidden_low, w_in[layer_id]) + b_in[layer_id])
        act_low, slope = act.astype(bf16), slope.astype(bf16)
        branch = dot(act_low, w_out[layer_id]) + b_out[layer_id]
        state, normed_ff, inv_ff = layer_norm(hidden + branch, norm_gain[layer_id, 1], norm_bias[layer_id, 1])
        stored.append((hidden_low, slope, act_low, normed_mix, inv_mix, normed_ff, inv_ff))
    outputs = place.give_back(state, size)
    upstream = place.collect(cotangent[0].astype(bf16)).astype(f32)
    win_out, wout_out, small_out = [None] * layers, [None] * layers, [None] * layers
    for layer_id in reversed(range(layers)):
        hidden_low, slope, act_low, normed_mix, inv_mix, normed_ff, inv_ff = stored[layer_id]
        resid_ff, gain_ff, bias_ff = norm_back(upstream, normed_ff, inv_ff, norm_gain[layer_id, 1])
        branch_grad = resid_ff.astype(bf16)
        bout = jnp.sum(branch_grad.astype(f32), axis=0)
        pre_grad = (dot(branch_grad, w_out[layer_id], ((1,), (1,))) * slope.astype(f32)).astype(bf16)
        bin_ = jnp.sum(pre_grad.astype(f32), axis=0)
        hidden_grad = resid_ff + dot(pre_grad, w_in[layer_id], ((1,), (1,)))
        resid_mix, gain_mix, bias_mix = norm_back(hidden_grad, normed_mix, inv_mix, norm_gain[layer_id, 0])
        wout_out[layer_id] = slot_grad(place, act_low, branch_grad, 1)
        win_out[layer_id] = slot_grad(place, pre_grad, hidden_low, 2).T
        small_out[layer_id] = all_sum(jnp.concatenate([gain_mix, gain_ff, bias_mix, bias_ff, bout, bin_]))
        upstream = resid_mix + mix(resid_mix.astype(bf16))
    small = jnp.stack(small_out)
    gains = small[:, : 2 * width].reshape(layers, 2, width)
    biases = small[:, 2 * width : 4 * width].reshape(layers, 2, width)
    bout = small[:, 4 * width : 5 * width]
    bin_ = small[:, 5 * width :]
    input_grad = place.give_back(upstream, size)
    return (outputs[None], input_grad[None], gains, biases, jnp.stack(win_out), bin_, jnp.stack(wout_out), bout)


SMALL_ROWS = 16
CHUNK = 768


def near(shape, dtype):
    return pltpu.VMEM(shape, dtype)


def halves(refs, rows):
    half = rows // 2

    def put(cut, value):
        first = cut.start < half

        @pl.when(first)
        def _():
            refs[0][cut, :] = value

        @pl.when(jnp.logical_not(first))
        def _():
            refs[1][pl.ds(pl.multiple_of(cut.start - half, STEP), STEP), :] = value

    return put


def far(shape, dtype):
    return pltpu.HBM(shape, dtype)


def result(shape, dtype):
    return jax.ShapeDtypeStruct(shape, dtype)


def call(kernel, outs, scratch, args, far_args=(), deps=(), flops=0, limit=16, sems=0, far_outs=()):
    nbytes = sum(a.size * a.dtype.itemsize for a in args)
    vmem = pl.BlockSpec(memory_space=pltpu.VMEM)
    hbm = pl.BlockSpec(memory_space=pl.ANY)
    n_in, n_dep, n_out = len(args) + len(far_args), len(deps), len(outs)

    def run(*refs):
        token = refs[n_in + n_dep + n_out]
        token[...] = jnp.zeros_like(token)
        kernel(refs[:n_in], refs[n_in + n_dep : n_in + n_dep + n_out], refs[n_in + n_dep + n_out + 1 :])

    scratch_shapes = [pltpu.VMEM(s, d) for s, d in scratch]
    if sems:
        scratch_shapes.append(pltpu.SemaphoreType.DMA((sems,)))
    return pl.pallas_call(
        run,
        in_specs=[vmem] * len(args) + [hbm] * (len(far_args) + n_dep),
        out_specs=[hbm if o in far_outs else vmem for o in range(n_out + 1)],
        out_shape=list(outs) + [near((8, 128), f32)],
        scratch_shapes=scratch_shapes,
        compiler_params=pltpu.CompilerParams(vmem_limit_bytes=limit << 20),
        cost_estimate=pl.CostEstimate(flops=int(flops), bytes_accessed=int(nbytes), transcendentals=0),
    )(*[pltpu.with_memory_space_constraint(a, pltpu.VMEM) for a in args],
      *[pltpu.with_memory_space_constraint(a, pltpu.HBM) for a in far_args], *deps)


def load(place, table, hid, params, w_in, w_out):
    gain, bias, b_in, b_out = params

    def kernel(ins, outs, scratch):
        (sems,) = scratch
        table_h, hid_h, gain_h, bias_h, bin_h, bout_h, win_h, wout_h = ins
        srcs = [table_h.at[place.core], hid_h, gain_h, bias_h, bin_h, bout_h, win_h.at[0], wout_h.at[0]]
        copies = [pltpu.make_async_copy(src, dst, sems.at[n]) for n, (src, dst) in enumerate(zip(srcs, outs))]
        for copy in copies:
            copy.start()
        for copy in copies:
            copy.wait()

    args = [table, hid, gain, bias, b_in, b_out, w_in, w_out]
    outs = [near(a.shape if 0 < n < 6 else a.shape[1:], a.dtype) for n, a in enumerate(args)]
    *got, token = call(kernel, outs, [], [], args, (), 0, 16, 8)
    return got[0], got[1], tuple(got[2:6]), got[6], got[7], token


def forward_first(own, other, table, hid, w_in, w_out, params, scale, deps=()):
    R, D = own.shape
    ff = w_in.shape[1]

    def kernel(ins, outs, scratch):
        own, other, table, hid, win, wout, gain, bias, b_in, b_out = ins
        low_a, low_b, norm1, act_h, slope_h, hlow_h, norm0_h, inv0_h, norm1_h, inv1_h = outs
        spec, hidden, act, slope, hlow, norm0, inv0, inv1, sems = scratch
        puts = [pltpu.make_async_copy(src, dst, sems.at[n]) for n, (src, dst) in enumerate(
            [(hlow, hlow_h), (norm0, norm0_h), (inv0, inv0_h), (act, act_h), (slope, slope_h), (norm1, norm1_h), (inv1, inv1_h)])]
        put = halves((low_a, low_b), R)

        def start(which):
            for n in which:
                puts[n].start()

        r = dict(table=table, hid=hid, pieces=[own, other], spec=spec, hidden=hidden, state=own, norm0=norm0, inv0=inv0,
                 hidden_low=hlow, w_in=win, w_out=wout, act=act, slope=slope, norm1=norm1, inv1=inv1, gain=gain, bias=bias,
                 b_in=b_in, b_out=b_out, chunk=CHUNK, put_state=lambda cut, value: put(cut, value.astype(bf16)),
                 wait_in=lambda: None, wait_out=lambda: None,
                 after_first=lambda: start((0, 1, 2)), after_ff=lambda: start((3, 4)))
        fwd_compute(0, R, scale, r)
        start((5, 6))
        for copy in puts:
            copy.wait()

    outs = [near((R // 2, D), bf16)] * 2 + [near((R, D), f32), far((R, ff), bf16), far((R, ff), bf16), far((R, D), bf16),
            far((R, D), f32), far((R, 128), f32), far((R, D), f32), far((R, 128), f32)]
    scratch = [((2 * R, D), bf16), ((R, D), f32), ((R, ff), bf16), ((R, ff), bf16), ((R, D), bf16), ((R, D), f32),
               ((R, 128), f32), ((R, 128), f32)]
    flops = 2 * R * D * (4 * R + 2 * D + 2 * ff)
    return call(kernel, outs, scratch, [own, other, table, hid, w_in, w_out, *params], [], deps, flops, 26, 7, range(3, 10))


def forward_back_last(place, size, layer, pieces, norm_in, cot, table, hid, w_in, w_out, params, scale, deps=()):
    R, D = norm_in.shape
    ff = w_in.shape[2]

    def kernel(ins, outs, scratch):
        *pieces, norm_in, cot, table, hid, gain, bias, b_in, b_out, win_h, wout_h = ins
        local_h, final_low_h, act, hlow, branch, pre, mix, resid, small = outs
        final, final_low, spec, norm0, inv0, norm1, inv1, win, wout, sems = scratch
        get_in = pltpu.make_async_copy(win_h.at[layer], win, sems.at[0])
        get_out = pltpu.make_async_copy(wout_h.at[layer], wout, sems.at[1])
        get_in.start()
        get_out.start()
        gain_b, bias_b = gain[layer - 1, 1:2, :], bias[layer - 1, 1:2, :]

        class State:
            def __getitem__(self, index):
                return norm_in[index] * gain_b + bias_b

        def put_state(cut, value):
            final[cut, :] = value

        def put_mix(cut, value):
            mix[cut, :] = value

        r = dict(table=table, hid=hid, pieces=pieces, spec=spec, hidden=resid, state=State(), norm0=norm0,
                 inv0=inv0, hidden_low=hlow, w_in=win, w_out=wout, act=act, slope=pre, norm1=norm1, inv1=inv1, gain=gain,
                 bias=bias, b_in=b_in, b_out=b_out, chunk=CHUNK, put_state=put_state, wait_in=get_in.wait,
                 wait_out=get_out.wait, resid=resid, resid_in=resid, branch_low=branch, pre_low=pre, small=small, put_mix=put_mix,
                 after_first=lambda: None, after_ff=lambda: None)
        small[...] = jnp.zeros_like(small)
        fwd_compute(layer, R, scale, r)
        block = place.row(size)
        final_low[...] = final[block, :].astype(bf16)
        puts = [pltpu.make_async_copy(final.at[block], local_h, sems.at[2]),
                pltpu.make_async_copy(final_low, final_low_h, sems.at[3])]
        for put in puts:
            put.start()
        last_norm_back(layer, R, r, lambda cut: cot[cut, :].astype(f32))
        ff_back_in(R, r)
        ff_back_out(layer, R, r)
        for put in puts:
            put.wait()

    outs = [far((size, D), f32), far((size, D), bf16), near((R, ff), bf16), near((R, D), bf16), near((R, D), bf16),
            near((R, ff), bf16), near((R, D), bf16), near((R, D), f32), near((SMALL_ROWS, D), f32)]
    scratch = [((R, D), f32), ((size, D), bf16), ((2 * R, D), bf16), ((R, D), f32), ((R, 128), f32), ((R, D), f32), ((R, 128), f32),
               ((D, ff), bf16), ((ff, D), bf16)]
    flops = 2 * R * D * (4 * R + 2 * D + 4 * ff)
    return call(kernel, outs, scratch, [*pieces, norm_in, cot, table, hid, *params], [w_in, w_out], deps, flops, 26, 4, (0, 1))


def back_norm(layer, own, other, resid_in, norm1, inv1, table, hid, gain, w_out, slope, scale, deps=()):
    R, D = own.shape
    ff = w_out.shape[1]

    def kernel(ins, outs, scratch):
        own, other, resid_in, table, hid, gain, norm1_h, inv1_h, wout_h, slope_h = ins
        branch, resid, small, wout, slope = outs
        spec, mixed_v, norm1, inv1, sems = scratch
        gets = [pltpu.make_async_copy(src, dst, sems.at[n]) for n, (src, dst) in enumerate(
            [(norm1_h, norm1), (inv1_h, inv1), (wout_h.at[layer], wout), (slope_h, slope)])]
        for get in gets:
            get.start()
        small[...] = jnp.zeros_like(small)

        def after_mix(mixed):
            mixed_v[...] = mixed

        mix_phase(table, hid, [own, other], spec, R, scale, after_mix)
        for get in gets[:2]:
            get.wait()
        r = dict(gain=gain, resid=resid, norm1=norm1, inv1=inv1, branch_low=branch, small=small)
        last_norm_back(layer, R, r, lambda cut: resid_in[cut, :] + mixed_v[cut, :])
        for get in gets[2:]:
            get.wait()

    outs = [near((R, D), bf16), near((R, D), f32), near((SMALL_ROWS, D), f32), near((ff, D), bf16), near((R, ff), bf16)]
    scratch = [((2 * R, D), bf16), ((R, D), f32), ((R, D), f32), ((R, 128), f32)]
    flops = 2 * R * D * (4 * R + 2 * D)
    return call(kernel, outs, scratch, [own, other, resid_in, table, hid, gain], [norm1, inv1, w_out, slope], deps, flops, 14, 4)


def back_in(layer, branch, slope, w_out, small_in, w_in, norm0, inv0, deps=()):
    R, D = branch.shape
    ff = w_out.shape[0]

    def kernel(ins, outs, scratch):
        branch, slope, wout, small_in, win_h, norm0_h, inv0_h = ins
        pre, small, win, norm0, inv0 = outs
        (sems,) = scratch
        gets = [pltpu.make_async_copy(src, dst, sems.at[n]) for n, (src, dst) in enumerate(
            [(win_h.at[layer], win), (norm0_h, norm0), (inv0_h, inv0)])]
        for get in gets:
            get.start()
        small[...] = small_in[...]
        ff_back_in(R, dict(branch_low=branch, small=small, slope=slope, w_out=wout, pre_low=pre, chunk=CHUNK))
        for get in gets:
            get.wait()

    outs = [near((R, ff), bf16), near((SMALL_ROWS, D), f32), near((D, ff), bf16), near((R, D), f32), near((R, 128), f32)]
    return call(kernel, outs, [], [branch, slope, w_out, small_in], [w_in, norm0, inv0], deps, 2 * R * D * ff, 12, 3)


def back_out(layer, pre, resid_in, norm0, inv0, w_in, gain, small_in, deps=()):
    R, D = resid_in.shape
    ff = w_in.shape[1]

    def kernel(ins, outs, scratch):
        pre, resid_in, norm0, inv0, win, gain, small_in = ins
        mix_a, mix_b, resid, small = outs
        small[...] = small_in[...]
        ff_back_out(layer, R, dict(gain=gain, resid=resid, resid_in=resid_in, norm0=norm0, inv0=inv0, small=small, w_in=win,
                                   pre_low=pre, put_mix=halves((mix_a, mix_b), R)))

    outs = [near((R // 2, D), bf16)] * 2 + [near((R, D), f32), near((SMALL_ROWS, D), f32)]
    return call(kernel, outs, [], [pre, resid_in, norm0, inv0, w_in, gain, small_in], [], deps, 2 * R * D * ff, 12)


def mix_last(place, size, pieces, resid_in, final_low, table, hid, scale, deps=()):
    R, D = resid_in.shape

    def kernel(ins, outs, scratch):
        *pieces, resid_in, table, hid, final_low = ins
        local, low = outs
        spec, grad, sems = scratch
        get = pltpu.make_async_copy(final_low, low.at[pl.ds(size, size)], sems.at[0])
        get.start()

        def after_mix(mixed):
            grad[...] = resid_in[...] + mixed

        mix_phase(table, hid, pieces, spec, R, scale, after_mix)
        cut = place.row(size)
        local[...] = grad[cut, :]
        low[:size, :] = grad[cut, :].astype(bf16)
        get.wait()

    flops = 2 * R * D * (4 * R + 2 * D)
    return call(kernel, [near((size, D), f32), near((2 * size, D), bf16)], [((2 * R, D), bf16), ((R, D), f32)],
                [*pieces, resid_in, table, hid], [final_low], deps, flops, 14, 1)


def gather_rows(place, block, pieces, deps=()):
    size, D = block.shape
    R = size * place.seq_count // 2

    def kernel(ins, outs, scratch):
        (rows,) = outs
        (sems,) = scratch
        home = place.home

        def put(ref, mask):
            rows[place.row(size, mask), :] = ref[:size, :]

        @pl.when(home)
        def _():
            own = pltpu.make_async_copy(ins[-1], rows.at[place.row(size)], sems.at[0])
            own.start()
            for ref, (home_mask, _) in zip(ins, [p[1] for p in pieces]):
                if home_mask is not None:
                    put(ref, home_mask)
            own.wait()

        @pl.when(jnp.logical_not(home))
        def _():
            for ref, (_, away_mask) in zip(ins, [p[1] for p in pieces]):
                put(ref, away_mask)

    return call(kernel, [near((R, D), block.dtype)], [], [p[0] for p in pieces], [block], deps, 0, 16, 1)


def send_blocks(place, block):
    odd = [m for m in range(1, place.seq_count) if parity_of(m)]
    even = [m for m in range(1, place.seq_count) if not parity_of(m)]
    pieces = []
    for n, mask in enumerate(odd):
        pairs = [((t, 1 - parity_of(t)), (t ^ mask, parity_of(t))) for t in range(place.seq_count)]
        home_mask = None
        if n < len(even):
            home_mask = even[n]
            pairs += [((t, parity_of(t)), (t ^ home_mask, parity_of(t))) for t in range(place.seq_count)]
        pieces.append((place.send(block, pairs), (home_mask, mask)))
    return pieces


class Chain:
    def __init__(self, place, grads, pieces, pad, extra=None):
        self.place = place
        self.m = len(grads)
        self.masks = [g[2] for g in grads]
        self.z_bits = (place.batch_count // 2).bit_length() - 1
        self.zs = 1 << self.z_bits
        self.pad = pad
        parts = []
        for left, right, mask in grads:
            span = left.shape[1] // place.seq_count
            self.n = span // place.batch_count
            self.width = right.shape[1]
            for slot in (place.s, place.s ^ mask):
                cut = lax.dynamic_slice(left, (0, slot * span), (left.shape[0], span))
                parts.append(dot(cut, right, ((0,), (0,))).astype(bf16))
        self.parts = parts
        zs, n, D = self.zs, self.n, self.width
        self.per = 2 * self.m // pieces
        self.extra = extra
        more = 0 if extra is None else 2 * extra.shape[0]
        self.more = more

        def kernel(ins, outs, scratch):
            core = place.core
            if more:
                outs[-1][pl.ds(zs * n, more), :] = two_parts(ins[-1][...])
            for i, ref in enumerate(ins[: 2 * self.m]):
                for z in range(zs):
                    outs[i // self.per][pl.ds((i % self.per) * zs * n + z * n, n), :] = ref[self.rows(z, 1 - core), :]

        outs = [near((self.per * zs * n + (more if k == pieces - 1 else 0), D), bf16) for k in range(pieces)]
        *gives, _ = call(kernel, outs, [], parts + ([] if extra is None else [extra]))
        self.got = [place.swap(give) for give in gives]

    def rows(self, z, core):
        return pl.ds(pl.multiple_of(z * 2 * self.n + core * self.n, 32), self.n)

    def core_done(self, deps=()):
        zs, n, m, D = self.zs, self.n, self.m, self.width
        place = self.place

        def kernel(ins, outs, scratch):
            core = place.core
            keep, *gives = outs
            if self.more:
                *gives, total = gives
                total[...] = one_part(two_parts(ins[-1][...])) + one_part(ins[-2][pl.ds(self.per * zs * n, self.more), :])
                gives[-1][pl.ds(zs * n, self.more), :] = two_parts(total[...])
            for i in range(2 * m):
                got = ins[2 * m + i // self.per]
                for z in range(zs):
                    cut = pl.ds(z * n, n)
                    value = ins[i][self.rows(z, core), :].astype(f32)
                    value += got[pl.ds((i % self.per) * zs * n + z * n, n), :].astype(f32)
                    if i % 2 == 0:
                        keep[i // 2, cut, :] = value
                    else:
                        gives[i // 2][cut, :] = value.astype(bf16)

        pad = max(self.pad, self.more)
        outs = [near((m, zs * n, D), f32)] + [near((zs * n + pad, D), bf16)] * m
        if self.more:
            outs.append(near(self.extra.shape, f32))
            self.keep, *gives, self.extra, self.token = call(kernel, outs, [], self.parts + self.got + [self.extra], (), deps)
        else:
            self.keep, *gives, self.token = call(kernel, outs, [], self.parts + self.got, (), deps)
        self.got = [xor_send(give, "seq", mask) for give, mask in zip(gives, self.masks)]
        return self.token

    def seq_done(self, deps=()):
        def read(ins):
            keep, *got = ins
            return (lambda i, cut: keep[i, cut, :] + got[i][cut, :].astype(f32)), got[-1]

        return self.z_step(0, read, [self.keep, *self.got], deps)

    def z_done(self, deps=()):
        def read(ins):
            keep, got = ins
            return (lambda i, cut: keep[i, cut, :] + got[pl.ds(i * keep.shape[1] + cut.start, cut.size), :].astype(f32)), got

        return self.z_step(self.bit + 1, read, [self.keep, self.got], deps)

    def z_step(self, bit, read, args, deps):
        m, n, D = self.m, self.n, self.width
        place = self.place
        self.bit = bit
        left = self.zs >> bit
        rows = left // 2 * n
        zs_rows = left * n if bit == 0 else m * left * n

        def kernel(ins, outs, scratch):
            keep, give = outs[:2]
            if self.more:
                *ins, extra = ins
            value, last = read(ins)
            if self.more:
                total = outs[2]
                from_row = zs_rows
                total[...] = one_part(two_parts(extra[...])) + one_part(last[pl.ds(from_row, self.more), :])
                give[pl.ds(m * rows, self.more), :] = two_parts(total[...])
            mine = (place.z >> bit) & 1
            for i in range(m):
                for z in range(left // 2):
                    cut = pl.ds(z * n, n)
                    keep[i, cut, :] = value(i, pl.ds(pl.multiple_of((2 * z + mine) * n, 32), n))
                    other = value(i, pl.ds(pl.multiple_of((2 * z + 1 - mine) * n, 32), n))
                    give[pl.ds(i * rows + z * n, n), :] = other.astype(bf16)

        outs = [near((m, rows, D), f32), near((m * rows + self.more, D), bf16)]
        if self.more:
            outs.append(near(self.extra.shape, f32))
            self.keep, give, self.extra, self.token = call(kernel, outs, [], [*args, self.extra], (), deps)
        else:
            self.keep, give, self.token = call(kernel, outs, [], args, (), deps)
        self.got = xor_send(give, "batch", 2 << bit)
        return self.token

    def last(self, deps=()):
        m, n, D = self.m, self.n, self.width

        def kernel(ins, outs, scratch):
            for i in range(m):
                outs[0][i] = ins[0][i] + ins[1][pl.ds(i * n, n), :].astype(f32)

        self.total, self.token = call(kernel, [near((m, n, D), f32)], [], [self.keep, self.got], (), deps)
        return self.token


def two_parts(value):
    high = value.astype(bf16)
    return jnp.concatenate([high, (value - high.astype(f32)).astype(bf16)], axis=0)


def one_part(parts):
    rows = parts.shape[0] // 2
    return parts[:rows].astype(f32) + parts[rows:].astype(f32)


def choose(place, grad_local, final_local, got, deps=()):
    size = grad_local.shape[0]

    def kernel(ins, outs, scratch):
        home = place.home
        outs[0][...] = jnp.where(home, ins[0][...], ins[2][:size, :].astype(f32))
        outs[1][...] = jnp.where(home, ins[1][...], ins[2][size:, :].astype(f32))

    return call(kernel, [result(grad_local.shape, f32)] * 2, [], [grad_local, final_local, got], [], deps)


def last_out(chain, upper, index, deps=()):
    n, D = upper.shape[1:]

    def kernel(ins, outs, scratch):
        keep, got, upper = ins
        outs[0][0] = keep[0] + got[:n, :].astype(f32)
        outs[0][1] = upper[index]

    return call(kernel, [result((2, n, D), f32)], [], [chain.keep, chain.got, upper], (), deps)


def last_small(chains, ff, deps=()):
    layers = len(chains)
    rows, D = chains[0].extra.shape

    def kernel(ins, outs, scratch):
        gains, biases, bins, bouts = outs
        for layer in range(layers):
            mine, got = ins[2 * layer : 2 * layer + 2]
            part = one_part(two_parts(mine[...])) + one_part(got[pl.ds(got.shape[0] - 2 * rows, 2 * rows), :])
            gains[layer] = part[0:2]
            biases[layer] = part[2:4]
            bouts[layer : layer + 1, :] = part[4:5]
            for n in range(ff // D):
                bins[layer : layer + 1, n * D : (n + 1) * D] = part[5 + n : 6 + n]

    outs = [result((layers, 2, D), f32), result((layers, 2, D), f32), result((layers, ff), f32), result((layers, D), f32)]
    args = [a for chain in chains for a in (chain.extra, chain.got)]
    return call(kernel, outs, [], args, (), deps)


def body(tables, hid_table, inputs, norm_gain, norm_bias, w_in, b_in, w_out, b_out, cotangent):
    place = Place()
    size = inputs.shape[1]
    width = inputs.shape[2]
    length = size * place.seq_count
    scale = 1.0 / math.sqrt(length * width)
    hid = jnp.asarray(hid_table)
    tables = jnp.asarray(tables)
    span = w_in.shape[2] // (place.seq_count * place.batch_count)
    if length > 1024 or span % 32 or w_in.shape[0] != 2:
        table = lax.dynamic_index_in_dim(tables, place.core, 0, keepdims=False)
        return plain_body(table, hid, inputs, norm_gain, norm_bias, w_in, b_in, w_out, b_out, cotangent)

    pieces = send_blocks(place, inputs[0])
    cot_low = cotangent[0].astype(bf16)
    cot_send = jnp.pad(cot_low, ((0, 16), (0, 0)))
    table, hid, params, win0, wout0, tok = load(place, tables, hid, (norm_gain, norm_bias, b_in, b_out), w_in, w_out)
    norm_gain = params[0]
    own, tok = gather_rows(place, inputs[0], pieces, (tok, cot_send))
    cot_pieces = send_blocks(place, cot_send)
    other = place.swap(own)
    state_a, state_b, norm01, act0, slope0, hlow0, norm00, inv00, norm01_far, inv01_far, tok = forward_first(
        own, other, table, hid, win0, wout0, params, scale, (tok,))
    others = [place.swap(half) for half in (state_a, state_b)]
    cot, tok = gather_rows(place, cot_low, cot_pieces, (tok,))
    final_local, final_low, act1, hlow1, branch1, pre1, mix1, resid1, small1, tok = forward_back_last(
        place, size, 1, [state_a, state_b, *others], norm01, cot, table, hid, w_in, w_out, params, scale, (tok,))
    mix1_other = place.swap(mix1)
    grads1 = Chain(place, [(act1, branch1, 1), (pre1, hlow1, 2)], 4, 48, small1)
    branch0, resid0, small0, wout0, slope0, tok = back_norm(
        0, mix1, mix1_other, resid1, norm01_far, inv01_far, table, hid, norm_gain, w_out, slope0, scale, (tok,))
    out0 = Chain(place, [(act0, branch0, 1)], 2, 16)
    tok = grads1.core_done((tok,))
    pre0, small0, win0, norm00, inv00, tok = back_in(0, branch0, slope0, wout0, small0, w_in, norm00, inv00, (tok,))
    tok = out0.core_done((tok,))
    mix_a, mix_b, resid0, small0, tok = back_out(0, pre0, resid0, norm00, inv00, win0, norm_gain, small0, (tok,))
    in0 = Chain(place, [(pre0, hlow0, 2)], 2, 16, small0)
    others = [place.swap(half) for half in (mix_a, mix_b)]
    tok = grads1.seq_done((tok,))
    tok = in0.core_done((tok,))
    grad_local, low, tok = mix_last(place, size, [mix_a, mix_b, *others], resid0, final_low, table, hid, scale, (tok,))
    back = place.send_back(low)
    out0.seq_done()
    grads1.z_done()
    in0.seq_done()
    out0.z_done()
    grads1.last()
    in0.z_done()
    input_grad, outputs, tok = choose(place, grad_local, final_local, back)
    wout, tok = last_out(out0, grads1.total, 0, (tok,))
    win, tok = last_out(in0, grads1.total, 1, (tok,))
    gains, biases, bin_, bout, tok = last_small([in0, grads1], w_in.shape[2])
    return (outputs[None], input_grad[None], gains, biases, jnp.swapaxes(win, 1, 2), bin_, wout, bout)


def solution(mesh):
    def run(inputs, norm_gain, norm_bias, w_in, b_in, w_out, b_out, cotangent):
        tables = seq_tables(inputs.shape[1], mesh.shape["seq"])
        cos_hid, sin_hid = np_tables(inputs.shape[2])
        hid_table = np.concatenate([cos_hid, -sin_hid], axis=0)

        def inner(*args):
            return body(tables, hid_table, *args)

        return jax.shard_map(
            inner,
            mesh=mesh,
            in_specs=(P("batch", "seq", None), P(), P(), P(), P(), P(), P(), P("batch", "seq", None)),
            out_specs=(
                P("batch", "seq", None),
                P("batch", "seq", None),
                P(),
                P(),
                P(None, None, ("seq", "batch")),
                P(),
                P(None, ("seq", "batch"), None),
                P(),
            ),
            check_vma=False,
        )(inputs, norm_gain, norm_bias, w_in, b_in, w_out, b_out, cotangent)

    return run
```

```python
import functools
import math

import jax
import jax.numpy as jnp
import numpy as np
from jax import lax
from jax.experimental import pallas as pl
from jax.experimental.pallas import tpu as pltpu
from jax.sharding import PartitionSpec as P

eps_norm = 1e-05
bf16 = jnp.bfloat16
f32 = jnp.float32


def parity_of(index):
    return bin(index).count("1") & 1


def np_tables(modulus):
    ids = np.arange(modulus, dtype=np.int64)
    product = (ids[:, None] * ids[None, :]) % modulus
    angles = product.astype(np.float32) * np.float32(2.0 * math.pi / modulus)
    return np.cos(angles).astype(bf16), np.sin(angles).astype(bf16)


def seq_tables(length, seq_count):
    rows = length // seq_count
    cos_t, sin_t = np_tables(length)
    ids = [
        np.concatenate([np.arange(t * rows, (t + 1) * rows) for t in range(seq_count) if parity_of(t) == c])
        for c in (0, 1)
    ]
    out = []
    for c in (0, 1):
        cols = np.concatenate([ids[c], ids[1 - c]])
        out.append(np.concatenate([t[ids[c]][:, cols] for t in (cos_t, sin_t)], axis=0))
    return np.stack(out)


class Place:
    def __init__(self):
        self.seq_count = lax.axis_size("seq")
        self.batch_count = lax.axis_size("batch")

    @property
    def s(self):
        return lax.axis_index("seq")

    @property
    def core(self):
        return lax.axis_index("batch") & 1

    @property
    def home(self):
        bits = self.s
        for shift in (4, 2, 1):
            bits = bits ^ (bits >> shift)
        return self.core == (bits & 1)

    def send(self, value, pairs):
        n = self.batch_count
        full = [
            (s0 * n + 2 * z + c0, s1 * n + 2 * z + c1)
            for (s0, c0), (s1, c1) in pairs
            for z in range(n // 2)
        ]
        return lax.ppermute(value, ("seq", "batch"), full)

    def swap(self, value):
        return xor_send(value, "batch", 1)

    @property
    def z(self):
        return lax.axis_index("batch") >> 1

    def row(self, size, mask=0):
        return pl.ds(pl.multiple_of(((self.s ^ mask) >> 1) * size, size), size)

    def send_back(self, low):
        pairs = [((t, 1 - parity_of(t)), (t ^ 1, parity_of(t))) for t in range(self.seq_count)]
        return self.send(low, pairs)

    def collect(self, block):
        odd = [m for m in range(1, self.seq_count) if parity_of(m)]
        even = [m for m in range(1, self.seq_count) if not parity_of(m)]
        size = block.shape[0]
        buffer = jnp.zeros((size * self.seq_count // 2, block.shape[1]), block.dtype)

        def put(buffer, piece, block_id):
            return lax.dynamic_update_slice(buffer, piece, ((block_id >> 1) * size, 0))

        for n, mask in enumerate(odd):
            pairs = [((t, 1 - parity_of(t)), (t ^ mask, parity_of(t))) for t in range(self.seq_count)]
            ids = self.s ^ mask
            piece = None
            if n < len(even):
                pairs += [((t, parity_of(t)), (t ^ even[n], parity_of(t))) for t in range(self.seq_count)]
                ids = jnp.where(self.home, self.s ^ even[n], ids)
                piece = self.send(block, pairs)
            else:
                ids = jnp.where(self.home, self.s, ids)
                piece = jnp.where(self.home, block, self.send(block, pairs))
            buffer = put(buffer, piece, ids)
        return buffer

    def give_back(self, rows, size):
        local = lax.dynamic_slice(rows, ((self.s >> 1) * size, 0), (size, rows.shape[1]))
        pairs = [((t, 1 - parity_of(t)), (t ^ 1, parity_of(t))) for t in range(self.seq_count)]
        got = self.send(local.astype(bf16), pairs)
        return jnp.where(self.home, local, got.astype(f32))


def xor_send(value, axis, mask):
    size = lax.axis_size(axis)
    return lax.ppermute(value, axis, [(i, i ^ mask) for i in range(size)])


def dot(a, b, dims=((1,), (0,))):
    return lax.dot_general(a, b, (dims, ((), ())), preferred_element_type=f32)


def dot_t(a, b):
    return dot(a, b, ((1,), (1,)))


def gelu_both(z):
    k = math.sqrt(2.0 / math.pi)
    z2 = z * z
    t = jnp.tanh(z * (k + (k * 0.044715) * z2))
    half = 0.5 + 0.5 * t
    act = z * half
    slope = half + act * (1.0 - half) * (2.0 * k + (6.0 * k * 0.044715) * z2)
    return act, slope


def row_loop(rows, step, fn, init=0):
    def one(i, carry):
        return fn(pl.ds(pl.multiple_of(i * step, step), step), carry)

    return lax.fori_loop(0, rows // step, one, init)


def mean_of(v):
    return jnp.mean(v, axis=-1, keepdims=True)


def norm_fwd(v):
    centered = v - mean_of(v)
    inv = lax.rsqrt(mean_of(centered * centered) + eps_norm)
    return centered * inv, inv


def norm_bwd(up, normed, inv, gain):
    scaled = up * gain
    return inv * (scaled - mean_of(scaled) - normed * mean_of(scaled * normed))


def wide(inv):
    return jnp.broadcast_to(inv, (inv.shape[0], 128))


def mix_phase(table, hid, pieces, spec, rows, scale, each):
    width = hid.shape[1]
    for part in range(2):
        cut = pl.ds(part * rows, rows)
        value, start = None, 0
        for piece in pieces:
            count = piece.shape[0] // 128 * 128
            term = dot(table[cut, start : start + count], piece[:count, :])
            value = term if value is None else value + term
            start += count
        spec[cut, :] = (value * scale).astype(bf16)
    mixed = dot(spec[pl.ds(0, rows), :], hid[pl.ds(0, width), :])
    mixed += dot(spec[pl.ds(rows, rows), :], hid[pl.ds(width, width), :])
    each(mixed)


STEP = 128


def fwd_compute(layer, rows, scale, refs):
    r = refs
    def after_mix(mixed):
        r["hidden"][...] = mixed
    mix_phase(r["table"], r["hid"], r["pieces"], r["spec"], rows, scale, after_mix)
    gain0, bias0 = r["gain"][layer, 0:1, :], r["bias"][layer, 0:1, :]
    gain1, bias1 = r["gain"][layer, 1:2, :], r["bias"][layer, 1:2, :]

    def first(cut, carry):
        normed, inv = norm_fwd(r["state"][cut, :].astype(f32) + r["hidden"][cut, :])
        r["norm0"][cut, :] = normed
        r["inv0"][cut, :] = wide(inv)
        hidden = normed * gain0 + bias0
        r["hidden"][cut, :] = hidden
        r["hidden_low"][cut, :] = hidden.astype(bf16)
        return carry

    r["before_first"]()
    row_loop(rows, STEP, first)
    r["after_first"]()
    r["wait_in"]()
    ff = r["w_in"].shape[1]
    chunk = r["chunk"]
    for j in range(ff // chunk):
        cut = pl.ds(j * chunk, chunk)
        z = dot(r["hidden_low"][...], r["w_in"][:, cut]) + r["b_in"][layer : layer + 1, cut]
        act, slope = gelu_both(z)
        act = act.astype(bf16)
        r["act"][:, cut] = act
        r["slope"][:, cut] = slope.astype(bf16)
        if j == 0:
            r["wait_out"]()
            r["norm1"][...] = dot(act, r["w_out"][cut, :])
        else:
            r["norm1"][...] += dot(act, r["w_out"][cut, :])
    r["after_ff"]()
    b_out = r["b_out"][layer : layer + 1, :]

    def second(cut, carry):
        normed, inv = norm_fwd(r["hidden"][cut, :] + (r["norm1"][cut, :] + b_out))
        r["norm1"][cut, :] = normed
        r["inv1"][cut, :] = wide(inv)
        r["put_state"](cut, normed * gain1 + bias1)
        return carry

    row_loop(rows, STEP, second)


def zero_sums(rows8):
    return tuple(jnp.zeros((8, n), f32) for n in rows8)


def fold(v):
    return jnp.sum(v.reshape(v.shape[0] // 8, 8, v.shape[1]), axis=0)


def last_norm_back(layer, rows, refs, upstream):
    r = refs
    gain1 = r["gain"][layer, 1:2, :]
    width = r["resid"].shape[1]

    def back(cut, sums):
        up, normed = upstream(cut), r["norm1"][cut, :]
        resid = norm_bwd(up, normed, r["inv1"][cut, :1], gain1)
        low = resid.astype(bf16)
        r["resid"][cut, :] = resid
        r["branch_low"][cut, :] = low
        return (sums[0] + fold(up * normed), sums[1] + fold(up), sums[2] + fold(low.astype(f32)))

    sums = row_loop(rows, STEP, back, zero_sums((width,) * 3))
    for slot, value in zip((1, 3, 4), sums):
        r["small"][slot : slot + 1, :] = jnp.sum(value, axis=0, keepdims=True)


def ff_back_in(rows, refs):
    r = refs
    ff = r["pre_low"].shape[1]
    chunk = r["chunk"]
    width = r["small"].shape[1]
    for j in range(ff // chunk):
        cut = pl.ds(j * chunk, chunk)
        act_grad = dot_t(r["branch_low"][...], r["w_out"][cut, :])
        if "wait_slope" in r:
            r["wait_slope"](j)
        low = (act_grad * r["slope"][:, cut].astype(f32)).astype(bf16)
        r["pre_low"][:, cut] = low
        sums = jnp.sum(low.astype(f32), axis=0, keepdims=True)
        for n in range(chunk // width):
            slot = 5 + j * (chunk // width) + n
            r["small"][slot : slot + 1, :] = sums[:, n * width : (n + 1) * width]


def ff_back_out(layer, rows, refs):
    r = refs
    width = r["resid"].shape[1]
    r["resid"][...] = r["resid_in"][...] + dot_t(r["pre_low"][...], r["w_in"][...])
    gain0 = r["gain"][layer, 0:1, :]

    def back(cut, sums):
        up, normed = r["resid"][cut, :], r["norm0"][cut, :]
        resid = norm_bwd(up, normed, r["inv0"][cut, :1], gain0)
        r["resid"][cut, :] = resid
        r["put_mix"](cut, resid.astype(bf16))
        return (sums[0] + fold(up * normed), sums[1] + fold(up))

    sums = row_loop(rows, STEP, back, zero_sums((width,) * 2))
    for slot, value in zip((0, 2), sums):
        r["small"][slot : slot + 1, :] = jnp.sum(value, axis=0, keepdims=True)
def layer_norm(values, gain_vec, bias_vec):
    centered = values - jnp.mean(values, axis=-1, keepdims=True)
    inv_std = lax.rsqrt(jnp.mean(centered * centered, axis=-1, keepdims=True) + eps_norm)
    normed = centered * inv_std
    return (normed * gain_vec + bias_vec, normed, inv_std)


def norm_back(upstream, normed, inv_std, gain_vec):
    gain_grad = jnp.sum(upstream * normed, axis=0)
    bias_grad = jnp.sum(upstream, axis=0)
    scaled = upstream * gain_vec
    inner = (
        scaled
        - jnp.mean(scaled, axis=-1, keepdims=True)
        - normed * jnp.mean(scaled * normed, axis=-1, keepdims=True)
    )
    return (inv_std * inner, gain_grad, bias_grad)


def exchange_sum(part, axis_name, bit, dim, out_dtype):
    mine = (lax.axis_index(axis_name) >> bit) & 1
    keep = lax.dynamic_index_in_dim(part, mine, dim, keepdims=False)
    give = lax.dynamic_index_in_dim(part, 1 - mine, dim, keepdims=False)
    got = xor_send(give, axis_name, 1 << bit)
    return (keep.astype(f32) + got.astype(f32)).astype(out_dtype)


def slot_grad(place, left, right, mask):
    batch_bits = place.batch_count.bit_length() - 1
    span = left.shape[1] // place.seq_count

    def one(slot):
        cut = lax.dynamic_slice(left, (0, slot * span), (left.shape[0], span))
        return dot(cut, right, ((0,), (0,))).astype(bf16)

    part = jnp.stack([one(place.s), one(place.s ^ mask)])
    part = part.reshape((2,) + (2,) * batch_bits + (-1, right.shape[1]))
    part = exchange_sum(part, "batch", 0, batch_bits, bf16)
    part = (part[0].astype(f32) + xor_send(part[1], "seq", mask).astype(f32)).astype(bf16)
    for bit in range(1, batch_bits):
        part = exchange_sum(part, "batch", bit, batch_bits - 1 - bit, f32 if bit == batch_bits - 1 else bf16)
    return part


def all_sum(vec):
    vec = vec + xor_send(vec, "batch", 1)
    vec = vec + xor_send(vec, "seq", 1)
    for bit in range(1, lax.axis_size("batch").bit_length() - 1):
        vec = vec + xor_send(vec, "batch", 1 << bit)
    return vec


def plain_body(table, hid_table, inputs, norm_gain, norm_bias, w_in, b_in, w_out, b_out, cotangent):
    place = Place()
    size = inputs.shape[1]
    width = inputs.shape[2]
    length = size * place.seq_count
    rows = length // 2
    layers = w_in.shape[0]
    dft_scale = 1.0 / math.sqrt(length * width)

    def mix(block):
        pieces = jnp.concatenate([block, place.swap(block)], axis=0)
        spec = (dot(table, pieces) * dft_scale).astype(bf16)
        return dot(spec[:rows], hid_table[:width]) + dot(spec[rows:], hid_table[width:])

    state = place.collect(inputs[0]).astype(f32)
    stored = []
    for layer_id in range(layers):
        mixed = mix(state.astype(bf16))
        hidden, normed_mix, inv_mix = layer_norm(state + mixed, norm_gain[layer_id, 0], norm_bias[layer_id, 0])
        hidden_low = hidden.astype(bf16)
        act, slope = gelu_both(dot(hidden_low, w_in[layer_id]) + b_in[layer_id])
        act_low, slope = act.astype(bf16), slope.astype(bf16)
        branch = dot(act_low, w_out[layer_id]) + b_out[layer_id]
        state, normed_ff, inv_ff = layer_norm(hidden + branch, norm_gain[layer_id, 1], norm_bias[layer_id, 1])
        stored.append((hidden_low, slope, act_low, normed_mix, inv_mix, normed_ff, inv_ff))
    outputs = place.give_back(state, size)
    upstream = place.collect(cotangent[0].astype(bf16)).astype(f32)
    win_out, wout_out, small_out = [None] * layers, [None] * layers, [None] * layers
    for layer_id in reversed(range(layers)):
        hidden_low, slope, act_low, normed_mix, inv_mix, normed_ff, inv_ff = stored[layer_id]
        resid_ff, gain_ff, bias_ff = norm_back(upstream, normed_ff, inv_ff, norm_gain[layer_id, 1])
        branch_grad = resid_ff.astype(bf16)
        bout = jnp.sum(branch_grad.astype(f32), axis=0)
        pre_grad = (dot(branch_grad, w_out[layer_id], ((1,), (1,))) * slope.astype(f32)).astype(bf16)
        bin_ = jnp.sum(pre_grad.astype(f32), axis=0)
        hidden_grad = resid_ff + dot(pre_grad, w_in[layer_id], ((1,), (1,)))
        resid_mix, gain_mix, bias_mix = norm_back(hidden_grad, normed_mix, inv_mix, norm_gain[layer_id, 0])
        wout_out[layer_id] = slot_grad(place, act_low, branch_grad, 1)
        win_out[layer_id] = slot_grad(place, pre_grad, hidden_low, 2).T
        small_out[layer_id] = all_sum(jnp.concatenate([gain_mix, gain_ff, bias_mix, bias_ff, bout, bin_]))
        upstream = resid_mix + mix(resid_mix.astype(bf16))
    small = jnp.stack(small_out)
    gains = small[:, : 2 * width].reshape(layers, 2, width)
    biases = small[:, 2 * width : 4 * width].reshape(layers, 2, width)
    bout = small[:, 4 * width : 5 * width]
    bin_ = small[:, 5 * width :]
    input_grad = place.give_back(upstream, size)
    return (outputs[None], input_grad[None], gains, biases, jnp.stack(win_out), bin_, jnp.stack(wout_out), bout)


SMALL_ROWS = 16
CHUNK = 768


def near(shape, dtype):
    return pltpu.VMEM(shape, dtype)


def halves(refs, rows):
    half = rows // 2

    def put(cut, value):
        first = cut.start < half

        @pl.when(first)
        def _():
            refs[0][cut, :] = value

        @pl.when(jnp.logical_not(first))
        def _():
            refs[1][pl.ds(pl.multiple_of(cut.start - half, STEP), STEP), :] = value

    return put


def far(shape, dtype):
    return pltpu.HBM(shape, dtype)


def result(shape, dtype):
    return jax.ShapeDtypeStruct(shape, dtype)


def sys_name(kernel):
    return kernel.__qualname__.split(".<locals>")[0].split(".")[-1]


def call(kernel, outs, scratch, args, far_args=(), deps=(), flops=0, limit=4, sems=0, far_outs=(), name=None):
    nbytes = sum(a.size * a.dtype.itemsize for a in args)
    vmem = pl.BlockSpec(memory_space=pltpu.VMEM)
    hbm = pl.BlockSpec(memory_space=pl.ANY)
    n_in, n_dep, n_out = len(args) + len(far_args), len(deps), len(outs)

    def run(*refs):
        token = refs[n_in + n_dep + n_out]
        token[...] = jnp.zeros_like(token)
        kernel(refs[:n_in], refs[n_in + n_dep : n_in + n_dep + n_out], refs[n_in + n_dep + n_out + 1 :])

    scratch_shapes = [pltpu.VMEM(s, d) for s, d in scratch]
    if sems:
        scratch_shapes.append(pltpu.SemaphoreType.DMA((sems,)))
    return pl.pallas_call(
        run,
        name=name or sys_name(kernel),
        in_specs=[vmem] * len(args) + [hbm] * (len(far_args) + n_dep),
        out_specs=[hbm if o in far_outs else vmem for o in range(n_out + 1)],
        out_shape=list(outs) + [near((8, 128), f32)],
        scratch_shapes=scratch_shapes,
        compiler_params=pltpu.CompilerParams(vmem_limit_bytes=limit << 20),
        cost_estimate=pl.CostEstimate(flops=0, bytes_accessed=0, transcendentals=0),
    )(*[pltpu.with_memory_space_constraint(a, pltpu.VMEM) for a in args],
      *[pltpu.with_memory_space_constraint(a, pltpu.HBM) for a in far_args], *deps)


def load(place, table, hid, params, w_in, w_out):
    gain, bias, b_in, b_out = params

    def kernel(ins, outs, scratch):
        (sems,) = scratch
        table_h, hid_h, gain_h, bias_h, bin_h, bout_h, win_h, wout_h = ins
        srcs = [table_h.at[place.core], hid_h, gain_h, bias_h, bin_h, bout_h, win_h.at[0], wout_h.at[0]]
        copies = [pltpu.make_async_copy(src, dst, sems.at[n]) for n, (src, dst) in enumerate(zip(srcs, outs))]
        for copy in copies:
            copy.start()
        for copy in copies:
            copy.wait()

    args = [table, hid, gain, bias, b_in, b_out, w_in, w_out]
    outs = [near(a.shape if 0 < n < 6 else a.shape[1:], a.dtype) for n, a in enumerate(args)]
    *got, token = call(kernel, outs, [], [], args, (), 0, 4, 8)
    return got[0], got[1], tuple(got[2:6]), got[6], got[7], token


def forward_first(own, other, table, hid, w_in, w_out, params, scale, deps=()):
    R, D = own.shape
    ff = w_in.shape[1]

    def kernel(ins, outs, scratch):
        own, other, table, hid, win, wout, gain, bias, b_in, b_out = ins
        low_a, low_b, act_h, slope_h, hlow_h, norm0_h, inv0_h, norm1_h, inv1_h = outs
        spec, hidden, act, slope, hlow, norm0, inv0, norm1, inv1, sems = scratch
        puts = [pltpu.make_async_copy(src, dst, sems.at[n]) for n, (src, dst) in enumerate(
            [(hlow, hlow_h), (norm0, norm0_h), (inv0, inv0_h), (act, act_h), (slope, slope_h), (norm1, norm1_h), (inv1, inv1_h)])]
        put = halves((low_a, low_b), R)

        def start(which):
            for n in which:
                puts[n].start()

        r = dict(table=table, hid=hid, pieces=[own, other], spec=spec, hidden=hidden, state=own, norm0=norm0, inv0=inv0,
                 hidden_low=hlow, w_in=win, w_out=wout, act=act, slope=slope, norm1=norm1, inv1=inv1, gain=gain, bias=bias,
                 b_in=b_in, b_out=b_out, chunk=CHUNK, put_state=lambda cut, value: put(cut, value.astype(bf16)),
                 wait_in=lambda: None, wait_out=lambda: None,
                 before_first=lambda: None, after_first=lambda: start((0, 1, 2)), after_ff=lambda: start((3, 4)))
        fwd_compute(0, R, scale, r)
        start((5, 6))
        for copy in puts:
            copy.wait()

    outs = [near((R // 2, D), bf16)] * 2 + [far((R, ff), bf16), far((R, ff), bf16), far((R, D), bf16),
            far((R, D), f32), far((R, 128), f32), far((R, D), f32), far((R, 128), f32)]
    scratch = [((2 * R, D), bf16), ((R, D), f32), ((R, ff), bf16), ((R, ff), bf16), ((R, D), bf16), ((R, D), f32),
               ((R, 128), f32), ((R, D), f32), ((R, 128), f32)]
    flops = 2 * R * D * (4 * R + 2 * D + 2 * ff)
    return call(kernel, outs, scratch, [own, other, table, hid, w_in, w_out, *params], [], deps, flops, 18, 7, range(2, 9))


def forward_back_last(place, size, layer, pieces, norm_in, cot, table, hid, w_in, w_out, params, scale, deps=()):
    R, D = norm_in.shape
    ff = w_in.shape[2]

    def kernel(ins, outs, scratch):
        *pieces, cot, table, hid, gain, bias, b_in, b_out, win_h, wout_h, norm_in_h = ins
        local_h, final_low_h, act, hlow, branch, pre, mix, resid, small = outs
        norm_in, final, final_low, spec, norm0, inv0, norm1, inv1, win, wout, sems = scratch
        get_norm = pltpu.make_async_copy(norm_in_h, norm_in, sems.at[4])
        get_in = pltpu.make_async_copy(win_h.at[layer], win, sems.at[0])
        get_out = pltpu.make_async_copy(wout_h.at[layer], wout, sems.at[1])
        get_norm.start()
        get_in.start()
        get_out.start()
        gain_b, bias_b = gain[layer - 1, 1:2, :], bias[layer - 1, 1:2, :]

        class State:
            def __getitem__(self, index):
                return norm_in[index] * gain_b + bias_b

        def put_state(cut, value):
            final[cut, :] = value

        def put_mix(cut, value):
            mix[cut, :] = value

        r = dict(table=table, hid=hid, pieces=pieces, spec=spec, hidden=resid, state=State(), norm0=norm0,
                 inv0=inv0, hidden_low=hlow, w_in=win, w_out=wout, act=act, slope=pre, norm1=norm1, inv1=inv1, gain=gain,
                 bias=bias, b_in=b_in, b_out=b_out, chunk=CHUNK, put_state=put_state, wait_in=get_in.wait,
                 wait_out=get_out.wait, resid=resid, resid_in=resid, branch_low=branch, pre_low=pre, small=small, put_mix=put_mix,
                 before_first=get_norm.wait, after_first=lambda: None, after_ff=lambda: None)
        small[...] = jnp.zeros_like(small)
        fwd_compute(layer, R, scale, r)
        block = place.row(size)
        final_low[...] = final[block, :].astype(bf16)
        puts = [pltpu.make_async_copy(final.at[block], local_h, sems.at[2]),
                pltpu.make_async_copy(final_low, final_low_h, sems.at[3])]
        for put in puts:
            put.start()
        last_norm_back(layer, R, r, lambda cut: cot[cut, :].astype(f32))
        ff_back_in(R, r)
        ff_back_out(layer, R, r)
        for put in puts:
            put.wait()

    outs = [far((size, D), f32), far((size, D), bf16), near((R, ff), bf16), near((R, D), bf16), near((R, D), bf16),
            near((R, ff), bf16), near((R, D), bf16), near((R, D), f32), near((SMALL_ROWS, D), f32)]
    scratch = [((R, D), f32), ((R, D), f32), ((size, D), bf16), ((2 * R, D), bf16), ((R, D), f32), ((R, 128), f32), ((R, D), f32), ((R, 128), f32),
               ((D, ff), bf16), ((ff, D), bf16)]
    flops = 2 * R * D * (4 * R + 2 * D + 4 * ff)
    return call(kernel, outs, scratch, [*pieces, cot, table, hid, *params], [w_in, w_out, norm_in], deps, flops, 22, 5, (0, 1))


def load_back(layer, norm1, inv1, w_out, deps=()):
    def kernel(ins, outs, scratch):
        norm1_h, inv1_h, wout_h = ins
        (sems,) = scratch
        gets = [pltpu.make_async_copy(src, dst, sems.at[n]) for n, (src, dst) in enumerate(
            zip([norm1_h, inv1_h, wout_h.at[layer]], outs))]
        for get in gets:
            get.start()
        for get in gets:
            get.wait()

    outs = [near(norm1.shape, f32), near(inv1.shape, f32), near(w_out.shape[1:], bf16)]
    return call(kernel, outs, [], [], [norm1, inv1, w_out], deps, sems=3)


def back_norm(layer, own, other, resid_in, norm1, inv1, table, hid, gain, slope, scale, deps=()):
    R, D = resid_in.shape

    def kernel(ins, outs, scratch):
        own, other, resid_in, norm1, inv1, table, hid, gain, slope_h = ins
        branch, resid, small, slope = outs
        spec, mixed_v, sems = scratch
        get = pltpu.make_async_copy(slope_h, slope, sems.at[0])
        get.start()
        small[...] = jnp.zeros_like(small)

        def after_mix(mixed):
            mixed_v[...] = mixed

        mix_phase(table, hid, [own, other], spec, R, scale, after_mix)
        r = dict(gain=gain, resid=resid, norm1=norm1, inv1=inv1, branch_low=branch, small=small)
        last_norm_back(layer, R, r, lambda cut: resid_in[cut, :] + mixed_v[cut, :])
        get.wait()

    outs = [near((R, D), bf16), near((R, D), f32), near((SMALL_ROWS, D), f32), near(slope.shape, bf16)]
    scratch = [((2 * R, D), bf16), ((R, D), f32)]
    flops = 2 * R * D * (4 * R + 2 * D)
    return call(kernel, outs, scratch, [own, other, resid_in, norm1, inv1, table, hid, gain], [slope], deps, flops, 6, 1)


def back_in(layer, branch, slope, w_out, small_in, w_in, norm0, inv0, deps=()):
    R, D = branch.shape
    ff = w_out.shape[0]

    def kernel(ins, outs, scratch):
        branch, slope, wout, small_in, win_h, norm0_h, inv0_h = ins
        pre, small, win, norm0, inv0 = outs
        (sems,) = scratch
        gets = [pltpu.make_async_copy(src, dst, sems.at[n]) for n, (src, dst) in enumerate(
            [(win_h.at[layer], win), (norm0_h, norm0), (inv0_h, inv0)])]
        for get in gets:
            get.start()
        small[...] = small_in[...]
        ff_back_in(R, dict(branch_low=branch, small=small, slope=slope, w_out=wout, pre_low=pre, chunk=CHUNK))
        for get in gets:
            get.wait()

    outs = [near((R, ff), bf16), near((SMALL_ROWS, D), f32), near((D, ff), bf16), near((R, D), f32), near((R, 128), f32)]
    return call(kernel, outs, [], [branch, slope, w_out, small_in], [w_in, norm0, inv0], deps, 2 * R * D * ff, 6, 3)


def back_out(layer, pre, resid_in, norm0, inv0, w_in, gain, small_in, deps=()):
    R, D = resid_in.shape
    ff = w_in.shape[1]

    def kernel(ins, outs, scratch):
        pre, resid_in, norm0, inv0, win, gain, small_in = ins
        mix_a, mix_b, resid, small = outs
        small[...] = small_in[...]
        ff_back_out(layer, R, dict(gain=gain, resid=resid, resid_in=resid_in, norm0=norm0, inv0=inv0, small=small, w_in=win,
                                   pre_low=pre, put_mix=halves((mix_a, mix_b), R)))

    outs = [near((R // 2, D), bf16)] * 2 + [near((R, D), f32), near((SMALL_ROWS, D), f32)]
    return call(kernel, outs, [], [pre, resid_in, norm0, inv0, w_in, gain, small_in], [], deps, 2 * R * D * ff, 6)


def mix_last(place, size, pieces, resid_in, final_low, table, hid, scale, deps=()):
    R, D = resid_in.shape

    def kernel(ins, outs, scratch):
        *pieces, resid_in, table, hid, final_low = ins
        local, low, low_final = outs
        spec, grad, sems = scratch
        get = pltpu.make_async_copy(final_low, low_final, sems.at[0])
        get.start()

        def after_mix(mixed):
            grad[...] = resid_in[...] + mixed

        mix_phase(table, hid, pieces, spec, R, scale, after_mix)
        cut = place.row(size)
        local[...] = grad[cut, :]
        low[...] = grad[cut, :].astype(bf16)
        get.wait()

    flops = 2 * R * D * (4 * R + 2 * D)
    return call(kernel, [near((size, D), f32)] + [near((size, D), bf16)] * 2, [((2 * R, D), bf16), ((R, D), f32)],
                [*pieces, resid_in, table, hid], [final_low], deps, flops, 7, 1)


def gather_rows(place, block, pieces, deps=(), tables=None):
    size, D = block.shape
    R = size * place.seq_count // 2

    def kernel(ins, outs, scratch):
        rows = outs[0]
        (sems,) = scratch
        home = place.home
        if tables is not None:
            *ins, tables_h = ins
            bring = pltpu.make_async_copy(tables_h.at[place.core], outs[1], sems.at[1])
            bring.start()

        def put(ref, mask):
            rows[place.row(size, mask), :] = ref[:size, :]

        @pl.when(home)
        def _():
            own = pltpu.make_async_copy(ins[-1], rows.at[place.row(size)], sems.at[0])
            own.start()
            for ref, (home_mask, _) in zip(ins, [p[1] for p in pieces]):
                if home_mask is not None:
                    put(ref, home_mask)
            own.wait()

        @pl.when(jnp.logical_not(home))
        def _():
            for ref, (_, away_mask) in zip(ins, [p[1] for p in pieces]):
                put(ref, away_mask)

        if tables is not None:
            bring.wait()

    outs, far_args = [near((R, D), block.dtype)], [block]
    if tables is not None:
        outs.append(near(tables.shape[1:], tables.dtype))
        far_args.append(tables)
    return call(kernel, outs, [], [p[0] for p in pieces], far_args, deps, 0, 4, 2)


def send_blocks(place, block):
    odd = [m for m in range(1, place.seq_count) if parity_of(m)]
    even = [m for m in range(1, place.seq_count) if not parity_of(m)]
    pieces = []
    for n, mask in enumerate(odd):
        pairs = [((t, 1 - parity_of(t)), (t ^ mask, parity_of(t))) for t in range(place.seq_count)]
        home_mask = None
        if n < len(even):
            home_mask = even[n]
            pairs += [((t, parity_of(t)), (t ^ home_mask, parity_of(t))) for t in range(place.seq_count)]
        pieces.append((place.send(block, pairs), (home_mask, mask)))
    return pieces


class Chain:
    def __init__(self, place, grads, pieces, pad):
        self.place = place
        self.m = len(grads)
        self.masks = [g[2] for g in grads]
        self.zs = place.batch_count // 2
        self.pad = pad
        self.extra, self.more, self.z_pad = None, 0, 0
        parts = []
        for left, right, mask in grads:
            span = left.shape[1] // place.seq_count
            self.n = span // place.batch_count
            self.width = right.shape[1]
            for slot in (place.s, place.s ^ mask):
                cut = lax.dynamic_slice(left, (0, slot * span), (left.shape[0], span))
                parts.append(dot(cut, right, ((0,), (0,))).astype(bf16))
        self.parts = parts
        zs, n, D = self.zs, self.n, self.width
        self.per = 2 * self.m // pieces

        def give(ins, outs, scratch):
            core = place.core
            for i, ref in enumerate(ins):
                for z in range(zs):
                    outs[i // self.per][pl.ds((i % self.per) * zs * n + z * n, n), :] = ref[self.rows(z, 1 - core), :]

        *gives, _ = call(give, [near((self.per * zs * n, D), bf16)] * pieces, [], parts, name="give")
        self.got = [place.swap(give) for give in gives]

    def rows(self, z, core):
        return pl.ds(pl.multiple_of(z * 2 * self.n + core * self.n, 32), self.n)

    def core_done(self, deps=(), extra=None, extra_got=()):
        zs, n, m, D = self.zs, self.n, self.m, self.width
        place = self.place
        if extra is not None:
            self.more = 2 * extra.shape[0]
        more = self.more

        def kernel(ins, outs, scratch):
            core = place.core
            keep, *gives = outs
            if more:
                *gives, total = gives
                messages = ins[len(ins) - len(extra_got) :]
                each = more // len(messages)
                parts = jnp.concatenate([ref[ref.shape[0] - each :, :] for ref in messages], axis=0)
                total[...] = one_part(two_parts(ins[2 * m + len(self.got)][...])) + one_part(parts)
                gives[-1][pl.ds(zs * n, more), :] = two_parts(total[...])
            for i in range(2 * m):
                got = ins[2 * m + i // self.per]
                for z in range(zs):
                    cut = pl.ds(z * n, n)
                    value = ins[i][self.rows(z, core), :].astype(f32)
                    value += got[pl.ds((i % self.per) * zs * n + z * n, n), :].astype(f32)
                    if i % 2 == 0:
                        keep[i // 2, cut, :] = value
                    else:
                        gives[i // 2][cut, :] = value.astype(bf16)

        pad = max(self.pad, more)
        outs = [near((m, zs * n, D), f32)] + [near((zs * n + pad, D), bf16)] * m
        args = self.parts + self.got
        if more:
            outs.append(near(extra.shape, f32))
            args = args + [extra, *extra_got]
        self.keep, *gives, self.token = call(kernel, outs, [], args, (), deps)
        if more:
            self.extra = gives.pop()
        self.got = [xor_send(give, "seq", mask) for give, mask in zip(gives, self.masks)]
        return self.token

    def seq_done(self, deps=(), carry=None, attach=None):
        if attach is not None:
            self.extra, self.more = attach, 2 * attach.shape[0]
        self.attached = attach is not None
        def read(ins):
            keep, *got = ins
            return (lambda i, cut: keep[i, cut, :] + got[i][cut, :].astype(f32)), got[-1]

        return self.z_step(0, read, [self.keep, *self.got], deps, carry)

    def z_done(self, deps=()):
        def read(ins):
            keep, got = ins
            return (lambda i, cut: keep[i, cut, :] + got[pl.ds(i * keep.shape[1] + cut.start, cut.size), :].astype(f32)), got

        return self.z_step(self.bit + 1, read, [self.keep, self.got], deps)

    def z_step(self, bit, read, args, deps, carry=None):
        m, n, D = self.m, self.n, self.width
        place = self.place
        self.bit = bit
        left = self.zs >> bit
        rows = left // 2 * n
        zs_rows = left * n if bit == 0 else m * left * n

        def kernel(ins, outs, scratch):
            keep, give = outs[:2]
            if carry is not None:
                *ins, carry_h = ins
                bring = pltpu.make_async_copy(carry_h, outs[-1], scratch[0].at[0])
                bring.start()
            if self.more:
                *ins, extra = ins
            value, last = read(ins)
            if self.more:
                total = outs[2]
                if bit == 0 and self.attached:
                    total[...] = extra[...]
                else:
                    total[...] = one_part(two_parts(extra[...])) + one_part(last[pl.ds(zs_rows, self.more), :])
                give[pl.ds(m * rows, self.more), :] = two_parts(total[...])
            mine = (place.z >> bit) & 1
            for i in range(m):
                for z in range(left // 2):
                    cut = pl.ds(z * n, n)
                    keep[i, cut, :] = value(i, pl.ds(pl.multiple_of((2 * z + mine) * n, 32), n))
                    other = value(i, pl.ds(pl.multiple_of((2 * z + 1 - mine) * n, 32), n))
                    give[pl.ds(i * rows + z * n, n), :] = other.astype(bf16)
            if carry is not None:
                bring.wait()

        outs = [near((m, rows, D), f32), near((m * rows + max(self.more, self.z_pad if bit == 0 else 0), D), bf16)]
        if self.more:
            outs.append(near(self.extra.shape, f32))
            args = [*args, self.extra]
        far_args = []
        if carry is not None:
            outs.append(near(carry.shape, carry.dtype))
            far_args = [carry]
        self.keep, give, *rest, self.token = call(kernel, outs, [], args, far_args, deps, 0, 6, len(far_args))
        if carry is not None:
            self.carried = rest.pop()
        if self.more:
            self.extra = rest.pop()
        self.got = xor_send(give, "batch", 2 << bit)
        return self.token

    def last(self, deps=()):
        m, n, D = self.m, self.n, self.width

        def kernel(ins, outs, scratch):
            for i in range(m):
                outs[0][i] = ins[0][i] + ins[1][pl.ds(i * n, n), :].astype(f32)

        self.total, self.token = call(kernel, [near((m, n, D), f32)], [], [self.keep, self.got], (), deps)
        return self.token


def two_parts(value):
    high = value.astype(bf16)
    return jnp.concatenate([high, (value - high.astype(f32)).astype(bf16)], axis=0)


def one_part(parts):
    rows = parts.shape[0] // 2
    return parts[:rows].astype(f32) + parts[rows:].astype(f32)


def choose(place, grad_local, final_local, got, deps=()):
    def kernel(ins, outs, scratch):
        home = place.home
        outs[0][...] = jnp.where(home, ins[0][...], ins[2][...].astype(f32))
        outs[1][...] = jnp.where(home, ins[1][...], ins[3][...].astype(f32))

    return call(kernel, [result(grad_local.shape, f32)] * 2, [], [grad_local, final_local, *got], [], deps)


def last_out(chain, upper, index, deps=()):
    n, D = upper.shape[1:]

    def kernel(ins, outs, scratch):
        keep, got, upper = ins
        outs[0][0] = keep[0] + got[:n, :].astype(f32)
        outs[0][1] = upper[index]

    return call(kernel, [result((2, n, D), f32)], [], [chain.keep, chain.got, upper], (), deps)


class SmallSum:
    def __init__(self, place, values):
        self.value, self.got = values, place.swap(values)
        self.sent = False

    def step(self, deps=()):
        def small_step(ins, outs, scratch):
            outs[0][...] = ins[0][...] + ins[1][...]

        self.value, tok = call(small_step, [near(self.value.shape, f32)], [], [self.value, self.got], (), deps, name="small_step")
        if not self.sent:
            self.got = xor_send(self.value, "seq", 2)
            self.sent = True
        return tok


def small_last(chain, ff, deps=()):
    rows, D = chain.extra.shape

    def kernel(ins, outs, scratch):
        gains, biases, bins, bouts = outs
        mine, got = ins
        total = one_part(two_parts(mine[...])) + one_part(got[pl.ds(got.shape[0] - 2 * rows, 2 * rows), :])
        for layer in range(2):
            part = total[layer * SMALL_ROWS : (layer + 1) * SMALL_ROWS]
            gains[layer] = part[0:2]
            biases[layer] = part[2:4]
            bouts[layer : layer + 1, :] = part[4:5]
            for n in range(ff // D):
                bins[layer : layer + 1, n * D : (n + 1) * D] = part[5 + n : 6 + n]

    outs = [result((2, 2, D), f32), result((2, 2, D), f32), result((2, ff), f32), result((2, D), f32)]
    return call(kernel, outs, [], [chain.extra, chain.got], (), deps)


def body(tables, hid_table, inputs, norm_gain, norm_bias, w_in, b_in, w_out, b_out, cotangent):
    place = Place()
    size = inputs.shape[1]
    width = inputs.shape[2]
    length = size * place.seq_count
    scale = 1.0 / math.sqrt(length * width)
    hid = jnp.asarray(hid_table)
    tables = jnp.asarray(tables)
    span = w_in.shape[2] // (place.seq_count * place.batch_count)
    if length > 1024 or span % 32 or w_in.shape[0] != 2 or place.batch_count != 8:
        table = lax.dynamic_index_in_dim(tables, place.core, 0, keepdims=False)
        return plain_body(table, hid, inputs, norm_gain, norm_bias, w_in, b_in, w_out, b_out, cotangent)

    pieces = send_blocks(place, inputs[0])
    cot_low = cotangent[0].astype(bf16)
    cot_send = jnp.pad(cot_low, ((0, 16), (0, 0)))
    table, hid, params, win0, wout0, tok = load(place, tables, hid, (norm_gain, norm_bias, b_in, b_out), w_in, w_out)
    norm_gain = params[0]
    own, tok = gather_rows(place, inputs[0], pieces, (tok, cot_send))
    cot_pieces = send_blocks(place, cot_send)
    other = place.swap(own)
    state_a, state_b, act0, slope0, hlow0, norm00, inv00, norm01_far, inv01_far, tok = forward_first(
        own, other, table, hid, win0, wout0, params, scale, (tok,))
    others = [place.swap(half) for half in (state_a, state_b)]
    cot, table_b, tok = gather_rows(place, cot_low, cot_pieces, (tok,), tables)
    final_local, final_low, act1, hlow1, branch1, pre1, mix1, resid1, small1, tok = forward_back_last(
        place, size, 1, [state_a, state_b, *others], norm01_far, cot, table_b, hid, w_in, w_out, params, scale, (tok,))
    mix1_other = place.swap(mix1)
    grads1 = Chain(place, [(act1, branch1, 1), (pre1, hlow1, 2)], 4, 32)
    norm01, inv01, wout0, tok = load_back(0, norm01_far, inv01_far, w_out, (tok,))
    tok = grads1.core_done((tok,))
    branch0, resid0, small0, slope0, tok = back_norm(
        0, mix1, mix1_other, resid1, norm01, inv01, table, hid, norm_gain, slope0, scale, (tok,))
    out0 = Chain(place, [(act0, branch0, 1)], 2, 16)
    pre0, small0, win0, norm00, inv00, tok = back_in(0, branch0, slope0, wout0, small0, w_in, norm00, inv00, (tok,))
    tok = out0.core_done((tok,))
    mix_a, mix_b, resid0, small0, tok = back_out(0, pre0, resid0, norm00, inv00, win0, norm_gain, small0, (tok,))
    small = SmallSum(place, jnp.concatenate([small0, small1]))
    others = [place.swap(half) for half in (mix_a, mix_b)]
    tok = grads1.seq_done((tok,), hlow0)
    in0 = Chain(place, [(pre0, grads1.carried, 2)], 2, 16)
    tok = small.step((tok,))
    tok = in0.core_done((tok,))
    tok = small.step((tok,))
    grad_local, low, low_final, tok = mix_last(
        place, size, [mix_a, mix_b, *others], resid0, final_low, table, hid, scale, (tok,))
    back = [place.send_back(low), place.send_back(low_final)]
    tok = grads1.z_done((tok,))
    tok = out0.seq_done((tok,), None, small.value)
    tok = in0.seq_done((tok,))
    tok = out0.z_done((tok,))
    tok = grads1.last((tok,))
    tok = in0.z_done((tok,))
    gains, biases, bin_, bout, tok = small_last(out0, w_in.shape[2], (tok,))
    wout, tok = last_out(out0, grads1.total, 0, (tok,))
    input_grad, outputs, tok = choose(place, grad_local, final_local, back, (tok,))
    win, tok = last_out(in0, grads1.total, 1, (tok,))
    return (outputs[None], input_grad[None], gains, biases, jnp.swapaxes(win, 1, 2), bin_, wout, bout)


def solution(mesh):
    def run(inputs, norm_gain, norm_bias, w_in, b_in, w_out, b_out, cotangent):
        tables = seq_tables(inputs.shape[1], mesh.shape["seq"])
        cos_hid, sin_hid = np_tables(inputs.shape[2])
        hid_table = np.concatenate([cos_hid, -sin_hid], axis=0)

        def inner(*args):
            return body(tables, hid_table, *args)

        return jax.shard_map(
            inner,
            mesh=mesh,
            in_specs=(P("batch", "seq", None), P(), P(), P(), P(), P(), P(), P("batch", "seq", None)),
            out_specs=(
                P("batch", "seq", None),
                P("batch", "seq", None),
                P(),
                P(),
                P(None, None, ("seq", "batch")),
                P(),
                P(None, ("seq", "batch"), None),
                P(),
            ),
            check_vma=False,
        )(inputs, norm_gain, norm_bias, w_in, b_in, w_out, b_out, cotangent)

    return run
```

```python
import functools
import math

import jax
import jax.numpy as jnp
import numpy as np
from jax import lax
from jax.experimental import pallas as pl
from jax.experimental.pallas import tpu as pltpu
from jax.sharding import PartitionSpec as P

eps_norm = 1e-05
bf16 = jnp.bfloat16
f32 = jnp.float32


def parity_of(index):
    return bin(index).count("1") & 1


def np_tables(modulus):
    ids = np.arange(modulus, dtype=np.int64)
    product = (ids[:, None] * ids[None, :]) % modulus
    angles = product.astype(np.float32) * np.float32(2.0 * math.pi / modulus)
    return np.cos(angles).astype(bf16), np.sin(angles).astype(bf16)


def seq_tables(length, seq_count):
    rows = length // seq_count
    cos_t, sin_t = np_tables(length)
    ids = [
        np.concatenate([np.arange(t * rows, (t + 1) * rows) for t in range(seq_count) if parity_of(t) == c])
        for c in (0, 1)
    ]
    out = []
    for c in (0, 1):
        cols = np.concatenate([ids[c], ids[1 - c]])
        out.append(np.concatenate([t[ids[c]][:, cols] for t in (cos_t, sin_t)], axis=0))
    return np.stack(out)


class Place:
    def __init__(self):
        self.seq_count = lax.axis_size("seq")
        self.batch_count = lax.axis_size("batch")

    @property
    def s(self):
        return lax.axis_index("seq")

    @property
    def core(self):
        return lax.axis_index("batch") & 1

    @property
    def home(self):
        bits = self.s
        for shift in (4, 2, 1):
            bits = bits ^ (bits >> shift)
        return self.core == (bits & 1)

    def send(self, value, pairs):
        n = self.batch_count
        full = [
            (s0 * n + 2 * z + c0, s1 * n + 2 * z + c1)
            for (s0, c0), (s1, c1) in pairs
            for z in range(n // 2)
        ]
        return lax.ppermute(value, ("seq", "batch"), full)

    def swap(self, value):
        return xor_send(value, "batch", 1)

    @property
    def z(self):
        return lax.axis_index("batch") >> 1

    def row(self, size, mask=0):
        return pl.ds(pl.multiple_of(((self.s ^ mask) >> 1) * size, size), size)

    def send_back(self, low):
        pairs = [((t, 1 - parity_of(t)), (t ^ 1, parity_of(t))) for t in range(self.seq_count)]
        return self.send(low, pairs)

    def collect(self, block):
        odd = [m for m in range(1, self.seq_count) if parity_of(m)]
        even = [m for m in range(1, self.seq_count) if not parity_of(m)]
        size = block.shape[0]
        buffer = jnp.zeros((size * self.seq_count // 2, block.shape[1]), block.dtype)

        def put(buffer, piece, block_id):
            return lax.dynamic_update_slice(buffer, piece, ((block_id >> 1) * size, 0))

        for n, mask in enumerate(odd):
            pairs = [((t, 1 - parity_of(t)), (t ^ mask, parity_of(t))) for t in range(self.seq_count)]
            ids = self.s ^ mask
            piece = None
            if n < len(even):
                pairs += [((t, parity_of(t)), (t ^ even[n], parity_of(t))) for t in range(self.seq_count)]
                ids = jnp.where(self.home, self.s ^ even[n], ids)
                piece = self.send(block, pairs)
            else:
                ids = jnp.where(self.home, self.s, ids)
                piece = jnp.where(self.home, block, self.send(block, pairs))
            buffer = put(buffer, piece, ids)
        return buffer

    def give_back(self, rows, size):
        local = lax.dynamic_slice(rows, ((self.s >> 1) * size, 0), (size, rows.shape[1]))
        pairs = [((t, 1 - parity_of(t)), (t ^ 1, parity_of(t))) for t in range(self.seq_count)]
        got = self.send(local.astype(bf16), pairs)
        return jnp.where(self.home, local, got.astype(f32))


def xor_send(value, axis, mask):
    size = lax.axis_size(axis)
    return lax.ppermute(value, axis, [(i, i ^ mask) for i in range(size)])


def dot(a, b, dims=((1,), (0,))):
    return lax.dot_general(a, b, (dims, ((), ())), preferred_element_type=f32)


def dot_t(a, b):
    return dot(a, b, ((1,), (1,)))


def gelu_both(z):
    k = math.sqrt(2.0 / math.pi)
    z2 = z * z
    t = jnp.tanh(z * (k + (k * 0.044715) * z2))
    half = 0.5 + 0.5 * t
    act = z * half
    slope = half + act * (1.0 - half) * (2.0 * k + (6.0 * k * 0.044715) * z2)
    return act, slope


def row_loop(rows, step, fn, init=0):
    def one(i, carry):
        return fn(pl.ds(pl.multiple_of(i * step, step), step), carry)

    return lax.fori_loop(0, rows // step, one, init)


def mean_of(v):
    return jnp.mean(v, axis=-1, keepdims=True)


def norm_fwd(v):
    centered = v - mean_of(v)
    inv = lax.rsqrt(mean_of(centered * centered) + eps_norm)
    return centered * inv, inv


def norm_bwd(up, normed, inv, gain):
    scaled = up * gain
    return inv * (scaled - mean_of(scaled) - normed * mean_of(scaled * normed))


def wide(inv):
    return jnp.broadcast_to(inv, (inv.shape[0], 128))


def mix_phase(table, hid, pieces, spec, rows, scale, each):
    width = hid.shape[1]
    for part in range(2):
        cut = pl.ds(part * rows, rows)
        value, start = None, 0
        for piece in pieces:
            count = piece.shape[0] // 128 * 128
            term = dot(table[cut, start : start + count], piece[:count, :])
            value = term if value is None else value + term
            start += count
        spec[cut, :] = (value * scale).astype(bf16)
    mixed = dot(spec[pl.ds(0, rows), :], hid[pl.ds(0, width), :])
    mixed += dot(spec[pl.ds(rows, rows), :], hid[pl.ds(width, width), :])
    each(mixed)


STEP = 128


def fwd_compute(layer, rows, scale, refs):
    r = refs
    def after_mix(mixed):
        r["hidden"][...] = mixed
    mix_phase(r["table"], r["hid"], r["pieces"], r["spec"], rows, scale, after_mix)
    gain0, bias0 = r["gain"][layer, 0:1, :], r["bias"][layer, 0:1, :]
    gain1, bias1 = r["gain"][layer, 1:2, :], r["bias"][layer, 1:2, :]

    def first(cut, carry):
        normed, inv = norm_fwd(r["state"][cut, :].astype(f32) + r["hidden"][cut, :])
        r["norm0"][cut, :] = normed
        r["inv0"][cut, :] = wide(inv)
        hidden = normed * gain0 + bias0
        r["hidden"][cut, :] = hidden
        r["hidden_low"][cut, :] = hidden.astype(bf16)
        return carry

    r["before_first"]()
    row_loop(rows, STEP, first)
    r["after_first"]()
    r["wait_in"]()
    ff = r["w_in"].shape[1]
    chunk = r["chunk"]
    r["wait_out"]()
    r["norm1"][...] = jnp.zeros_like(r["norm1"])

    def chunk_step(j, carry):
        cut = pl.ds(pl.multiple_of(j * chunk, chunk), chunk)
        z = dot(r["hidden_low"][...], r["w_in"][:, cut]) + r["b_in"][layer : layer + 1, cut]
        act, slope = gelu_both(z)
        act = act.astype(bf16)
        r["act"][:, cut] = act
        r["slope"][:, cut] = slope.astype(bf16)
        r["norm1"][...] += dot(act, r["w_out"][cut, :])
        return carry

    lax.fori_loop(0, ff // chunk, chunk_step, 0)
    r["after_ff"]()
    b_out = r["b_out"][layer : layer + 1, :]

    def second(cut, carry):
        normed, inv = norm_fwd(r["hidden"][cut, :] + (r["norm1"][cut, :] + b_out))
        r["norm1"][cut, :] = normed
        r["inv1"][cut, :] = wide(inv)
        r["put_state"](cut, normed * gain1 + bias1)
        return carry

    row_loop(rows, STEP, second)


def zero_sums(rows8):
    return tuple(jnp.zeros((8, n), f32) for n in rows8)


def fold(v):
    return jnp.sum(v.reshape(v.shape[0] // 8, 8, v.shape[1]), axis=0)


def last_norm_back(layer, rows, refs, upstream):
    r = refs
    gain1 = r["gain"][layer, 1:2, :]
    width = r["resid"].shape[1]

    def back(cut, sums):
        up, normed = upstream(cut), r["norm1"][cut, :]
        resid = norm_bwd(up, normed, r["inv1"][cut, :1], gain1)
        low = resid.astype(bf16)
        r["resid"][cut, :] = resid
        r["branch_low"][cut, :] = low
        return (sums[0] + fold(up * normed), sums[1] + fold(up), sums[2] + fold(low.astype(f32)))

    sums = row_loop(rows, STEP, back, zero_sums((width,) * 3))
    for slot, value in zip((1, 3, 4), sums):
        r["small"][slot : slot + 1, :] = jnp.sum(value, axis=0, keepdims=True)


def ff_back_in(rows, refs):
    r = refs
    ff = r["pre_low"].shape[1]
    chunk = r["chunk"]
    width = r["small"].shape[1]
    def chunk_step(j, carry):
        cut = pl.ds(pl.multiple_of(j * chunk, chunk), chunk)
        act_grad = dot_t(r["branch_low"][...], r["w_out"][cut, :])
        if "wait_slope" in r:
            r["wait_slope"](j)
        low = (act_grad * r["slope"][:, cut].astype(f32)).astype(bf16)
        r["pre_low"][:, cut] = low
        sums = jnp.sum(low.astype(f32), axis=0, keepdims=True)
        for n in range(chunk // width):
            r["small"][pl.ds(5 + j * (chunk // width) + n, 1), :] = sums[:, n * width : (n + 1) * width]
        return carry

    lax.fori_loop(0, ff // chunk, chunk_step, 0)


def ff_back_out(layer, rows, refs):
    r = refs
    width = r["resid"].shape[1]
    r["resid"][...] = r["resid_in"][...]

    def chunk_step(j, carry):
        cut = pl.ds(pl.multiple_of(j * FF_CUT, FF_CUT), FF_CUT)
        r["resid"][...] += dot_t(r["pre_low"][:, cut], r["w_in"][:, cut])
        return carry

    lax.fori_loop(0, r["pre_low"].shape[1] // FF_CUT, chunk_step, 0)
    gain0 = r["gain"][layer, 0:1, :]

    def back(cut, sums):
        up, normed = r["resid"][cut, :], r["norm0"][cut, :]
        resid = norm_bwd(up, normed, r["inv0"][cut, :1], gain0)
        r["resid"][cut, :] = resid
        r["put_mix"](cut, resid.astype(bf16))
        return (sums[0] + fold(up * normed), sums[1] + fold(up))

    sums = row_loop(rows, STEP, back, zero_sums((width,) * 2))
    for slot, value in zip((0, 2), sums):
        r["small"][slot : slot + 1, :] = jnp.sum(value, axis=0, keepdims=True)
def layer_norm(values, gain_vec, bias_vec):
    centered = values - jnp.mean(values, axis=-1, keepdims=True)
    inv_std = lax.rsqrt(jnp.mean(centered * centered, axis=-1, keepdims=True) + eps_norm)
    normed = centered * inv_std
    return (normed * gain_vec + bias_vec, normed, inv_std)


def norm_back(upstream, normed, inv_std, gain_vec):
    gain_grad = jnp.sum(upstream * normed, axis=0)
    bias_grad = jnp.sum(upstream, axis=0)
    scaled = upstream * gain_vec
    inner = (
        scaled
        - jnp.mean(scaled, axis=-1, keepdims=True)
        - normed * jnp.mean(scaled * normed, axis=-1, keepdims=True)
    )
    return (inv_std * inner, gain_grad, bias_grad)


def exchange_sum(part, axis_name, bit, dim, out_dtype):
    mine = (lax.axis_index(axis_name) >> bit) & 1
    keep = lax.dynamic_index_in_dim(part, mine, dim, keepdims=False)
    give = lax.dynamic_index_in_dim(part, 1 - mine, dim, keepdims=False)
    got = xor_send(give, axis_name, 1 << bit)
    return (keep.astype(f32) + got.astype(f32)).astype(out_dtype)


def slot_grad(place, left, right, mask):
    batch_bits = place.batch_count.bit_length() - 1
    span = left.shape[1] // place.seq_count

    def one(slot):
        cut = lax.dynamic_slice(left, (0, slot * span), (left.shape[0], span))
        return dot(cut, right, ((0,), (0,))).astype(bf16)

    part = jnp.stack([one(place.s), one(place.s ^ mask)])
    part = part.reshape((2,) + (2,) * batch_bits + (-1, right.shape[1]))
    part = exchange_sum(part, "batch", 0, batch_bits, bf16)
    part = (part[0].astype(f32) + xor_send(part[1], "seq", mask).astype(f32)).astype(bf16)
    for bit in range(1, batch_bits):
        part = exchange_sum(part, "batch", bit, batch_bits - 1 - bit, f32 if bit == batch_bits - 1 else bf16)
    return part


def all_sum(vec):
    vec = vec + xor_send(vec, "batch", 1)
    vec = vec + xor_send(vec, "seq", 1)
    for bit in range(1, lax.axis_size("batch").bit_length() - 1):
        vec = vec + xor_send(vec, "batch", 1 << bit)
    return vec


def plain_body(table, hid_table, inputs, norm_gain, norm_bias, w_in, b_in, w_out, b_out, cotangent):
    place = Place()
    size = inputs.shape[1]
    width = inputs.shape[2]
    length = size * place.seq_count
    rows = length // 2
    layers = w_in.shape[0]
    dft_scale = 1.0 / math.sqrt(length * width)

    def mix(block):
        pieces = jnp.concatenate([block, place.swap(block)], axis=0)
        spec = (dot(table, pieces) * dft_scale).astype(bf16)
        return dot(spec[:rows], hid_table[:width]) + dot(spec[rows:], hid_table[width:])

    state = place.collect(inputs[0]).astype(f32)
    stored = []
    for layer_id in range(layers):
        mixed = mix(state.astype(bf16))
        hidden, normed_mix, inv_mix = layer_norm(state + mixed, norm_gain[layer_id, 0], norm_bias[layer_id, 0])
        hidden_low = hidden.astype(bf16)
        act, slope = gelu_both(dot(hidden_low, w_in[layer_id]) + b_in[layer_id])
        act_low, slope = act.astype(bf16), slope.astype(bf16)
        branch = dot(act_low, w_out[layer_id]) + b_out[layer_id]
        state, normed_ff, inv_ff = layer_norm(hidden + branch, norm_gain[layer_id, 1], norm_bias[layer_id, 1])
        stored.append((hidden_low, slope, act_low, normed_mix, inv_mix, normed_ff, inv_ff))
    outputs = place.give_back(state, size)
    upstream = place.collect(cotangent[0].astype(bf16)).astype(f32)
    win_out, wout_out, small_out = [None] * layers, [None] * layers, [None] * layers
    for layer_id in reversed(range(layers)):
        hidden_low, slope, act_low, normed_mix, inv_mix, normed_ff, inv_ff = stored[layer_id]
        resid_ff, gain_ff, bias_ff = norm_back(upstream, normed_ff, inv_ff, norm_gain[layer_id, 1])
        branch_grad = resid_ff.astype(bf16)
        bout = jnp.sum(branch_grad.astype(f32), axis=0)
        pre_grad = (dot(branch_grad, w_out[layer_id], ((1,), (1,))) * slope.astype(f32)).astype(bf16)
        bin_ = jnp.sum(pre_grad.astype(f32), axis=0)
        hidden_grad = resid_ff + dot(pre_grad, w_in[layer_id], ((1,), (1,)))
        resid_mix, gain_mix, bias_mix = norm_back(hidden_grad, normed_mix, inv_mix, norm_gain[layer_id, 0])
        wout_out[layer_id] = slot_grad(place, act_low, branch_grad, 1)
        win_out[layer_id] = slot_grad(place, pre_grad, hidden_low, 2).T
        small_out[layer_id] = all_sum(jnp.concatenate([gain_mix, gain_ff, bias_mix, bias_ff, bout, bin_]))
        upstream = resid_mix + mix(resid_mix.astype(bf16))
    small = jnp.stack(small_out)
    gains = small[:, : 2 * width].reshape(layers, 2, width)
    biases = small[:, 2 * width : 4 * width].reshape(layers, 2, width)
    bout = small[:, 4 * width : 5 * width]
    bin_ = small[:, 5 * width :]
    input_grad = place.give_back(upstream, size)
    return (outputs[None], input_grad[None], gains, biases, jnp.stack(win_out), bin_, jnp.stack(wout_out), bout)


SMALL_ROWS = 16
CHUNK = 1536
FF_CUT = 3072


def near(shape, dtype):
    return pltpu.VMEM(shape, dtype)


def halves(refs, rows):
    half = rows // 2

    def put(cut, value):
        first = cut.start < half

        @pl.when(first)
        def _():
            refs[0][cut, :] = value

        @pl.when(jnp.logical_not(first))
        def _():
            refs[1][pl.ds(pl.multiple_of(cut.start - half, STEP), STEP), :] = value

    return put


def far(shape, dtype):
    return pltpu.HBM(shape, dtype)


def result(shape, dtype):
    return jax.ShapeDtypeStruct(shape, dtype)


def sys_name(kernel):
    return kernel.__qualname__.split(".<locals>")[0].split(".")[-1]


def call(kernel, outs, scratch, args, far_args=(), deps=(), flops=0, limit=4, sems=0, far_outs=(), name=None):
    nbytes = sum(a.size * a.dtype.itemsize for a in args)
    vmem = pl.BlockSpec(memory_space=pltpu.VMEM)
    hbm = pl.BlockSpec(memory_space=pl.ANY)
    n_in, n_dep, n_out = len(args) + len(far_args), len(deps), len(outs)

    def run(*refs):
        token = refs[n_in + n_dep + n_out]
        token[...] = jnp.zeros_like(token)
        kernel(refs[:n_in], refs[n_in + n_dep : n_in + n_dep + n_out], refs[n_in + n_dep + n_out + 1 :])

    scratch_shapes = [pltpu.VMEM(s, d) for s, d in scratch]
    if sems:
        scratch_shapes.append(pltpu.SemaphoreType.DMA((sems,)))
    return pl.pallas_call(
        run,
        name=name or sys_name(kernel),
        in_specs=[vmem] * len(args) + [hbm] * (len(far_args) + n_dep),
        out_specs=[hbm if o in far_outs else vmem for o in range(n_out + 1)],
        out_shape=list(outs) + [near((8, 128), f32)],
        scratch_shapes=scratch_shapes,
        compiler_params=pltpu.CompilerParams(vmem_limit_bytes=limit << 20),
        cost_estimate=pl.CostEstimate(flops=0, bytes_accessed=0, transcendentals=0),
    )(*[pltpu.with_memory_space_constraint(a, pltpu.VMEM) for a in args],
      *[pltpu.with_memory_space_constraint(a, pltpu.HBM) for a in far_args], *deps)


def load(place, table, hid, params, w_in, w_out):
    gain, bias, b_in, b_out = params

    def kernel(ins, outs, scratch):
        (sems,) = scratch
        table_h, hid_h, gain_h, bias_h, bin_h, bout_h, win_h, wout_h = ins
        srcs = [table_h.at[place.core], hid_h, gain_h, bias_h, bin_h, bout_h, win_h.at[0], wout_h.at[0]]
        copies = [pltpu.make_async_copy(src, dst, sems.at[n]) for n, (src, dst) in enumerate(zip(srcs, outs))]
        for copy in copies:
            copy.start()
        for copy in copies:
            copy.wait()

    args = [table, hid, gain, bias, b_in, b_out, w_in, w_out]
    outs = [near(a.shape if 0 < n < 6 else a.shape[1:], a.dtype) for n, a in enumerate(args)]
    *got, token = call(kernel, outs, [], [], args, (), 0, 4, 8)
    return got[0], got[1], tuple(got[2:6]), got[6], got[7], token


def forward_first(own, other, table, hid, w_in, w_out, params, scale, deps=()):
    R, D = own.shape
    ff = w_in.shape[1]

    def kernel(ins, outs, scratch):
        own, other, table, hid, win, wout, gain, bias, b_in, b_out = ins
        low_a, low_b, act_h, slope_h, hlow_h, norm0_h, inv0_h, norm1_h, inv1_h = outs
        spec, hidden, act, slope, hlow, norm0, inv0, norm1, inv1, sems = scratch
        puts = [pltpu.make_async_copy(src, dst, sems.at[n]) for n, (src, dst) in enumerate(
            [(hlow, hlow_h), (norm0, norm0_h), (inv0, inv0_h), (act, act_h), (slope, slope_h), (norm1, norm1_h), (inv1, inv1_h)])]
        put = halves((low_a, low_b), R)

        def start(which):
            for n in which:
                puts[n].start()

        r = dict(table=table, hid=hid, pieces=[own, other], spec=spec, hidden=hidden, state=own, norm0=norm0, inv0=inv0,
                 hidden_low=hlow, w_in=win, w_out=wout, act=act, slope=slope, norm1=norm1, inv1=inv1, gain=gain, bias=bias,
                 b_in=b_in, b_out=b_out, chunk=CHUNK, put_state=lambda cut, value: put(cut, value.astype(bf16)),
                 wait_in=lambda: None, wait_out=lambda: None,
                 before_first=lambda: None, after_first=lambda: start((0, 1, 2)), after_ff=lambda: start((3, 4)))
        fwd_compute(0, R, scale, r)
        start((5, 6))
        for copy in puts:
            copy.wait()

    outs = [near((R // 2, D), bf16)] * 2 + [far((R, ff), bf16), far((R, ff), bf16), far((R, D), bf16),
            far((R, D), f32), far((R, 128), f32), far((R, D), f32), far((R, 128), f32)]
    scratch = [((2 * R, D), bf16), ((R, D), f32), ((R, ff), bf16), ((R, ff), bf16), ((R, D), bf16), ((R, D), f32),
               ((R, 128), f32), ((R, D), f32), ((R, 128), f32)]
    flops = 2 * R * D * (4 * R + 2 * D + 2 * ff)
    return call(kernel, outs, scratch, [own, other, table, hid, w_in, w_out, *params], [], deps, flops, 24, 7, range(2, 9))


def forward_back_last(place, size, layer, pieces, norm_in, cot, table, hid, w_in, w_out, params, scale, deps=()):
    R, D = norm_in.shape
    ff = w_in.shape[2]

    def kernel(ins, outs, scratch):
        *pieces, cot, table, hid, gain, bias, b_in, b_out, win_h, wout_h, norm_in_h = ins
        local_h, final_low_h, act, hlow, branch, pre, mix, resid, small = outs
        norm_in, final, final_low, spec, norm0, inv0, norm1, inv1, win, wout, sems = scratch
        get_norm = pltpu.make_async_copy(norm_in_h, norm_in, sems.at[4])
        get_in = pltpu.make_async_copy(win_h.at[layer], win, sems.at[0])
        get_out = pltpu.make_async_copy(wout_h.at[layer], wout, sems.at[1])
        get_norm.start()
        get_in.start()
        get_out.start()
        gain_b, bias_b = gain[layer - 1, 1:2, :], bias[layer - 1, 1:2, :]

        class State:
            def __getitem__(self, index):
                return norm_in[index] * gain_b + bias_b

        def put_state(cut, value):
            final[cut, :] = value

        def put_mix(cut, value):
            mix[cut, :] = value

        r = dict(table=table, hid=hid, pieces=pieces, spec=spec, hidden=resid, state=State(), norm0=norm0,
                 inv0=inv0, hidden_low=hlow, w_in=win, w_out=wout, act=act, slope=pre, norm1=norm1, inv1=inv1, gain=gain,
                 bias=bias, b_in=b_in, b_out=b_out, chunk=CHUNK, put_state=put_state, wait_in=get_in.wait,
                 wait_out=get_out.wait, resid=resid, resid_in=resid, branch_low=branch, pre_low=pre, small=small, put_mix=put_mix,
                 before_first=get_norm.wait, after_first=lambda: None, after_ff=lambda: None)
        small[...] = jnp.zeros_like(small)
        fwd_compute(layer, R, scale, r)
        block = place.row(size)
        final_low[...] = final[block, :].astype(bf16)
        puts = [pltpu.make_async_copy(final.at[block], local_h, sems.at[2]),
                pltpu.make_async_copy(final_low, final_low_h, sems.at[3])]
        for put in puts:
            put.start()
        last_norm_back(layer, R, r, lambda cut: cot[cut, :].astype(f32))
        ff_back_in(R, r)
        ff_back_out(layer, R, r)
        for put in puts:
            put.wait()

    outs = [far((size, D), f32), far((size, D), bf16), near((R, ff), bf16), near((R, D), bf16), near((R, D), bf16),
            near((R, ff), bf16), near((R, D), bf16), near((R, D), f32), near((SMALL_ROWS, D), f32)]
    scratch = [((R, D), f32), ((R, D), f32), ((size, D), bf16), ((2 * R, D), bf16), ((R, D), f32), ((R, 128), f32), ((R, D), f32), ((R, 128), f32),
               ((D, ff), bf16), ((ff, D), bf16)]
    flops = 2 * R * D * (4 * R + 2 * D + 4 * ff)
    return call(kernel, outs, scratch, [*pieces, cot, table, hid, *params], [w_in, w_out, norm_in], deps, flops, 28, 5, (0, 1))


def load_back(layer, norm1, inv1, w_out, deps=()):
    def kernel(ins, outs, scratch):
        norm1_h, inv1_h, wout_h = ins
        (sems,) = scratch
        gets = [pltpu.make_async_copy(src, dst, sems.at[n]) for n, (src, dst) in enumerate(
            zip([norm1_h, inv1_h, wout_h.at[layer]], outs))]
        for get in gets:
            get.start()
        for get in gets:
            get.wait()

    outs = [near(norm1.shape, f32), near(inv1.shape, f32), near(w_out.shape[1:], bf16)]
    return call(kernel, outs, [], [], [norm1, inv1, w_out], deps, sems=3)


def back_norm(layer, own, other, resid_in, norm1, inv1, table, hid, gain, slope, scale, deps=()):
    R, D = resid_in.shape

    def kernel(ins, outs, scratch):
        own, other, resid_in, norm1, inv1, table, hid, gain, slope_h = ins
        branch, resid, small, slope = outs
        spec, mixed_v, sems = scratch
        get = pltpu.make_async_copy(slope_h, slope, sems.at[0])
        get.start()
        small[...] = jnp.zeros_like(small)

        def after_mix(mixed):
            mixed_v[...] = mixed

        mix_phase(table, hid, [own, other], spec, R, scale, after_mix)
        r = dict(gain=gain, resid=resid, norm1=norm1, inv1=inv1, branch_low=branch, small=small)
        last_norm_back(layer, R, r, lambda cut: resid_in[cut, :] + mixed_v[cut, :])
        get.wait()

    outs = [near((R, D), bf16), near((R, D), f32), near((SMALL_ROWS, D), f32), near(slope.shape, bf16)]
    scratch = [((2 * R, D), bf16), ((R, D), f32)]
    flops = 2 * R * D * (4 * R + 2 * D)
    return call(kernel, outs, scratch, [own, other, resid_in, norm1, inv1, table, hid, gain], [slope], deps, flops, 6, 1)


def back_in(layer, branch, slope, w_out, small_in, w_in, norm0, inv0, deps=()):
    R, D = branch.shape
    ff = w_out.shape[0]

    def kernel(ins, outs, scratch):
        branch, slope, wout, small_in, win_h, norm0_h, inv0_h = ins
        pre, small, win, norm0, inv0 = outs
        (sems,) = scratch
        gets = [pltpu.make_async_copy(src, dst, sems.at[n]) for n, (src, dst) in enumerate(
            [(win_h.at[layer], win), (norm0_h, norm0), (inv0_h, inv0)])]
        for get in gets:
            get.start()
        small[...] = small_in[...]
        ff_back_in(R, dict(branch_low=branch, small=small, slope=slope, w_out=wout, pre_low=pre, chunk=CHUNK))
        for get in gets:
            get.wait()

    outs = [near((R, ff), bf16), near((SMALL_ROWS, D), f32), near((D, ff), bf16), near((R, D), f32), near((R, 128), f32)]
    return call(kernel, outs, [], [branch, slope, w_out, small_in], [w_in, norm0, inv0], deps, 2 * R * D * ff, 10, 3)


def back_out(layer, pre, resid_in, norm0, inv0, w_in, gain, small_in, deps=()):
    R, D = resid_in.shape
    ff = w_in.shape[1]

    def kernel(ins, outs, scratch):
        pre, resid_in, norm0, inv0, win, gain, small_in = ins
        mix_a, mix_b, resid, small = outs
        small[...] = small_in[...]
        ff_back_out(layer, R, dict(gain=gain, resid=resid, resid_in=resid_in, norm0=norm0, inv0=inv0, small=small, w_in=win,
                                   pre_low=pre, put_mix=halves((mix_a, mix_b), R)))

    outs = [near((R // 2, D), bf16)] * 2 + [near((R, D), f32), near((SMALL_ROWS, D), f32)]
    return call(kernel, outs, [], [pre, resid_in, norm0, inv0, w_in, gain, small_in], [], deps, 2 * R * D * ff, 6)


def mix_last(place, size, pieces, resid_in, final_low, table, hid, scale, deps=()):
    R, D = resid_in.shape

    def kernel(ins, outs, scratch):
        *pieces, resid_in, table, hid, final_low = ins
        local, low, low_final = outs
        spec, grad, sems = scratch
        get = pltpu.make_async_copy(final_low, low_final, sems.at[0])
        get.start()

        def after_mix(mixed):
            grad[...] = resid_in[...] + mixed

        mix_phase(table, hid, pieces, spec, R, scale, after_mix)
        cut = place.row(size)
        local[...] = grad[cut, :]
        low[...] = grad[cut, :].astype(bf16)
        get.wait()

    flops = 2 * R * D * (4 * R + 2 * D)
    return call(kernel, [near((size, D), f32)] + [near((size, D), bf16)] * 2, [((2 * R, D), bf16), ((R, D), f32)],
                [*pieces, resid_in, table, hid], [final_low], deps, flops, 7, 1)


def gather_rows(place, block, pieces, deps=(), tables=None):
    size, D = block.shape
    R = size * place.seq_count // 2

    def kernel(ins, outs, scratch):
        rows = outs[0]
        (sems,) = scratch
        home = place.home
        if tables is not None:
            *ins, tables_h = ins
            bring = pltpu.make_async_copy(tables_h.at[place.core], outs[1], sems.at[1])
            bring.start()

        def put(ref, mask):
            rows[place.row(size, mask), :] = ref[:size, :]

        @pl.when(home)
        def _():
            own = pltpu.make_async_copy(ins[-1], rows.at[place.row(size)], sems.at[0])
            own.start()
            for ref, (home_mask, _) in zip(ins, [p[1] for p in pieces]):
                if home_mask is not None:
                    put(ref, home_mask)
            own.wait()

        @pl.when(jnp.logical_not(home))
        def _():
            for ref, (_, away_mask) in zip(ins, [p[1] for p in pieces]):
                put(ref, away_mask)

        if tables is not None:
            bring.wait()

    outs, far_args = [near((R, D), block.dtype)], [block]
    if tables is not None:
        outs.append(near(tables.shape[1:], tables.dtype))
        far_args.append(tables)
    return call(kernel, outs, [], [p[0] for p in pieces], far_args, deps, 0, 4, 2)


def send_blocks(place, block):
    odd = [m for m in range(1, place.seq_count) if parity_of(m)]
    even = [m for m in range(1, place.seq_count) if not parity_of(m)]
    pieces = []
    for n, mask in enumerate(odd):
        pairs = [((t, 1 - parity_of(t)), (t ^ mask, parity_of(t))) for t in range(place.seq_count)]
        home_mask = None
        if n < len(even):
            home_mask = even[n]
            pairs += [((t, parity_of(t)), (t ^ home_mask, parity_of(t))) for t in range(place.seq_count)]
        pieces.append((place.send(block, pairs), (home_mask, mask)))
    return pieces


class Chain:
    def __init__(self, place, grads, pieces, pad):
        self.place = place
        self.m = len(grads)
        self.masks = [g[2] for g in grads]
        self.zs = place.batch_count // 2
        self.pad = pad
        self.extra, self.more, self.z_pad = None, 0, 0
        parts = []
        for left, right, mask in grads:
            span = left.shape[1] // place.seq_count
            self.n = span // place.batch_count
            self.width = right.shape[1]
            for slot in (place.s, place.s ^ mask):
                cut = lax.dynamic_slice(left, (0, slot * span), (left.shape[0], span))
                parts.append(dot(cut, right, ((0,), (0,))).astype(bf16))
        self.parts = parts
        zs, n, D = self.zs, self.n, self.width
        self.per = 2 * self.m // pieces

        def give(ins, outs, scratch):
            core = place.core
            for i, ref in enumerate(ins):
                for z in range(zs):
                    outs[i // self.per][pl.ds((i % self.per) * zs * n + z * n, n), :] = ref[self.rows(z, 1 - core), :]

        *gives, _ = call(give, [near((self.per * zs * n, D), bf16)] * pieces, [], parts, name="give")
        self.got = [place.swap(give) for give in gives]

    def rows(self, z, core):
        return pl.ds(pl.multiple_of(z * 2 * self.n + core * self.n, 32), self.n)

    def core_done(self, deps=(), extra=None, extra_got=()):
        zs, n, m, D = self.zs, self.n, self.m, self.width
        place = self.place
        if extra is not None:
            self.more = 2 * extra.shape[0]
        more = self.more

        def kernel(ins, outs, scratch):
            core = place.core
            keep, *gives = outs
            if more:
                *gives, total = gives
                messages = ins[len(ins) - len(extra_got) :]
                each = more // len(messages)
                parts = jnp.concatenate([ref[ref.shape[0] - each :, :] for ref in messages], axis=0)
                total[...] = one_part(two_parts(ins[2 * m + len(self.got)][...])) + one_part(parts)
                gives[-1][pl.ds(zs * n, more), :] = two_parts(total[...])
            for i in range(2 * m):
                got = ins[2 * m + i // self.per]
                for z in range(zs):
                    cut = pl.ds(z * n, n)
                    value = ins[i][self.rows(z, core), :].astype(f32)
                    value += got[pl.ds((i % self.per) * zs * n + z * n, n), :].astype(f32)
                    if i % 2 == 0:
                        keep[i // 2, cut, :] = value
                    else:
                        gives[i // 2][cut, :] = value.astype(bf16)

        pad = max(self.pad, more)
        outs = [near((m, zs * n, D), f32)] + [near((zs * n + pad, D), bf16)] * m
        args = self.parts + self.got
        if more:
            outs.append(near(extra.shape, f32))
            args = args + [extra, *extra_got]
        self.keep, *gives, self.token = call(kernel, outs, [], args, (), deps)
        if more:
            self.extra = gives.pop()
        self.got = [xor_send(give, "seq", mask) for give, mask in zip(gives, self.masks)]
        return self.token

    def seq_done(self, deps=(), carry=None, attach=None):
        if attach is not None:
            self.extra, self.more = attach, 2 * attach.shape[0]
        self.attached = attach is not None
        def read(ins):
            keep, *got = ins
            return (lambda i, cut: keep[i, cut, :] + got[i][cut, :].astype(f32)), got[-1]

        return self.z_step(0, read, [self.keep, *self.got], deps, carry)

    def z_done(self, deps=()):
        def read(ins):
            keep, got = ins
            return (lambda i, cut: keep[i, cut, :] + got[pl.ds(i * keep.shape[1] + cut.start, cut.size), :].astype(f32)), got

        return self.z_step(self.bit + 1, read, [self.keep, self.got], deps)

    def z_step(self, bit, read, args, deps, carry=None):
        m, n, D = self.m, self.n, self.width
        place = self.place
        self.bit = bit
        left = self.zs >> bit
        rows = left // 2 * n
        zs_rows = left * n if bit == 0 else m * left * n

        def kernel(ins, outs, scratch):
            keep, give = outs[:2]
            if carry is not None:
                *ins, carry_h = ins
                bring = pltpu.make_async_copy(carry_h, outs[-1], scratch[0].at[0])
                bring.start()
            if self.more:
                *ins, extra = ins
            value, last = read(ins)
            if self.more:
                total = outs[2]
                if bit == 0 and self.attached:
                    total[...] = extra[...]
                else:
                    total[...] = one_part(two_parts(extra[...])) + one_part(last[pl.ds(zs_rows, self.more), :])
                give[pl.ds(m * rows, self.more), :] = two_parts(total[...])
            mine = (place.z >> bit) & 1
            for i in range(m):
                for z in range(left // 2):
                    cut = pl.ds(z * n, n)
                    keep[i, cut, :] = value(i, pl.ds(pl.multiple_of((2 * z + mine) * n, 32), n))
                    other = value(i, pl.ds(pl.multiple_of((2 * z + 1 - mine) * n, 32), n))
                    give[pl.ds(i * rows + z * n, n), :] = other.astype(bf16)
            if carry is not None:
                bring.wait()

        outs = [near((m, rows, D), f32), near((m * rows + max(self.more, self.z_pad if bit == 0 else 0), D), bf16)]
        if self.more:
            outs.append(near(self.extra.shape, f32))
            args = [*args, self.extra]
        far_args = []
        if carry is not None:
            outs.append(near(carry.shape, carry.dtype))
            far_args = [carry]
        self.keep, give, *rest, self.token = call(kernel, outs, [], args, far_args, deps, 0, 6, len(far_args))
        if carry is not None:
            self.carried = rest.pop()
        if self.more:
            self.extra = rest.pop()
        self.got = xor_send(give, "batch", 2 << bit)
        return self.token

    def last(self, deps=()):
        m, n, D = self.m, self.n, self.width

        def kernel(ins, outs, scratch):
            for i in range(m):
                outs[0][i] = ins[0][i] + ins[1][pl.ds(i * n, n), :].astype(f32)

        self.total, self.token = call(kernel, [near((m, n, D), f32)], [], [self.keep, self.got], (), deps)
        return self.token


def two_parts(value):
    high = value.astype(bf16)
    return jnp.concatenate([high, (value - high.astype(f32)).astype(bf16)], axis=0)


def one_part(parts):
    rows = parts.shape[0] // 2
    return parts[:rows].astype(f32) + parts[rows:].astype(f32)


def choose(place, grad_local, final_local, got, deps=()):
    def kernel(ins, outs, scratch):
        home = place.home
        outs[0][...] = jnp.where(home, ins[0][...], ins[2][...].astype(f32))
        outs[1][...] = jnp.where(home, ins[1][...], ins[3][...].astype(f32))

    return call(kernel, [result(grad_local.shape, f32)] * 2, [], [grad_local, final_local, *got], [], deps)


def last_out(chain, upper, index, deps=()):
    n, D = upper.shape[1:]

    def kernel(ins, outs, scratch):
        keep, got, upper = ins
        outs[0][0] = keep[0] + got[:n, :].astype(f32)
        outs[0][1] = upper[index]

    return call(kernel, [result((2, n, D), f32)], [], [chain.keep, chain.got, upper], (), deps)


class SmallSum:
    def __init__(self, place, values):
        self.value, self.got = values, place.swap(values)
        self.sent = False

    def step(self, deps=()):
        def small_step(ins, outs, scratch):
            outs[0][...] = ins[0][...] + ins[1][...]

        self.value, tok = call(small_step, [near(self.value.shape, f32)], [], [self.value, self.got], (), deps, name="small_step")
        if not self.sent:
            self.got = xor_send(self.value, "seq", 2)
            self.sent = True
        return tok


def small_last(chain, ff, deps=()):
    rows, D = chain.extra.shape

    def kernel(ins, outs, scratch):
        gains, biases, bins, bouts = outs
        mine, got = ins
        total = one_part(two_parts(mine[...])) + one_part(got[pl.ds(got.shape[0] - 2 * rows, 2 * rows), :])
        for layer in range(2):
            part = total[layer * SMALL_ROWS : (layer + 1) * SMALL_ROWS]
            gains[layer] = part[0:2]
            biases[layer] = part[2:4]
            bouts[layer : layer + 1, :] = part[4:5]
            for n in range(ff // D):
                bins[layer : layer + 1, n * D : (n + 1) * D] = part[5 + n : 6 + n]

    outs = [result((2, 2, D), f32), result((2, 2, D), f32), result((2, ff), f32), result((2, D), f32)]
    return call(kernel, outs, [], [chain.extra, chain.got], (), deps)


def body(tables, hid_table, inputs, norm_gain, norm_bias, w_in, b_in, w_out, b_out, cotangent):
    place = Place()
    size = inputs.shape[1]
    width = inputs.shape[2]
    length = size * place.seq_count
    scale = 1.0 / math.sqrt(length * width)
    hid = jnp.asarray(hid_table)
    tables = jnp.asarray(tables)
    span = w_in.shape[2] // (place.seq_count * place.batch_count)
    if length > 1024 or span % 32 or w_in.shape[0] != 2 or place.batch_count != 8:
        table = lax.dynamic_index_in_dim(tables, place.core, 0, keepdims=False)
        return plain_body(table, hid, inputs, norm_gain, norm_bias, w_in, b_in, w_out, b_out, cotangent)

    pieces = send_blocks(place, inputs[0])
    cot_low = cotangent[0].astype(bf16)
    cot_send = jnp.pad(cot_low, ((0, 16), (0, 0)))
    table, hid, params, win0, wout0, tok = load(place, tables, hid, (norm_gain, norm_bias, b_in, b_out), w_in, w_out)
    norm_gain = params[0]
    own, tok = gather_rows(place, inputs[0], pieces, (tok, cot_send))
    cot_pieces = send_blocks(place, cot_send)
    other = place.swap(own)
    state_a, state_b, act0, slope0, hlow0, norm00, inv00, norm01_far, inv01_far, tok = forward_first(
        own, other, table, hid, win0, wout0, params, scale, (tok,))
    others = [place.swap(half) for half in (state_a, state_b)]
    cot, table_b, tok = gather_rows(place, cot_low, cot_pieces, (tok,), tables)
    final_local, final_low, act1, hlow1, branch1, pre1, mix1, resid1, small1, tok = forward_back_last(
        place, size, 1, [state_a, state_b, *others], norm01_far, cot, table_b, hid, w_in, w_out, params, scale, (tok,))
    mix1_other = place.swap(mix1)
    grads1 = Chain(place, [(act1, branch1, 1), (pre1, hlow1, 2)], 4, 32)
    norm01, inv01, wout0, tok = load_back(0, norm01_far, inv01_far, w_out, (tok,))
    tok = grads1.core_done((tok,))
    branch0, resid0, small0, slope0, tok = back_norm(
        0, mix1, mix1_other, resid1, norm01, inv01, table, hid, norm_gain, slope0, scale, (tok,))
    out0 = Chain(place, [(act0, branch0, 1)], 2, 16)
    pre0, small0, win0, norm00, inv00, tok = back_in(0, branch0, slope0, wout0, small0, w_in, norm00, inv00, (tok,))
    tok = out0.core_done((tok,))
    mix_a, mix_b, resid0, small0, tok = back_out(0, pre0, resid0, norm00, inv00, win0, norm_gain, small0, (tok,))
    small = SmallSum(place, jnp.concatenate([small0, small1]))
    others = [place.swap(half) for half in (mix_a, mix_b)]
    tok = grads1.seq_done((tok,), hlow0)
    in0 = Chain(place, [(pre0, grads1.carried, 2)], 2, 16)
    tok = small.step((tok,))
    tok = in0.core_done((tok,))
    tok = small.step((tok,))
    grad_local, low, low_final, tok = mix_last(
        place, size, [mix_a, mix_b, *others], resid0, final_low, table, hid, scale, (tok,))
    back = [place.send_back(low), place.send_back(low_final)]
    tok = grads1.z_done((tok,))
    tok = out0.seq_done((tok,), None, small.value)
    tok = in0.seq_done((tok,))
    tok = out0.z_done((tok,))
    tok = grads1.last((tok,))
    tok = in0.z_done((tok,))
    gains, biases, bin_, bout, tok = small_last(out0, w_in.shape[2], (tok,))
    wout, tok = last_out(out0, grads1.total, 0, (tok,))
    input_grad, outputs, tok = choose(place, grad_local, final_local, back, (tok,))
    win, tok = last_out(in0, grads1.total, 1, (tok,))
    return (outputs[None], input_grad[None], gains, biases, jnp.swapaxes(win, 1, 2), bin_, wout, bout)


def solution(mesh):
    def run(inputs, norm_gain, norm_bias, w_in, b_in, w_out, b_out, cotangent):
        tables = seq_tables(inputs.shape[1], mesh.shape["seq"])
        cos_hid, sin_hid = np_tables(inputs.shape[2])
        hid_table = np.concatenate([cos_hid, -sin_hid], axis=0)

        def inner(*args):
            return body(tables, hid_table, *args)

        return jax.shard_map(
            inner,
            mesh=mesh,
            in_specs=(P("batch", "seq", None), P(), P(), P(), P(), P(), P(), P("batch", "seq", None)),
            out_specs=(
                P("batch", "seq", None),
                P("batch", "seq", None),
                P(),
                P(),
                P(None, None, ("seq", "batch")),
                P(),
                P(None, ("seq", "batch"), None),
                P(),
            ),
            check_vma=False,
        )(inputs, norm_gain, norm_bias, w_in, b_in, w_out, b_out, cotangent)

    return run
```

```python
import functools
import math

import jax
import jax.numpy as jnp
import numpy as np
from jax import lax
from jax.experimental import pallas as pl
from jax.experimental.pallas import tpu as pltpu
from jax.sharding import PartitionSpec as P

eps_norm = 1e-05
bf16 = jnp.bfloat16
f32 = jnp.float32


def parity_of(index):
    return bin(index).count("1") & 1


def np_tables(modulus):
    ids = np.arange(modulus, dtype=np.int64)
    product = (ids[:, None] * ids[None, :]) % modulus
    angles = product.astype(np.float32) * np.float32(2.0 * math.pi / modulus)
    return np.cos(angles).astype(bf16), np.sin(angles).astype(bf16)


def seq_tables(length, seq_count):
    rows = length // seq_count
    cos_t, sin_t = np_tables(length)
    ids = [
        np.concatenate([np.arange(t * rows, (t + 1) * rows) for t in range(seq_count) if parity_of(t) == c])
        for c in (0, 1)
    ]
    out = []
    for c in (0, 1):
        cols = np.concatenate([ids[c], ids[1 - c]])
        out.append(np.concatenate([t[ids[c]][:, cols] for t in (cos_t, sin_t)], axis=0))
    return np.stack(out)


class Place:
    def __init__(self):
        self.seq_count = lax.axis_size("seq")
        self.batch_count = lax.axis_size("batch")

    @property
    def s(self):
        return lax.axis_index("seq")

    @property
    def core(self):
        return lax.axis_index("batch") & 1

    @property
    def home(self):
        bits = self.s
        for shift in (4, 2, 1):
            bits = bits ^ (bits >> shift)
        return self.core == (bits & 1)

    def send(self, value, pairs):
        n = self.batch_count
        full = [
            (s0 * n + 2 * z + c0, s1 * n + 2 * z + c1)
            for (s0, c0), (s1, c1) in pairs
            for z in range(n // 2)
        ]
        return lax.ppermute(value, ("seq", "batch"), full)

    def swap(self, value):
        return xor_send(value, "batch", 1)

    @property
    def z(self):
        return lax.axis_index("batch") >> 1

    def row(self, size, mask=0):
        return pl.ds(pl.multiple_of(((self.s ^ mask) >> 1) * size, size), size)

    def send_back(self, low):
        pairs = [((t, 1 - parity_of(t)), (t ^ 1, parity_of(t))) for t in range(self.seq_count)]
        return self.send(low, pairs)

    def collect(self, block):
        odd = [m for m in range(1, self.seq_count) if parity_of(m)]
        even = [m for m in range(1, self.seq_count) if not parity_of(m)]
        size = block.shape[0]
        buffer = jnp.zeros((size * self.seq_count // 2, block.shape[1]), block.dtype)

        def put(buffer, piece, block_id):
            return lax.dynamic_update_slice(buffer, piece, ((block_id >> 1) * size, 0))

        for n, mask in enumerate(odd):
            pairs = [((t, 1 - parity_of(t)), (t ^ mask, parity_of(t))) for t in range(self.seq_count)]
            ids = self.s ^ mask
            piece = None
            if n < len(even):
                pairs += [((t, parity_of(t)), (t ^ even[n], parity_of(t))) for t in range(self.seq_count)]
                ids = jnp.where(self.home, self.s ^ even[n], ids)
                piece = self.send(block, pairs)
            else:
                ids = jnp.where(self.home, self.s, ids)
                piece = jnp.where(self.home, block, self.send(block, pairs))
            buffer = put(buffer, piece, ids)
        return buffer

    def give_back(self, rows, size):
        local = lax.dynamic_slice(rows, ((self.s >> 1) * size, 0), (size, rows.shape[1]))
        pairs = [((t, 1 - parity_of(t)), (t ^ 1, parity_of(t))) for t in range(self.seq_count)]
        got = self.send(local.astype(bf16), pairs)
        return jnp.where(self.home, local, got.astype(f32))


def xor_send(value, axis, mask):
    size = lax.axis_size(axis)
    return lax.ppermute(value, axis, [(i, i ^ mask) for i in range(size)])


def dot(a, b, dims=((1,), (0,))):
    return lax.dot_general(a, b, (dims, ((), ())), preferred_element_type=f32)


def dot_t(a, b):
    return dot(a, b, ((1,), (1,)))


def gelu_both(z):
    k = math.sqrt(2.0 / math.pi)
    z2 = z * z
    t = jnp.tanh(z * (k + (k * 0.044715) * z2))
    half = 0.5 + 0.5 * t
    act = z * half
    slope = half + act * (1.0 - half) * (2.0 * k + (6.0 * k * 0.044715) * z2)
    return act, slope


def row_loop(rows, step, fn, init=0):
    def one(i, carry):
        return fn(pl.ds(pl.multiple_of(i * step, step), step), carry)

    return lax.fori_loop(0, rows // step, one, init)


def mean_of(v):
    return jnp.mean(v, axis=-1, keepdims=True)


def norm_fwd(v):
    centered = v - mean_of(v)
    inv = lax.rsqrt(mean_of(centered * centered) + eps_norm)
    return centered * inv, inv


def norm_bwd(up, normed, inv, gain):
    scaled = up * gain
    return inv * (scaled - mean_of(scaled) - normed * mean_of(scaled * normed))


def wide(inv):
    return jnp.broadcast_to(inv, (inv.shape[0], 128))


def mix_phase(table, hid, pieces, whole, spec, rows, scale, each, wait=None):
    width = hid.shape[1]
    x, start = whole, 0
    for piece in pieces:
        count = piece.shape[0] // 128 * 128
        x[start : start + count, :] = piece[:count, :]
        start += count
    for part in range(2):
        cut = pl.ds(part * rows, rows)
        if wait is not None:
            wait(part)
        value = dot(table[cut, :], x[...])
        spec[cut, :] = (value * scale).astype(bf16)
    mixed = dot(spec[pl.ds(0, rows), :], hid[pl.ds(0, width), :])
    mixed += dot(spec[pl.ds(rows, rows), :], hid[pl.ds(width, width), :])
    each(mixed)


STEP = 256


def fwd_compute(layer, rows, scale, refs):
    r = refs
    def after_mix(mixed):
        r["hidden"][...] = mixed
    mix_phase(r["table"], r["hid"], r["pieces"], r["whole"], r["spec"], rows, scale, after_mix, r.get("wait_table"))
    gain0, bias0 = r["gain"][layer, 0:1, :], r["bias"][layer, 0:1, :]
    gain1, bias1 = r["gain"][layer, 1:2, :], r["bias"][layer, 1:2, :]

    def first(cut, carry):
        normed, inv = norm_fwd(r["state"][cut, :].astype(f32) + r["hidden"][cut, :])
        r["norm0"][cut, :] = normed
        r["inv0"][cut, :] = wide(inv)
        hidden = normed * gain0 + bias0
        r["hidden"][cut, :] = hidden
        r["hidden_low"][cut, :] = hidden.astype(bf16)
        return carry

    r["before_first"]()
    row_loop(rows, STEP, first)
    r["after_first"]()
    r["wait_in"]()
    ff = r["w_in"].shape[1]
    chunk = r["chunk"]
    r["wait_out"]()
    r["norm1"][...] = jnp.zeros_like(r["norm1"])

    def chunk_step(j, carry):
        cut = pl.ds(pl.multiple_of(j * chunk, chunk), chunk)
        z = dot(r["hidden_low"][...], r["w_in"][:, cut]) + r["b_in"][layer : layer + 1, cut]
        act, slope = gelu_both(z)
        act = act.astype(bf16)
        r["act"][:, cut] = act
        r["slope"][:, cut] = slope.astype(bf16)
        r["norm1"][...] += dot(act, r["w_out"][cut, :])
        return carry

    lax.fori_loop(0, ff // chunk, chunk_step, 0)
    r["after_ff"]()
    b_out = r["b_out"][layer : layer + 1, :]

    def second(cut, carry):
        normed, inv = norm_fwd(r["hidden"][cut, :] + (r["norm1"][cut, :] + b_out))
        r["norm1"][cut, :] = normed
        r["inv1"][cut, :] = wide(inv)
        r["put_state"](cut, normed * gain1 + bias1)
        return carry

    row_loop(rows, STEP, second)


def zero_sums(rows8):
    return tuple(jnp.zeros((8, n), f32) for n in rows8)


def fold(v):
    return jnp.sum(v.reshape(v.shape[0] // 8, 8, v.shape[1]), axis=0)


def last_norm_back(layer, rows, refs, upstream):
    r = refs
    gain1 = r["gain"][layer, 1:2, :]
    width = r["resid"].shape[1]

    def back(cut, sums):
        up, normed = upstream(cut), r["norm1"][cut, :]
        resid = norm_bwd(up, normed, r["inv1"][cut, :1], gain1)
        low = resid.astype(bf16)
        r["resid"][cut, :] = resid
        r["branch_low"][cut, :] = low
        return (sums[0] + fold(up * normed), sums[1] + fold(up), sums[2] + fold(low.astype(f32)))

    sums = row_loop(rows, STEP, back, zero_sums((width,) * 3))
    for slot, value in zip((1, 3, 4), sums):
        r["small"][slot : slot + 1, :] = jnp.sum(value, axis=0, keepdims=True)


def ff_back_in(rows, refs):
    r = refs
    ff = r["pre_low"].shape[1]
    chunk = r["chunk"]
    width = r["small"].shape[1]
    def chunk_step(j, carry):
        cut = pl.ds(pl.multiple_of(j * chunk, chunk), chunk)
        act_grad = dot_t(r["branch_low"][...], r["w_out"][cut, :])
        if "wait_slope" in r:
            r["wait_slope"](j)
        low = (act_grad * r["slope"][:, cut].astype(f32)).astype(bf16)
        r["pre_low"][:, cut] = low
        sums = jnp.sum(low.astype(f32), axis=0, keepdims=True)
        for n in range(chunk // width):
            r["small"][pl.ds(5 + j * (chunk // width) + n, 1), :] = sums[:, n * width : (n + 1) * width]
        return carry

    lax.fori_loop(0, ff // chunk, chunk_step, 0)


def ff_back_out(layer, rows, refs):
    r = refs
    width = r["resid"].shape[1]
    r["resid"][...] = r["resid_in"][...]

    def chunk_step(j, carry):
        cut = pl.ds(pl.multiple_of(j * FF_CUT, FF_CUT), FF_CUT)
        r["resid"][...] += dot_t(r["pre_low"][:, cut], r["w_in"][:, cut])
        return carry

    lax.fori_loop(0, r["pre_low"].shape[1] // FF_CUT, chunk_step, 0)
    gain0 = r["gain"][layer, 0:1, :]

    def back(cut, sums):
        up, normed = r["resid"][cut, :], r["norm0"][cut, :]
        resid = norm_bwd(up, normed, r["inv0"][cut, :1], gain0)
        r["resid"][cut, :] = resid
        r["put_mix"](cut, resid.astype(bf16))
        return (sums[0] + fold(up * normed), sums[1] + fold(up))

    sums = row_loop(rows, STEP, back, zero_sums((width,) * 2))
    for slot, value in zip((0, 2), sums):
        r["small"][slot : slot + 1, :] = jnp.sum(value, axis=0, keepdims=True)
def layer_norm(values, gain_vec, bias_vec):
    centered = values - jnp.mean(values, axis=-1, keepdims=True)
    inv_std = lax.rsqrt(jnp.mean(centered * centered, axis=-1, keepdims=True) + eps_norm)
    normed = centered * inv_std
    return (normed * gain_vec + bias_vec, normed, inv_std)


def norm_back(upstream, normed, inv_std, gain_vec):
    gain_grad = jnp.sum(upstream * normed, axis=0)
    bias_grad = jnp.sum(upstream, axis=0)
    scaled = upstream * gain_vec
    inner = (
        scaled
        - jnp.mean(scaled, axis=-1, keepdims=True)
        - normed * jnp.mean(scaled * normed, axis=-1, keepdims=True)
    )
    return (inv_std * inner, gain_grad, bias_grad)


def exchange_sum(part, axis_name, bit, dim, out_dtype):
    mine = (lax.axis_index(axis_name) >> bit) & 1
    keep = lax.dynamic_index_in_dim(part, mine, dim, keepdims=False)
    give = lax.dynamic_index_in_dim(part, 1 - mine, dim, keepdims=False)
    got = xor_send(give, axis_name, 1 << bit)
    return (keep.astype(f32) + got.astype(f32)).astype(out_dtype)


def slot_grad(place, left, right, mask):
    batch_bits = place.batch_count.bit_length() - 1
    span = left.shape[1] // place.seq_count

    def one(slot):
        cut = lax.dynamic_slice(left, (0, slot * span), (left.shape[0], span))
        return dot(cut, right, ((0,), (0,))).astype(bf16)

    part = jnp.stack([one(place.s), one(place.s ^ mask)])
    part = part.reshape((2,) + (2,) * batch_bits + (-1, right.shape[1]))
    part = exchange_sum(part, "batch", 0, batch_bits, bf16)
    part = (part[0].astype(f32) + xor_send(part[1], "seq", mask).astype(f32)).astype(bf16)
    for bit in range(1, batch_bits):
        part = exchange_sum(part, "batch", bit, batch_bits - 1 - bit, f32 if bit == batch_bits - 1 else bf16)
    return part


def all_sum(vec):
    vec = vec + xor_send(vec, "batch", 1)
    vec = vec + xor_send(vec, "seq", 1)
    for bit in range(1, lax.axis_size("batch").bit_length() - 1):
        vec = vec + xor_send(vec, "batch", 1 << bit)
    return vec


def plain_body(table, hid_table, inputs, norm_gain, norm_bias, w_in, b_in, w_out, b_out, cotangent):
    place = Place()
    size = inputs.shape[1]
    width = inputs.shape[2]
    length = size * place.seq_count
    rows = length // 2
    layers = w_in.shape[0]
    dft_scale = 1.0 / math.sqrt(length * width)

    def mix(block):
        pieces = jnp.concatenate([block, place.swap(block)], axis=0)
        spec = (dot(table, pieces) * dft_scale).astype(bf16)
        return dot(spec[:rows], hid_table[:width]) + dot(spec[rows:], hid_table[width:])

    state = place.collect(inputs[0]).astype(f32)
    stored = []
    for layer_id in range(layers):
        mixed = mix(state.astype(bf16))
        hidden, normed_mix, inv_mix = layer_norm(state + mixed, norm_gain[layer_id, 0], norm_bias[layer_id, 0])
        hidden_low = hidden.astype(bf16)
        act, slope = gelu_both(dot(hidden_low, w_in[layer_id]) + b_in[layer_id])
        act_low, slope = act.astype(bf16), slope.astype(bf16)
        branch = dot(act_low, w_out[layer_id]) + b_out[layer_id]
        state, normed_ff, inv_ff = layer_norm(hidden + branch, norm_gain[layer_id, 1], norm_bias[layer_id, 1])
        stored.append((hidden_low, slope, act_low, normed_mix, inv_mix, normed_ff, inv_ff))
    outputs = place.give_back(state, size)
    upstream = place.collect(cotangent[0].astype(bf16)).astype(f32)
    win_out, wout_out, small_out = [None] * layers, [None] * layers, [None] * layers
    for layer_id in reversed(range(layers)):
        hidden_low, slope, act_low, normed_mix, inv_mix, normed_ff, inv_ff = stored[layer_id]
        resid_ff, gain_ff, bias_ff = norm_back(upstream, normed_ff, inv_ff, norm_gain[layer_id, 1])
        branch_grad = resid_ff.astype(bf16)
        bout = jnp.sum(branch_grad.astype(f32), axis=0)
        pre_grad = (dot(branch_grad, w_out[layer_id], ((1,), (1,))) * slope.astype(f32)).astype(bf16)
        bin_ = jnp.sum(pre_grad.astype(f32), axis=0)
        hidden_grad = resid_ff + dot(pre_grad, w_in[layer_id], ((1,), (1,)))
        resid_mix, gain_mix, bias_mix = norm_back(hidden_grad, normed_mix, inv_mix, norm_gain[layer_id, 0])
        wout_out[layer_id] = slot_grad(place, act_low, branch_grad, 1)
        win_out[layer_id] = slot_grad(place, pre_grad, hidden_low, 2).T
        small_out[layer_id] = all_sum(jnp.concatenate([gain_mix, gain_ff, bias_mix, bias_ff, bout, bin_]))
        upstream = resid_mix + mix(resid_mix.astype(bf16))
    small = jnp.stack(small_out)
    gains = small[:, : 2 * width].reshape(layers, 2, width)
    biases = small[:, 2 * width : 4 * width].reshape(layers, 2, width)
    bout = small[:, 4 * width : 5 * width]
    bin_ = small[:, 5 * width :]
    input_grad = place.give_back(upstream, size)
    return (outputs[None], input_grad[None], gains, biases, jnp.stack(win_out), bin_, jnp.stack(wout_out), bout)


SMALL_ROWS = 16
CHUNK = 1536
FF_CUT = 3072


def near(shape, dtype):
    return pltpu.VMEM(shape, dtype)


def halves(refs, rows):
    half = rows // 2

    def put(cut, value):
        first = cut.start < half

        @pl.when(first)
        def _():
            refs[0][cut, :] = value

        @pl.when(jnp.logical_not(first))
        def _():
            refs[1][pl.ds(pl.multiple_of(cut.start - half, STEP), STEP), :] = value

    return put


def far(shape, dtype):
    return pltpu.HBM(shape, dtype)


def result(shape, dtype):
    return jax.ShapeDtypeStruct(shape, dtype)


def sys_name(kernel):
    return kernel.__qualname__.split(".<locals>")[0].split(".")[-1]


def call(kernel, outs, scratch, args, far_args=(), deps=(), flops=0, limit=4, sems=0, far_outs=(), name=None):
    nbytes = sum(a.size * a.dtype.itemsize for a in args)
    vmem = pl.BlockSpec(memory_space=pltpu.VMEM)
    hbm = pl.BlockSpec(memory_space=pl.ANY)
    n_in, n_dep, n_out = len(args) + len(far_args), len(deps), len(outs)

    def run(*refs):
        token = refs[n_in + n_dep + n_out]
        token[...] = jnp.zeros_like(token)
        kernel(refs[:n_in], refs[n_in + n_dep : n_in + n_dep + n_out], refs[n_in + n_dep + n_out + 1 :])

    scratch_shapes = [pltpu.VMEM(s, d) for s, d in scratch]
    if sems:
        scratch_shapes.append(pltpu.SemaphoreType.DMA((sems,)))
    return pl.pallas_call(
        run,
        name=name or sys_name(kernel),
        in_specs=[vmem] * len(args) + [hbm] * (len(far_args) + n_dep),
        out_specs=[hbm if o in far_outs else vmem for o in range(n_out + 1)],
        out_shape=list(outs) + [near((8, 128), f32)],
        scratch_shapes=scratch_shapes,
        compiler_params=pltpu.CompilerParams(vmem_limit_bytes=limit << 20),
        cost_estimate=pl.CostEstimate(flops=0, bytes_accessed=0, transcendentals=0),
    )(*[pltpu.with_memory_space_constraint(a, pltpu.VMEM) for a in args],
      *[pltpu.with_memory_space_constraint(a, pltpu.HBM) for a in far_args], *deps)


def load(place, table, hid, params, w_in, w_out):
    gain, bias, b_in, b_out = params

    def kernel(ins, outs, scratch):
        (sems,) = scratch
        table_h, hid_h, gain_h, bias_h, bin_h, bout_h, win_h, wout_h = ins
        srcs = [table_h.at[place.core], hid_h, gain_h, bias_h, bin_h, bout_h, win_h.at[0], wout_h.at[0]]
        copies = [pltpu.make_async_copy(src, dst, sems.at[n]) for n, (src, dst) in enumerate(zip(srcs, outs))]
        for copy in copies:
            copy.start()
        for copy in copies:
            copy.wait()

    args = [table, hid, gain, bias, b_in, b_out, w_in, w_out]
    outs = [near(a.shape if 0 < n < 6 else a.shape[1:], a.dtype) for n, a in enumerate(args)]
    *got, token = call(kernel, outs, [], [], args, (), 0, 4, 8)
    return got[0], got[1], tuple(got[2:6]), got[6], got[7], token


def forward_first(own, other, table, hid, w_in, w_out, params, scale, deps=()):
    R, D = own.shape
    ff = w_in.shape[1]

    def kernel(ins, outs, scratch):
        own, other, table, hid, win, wout, gain, bias, b_in, b_out = ins
        low_a, low_b, act_h, slope_h, hlow_h, norm0_h, inv0_h, norm1_h, inv1_h = outs
        whole, spec, hidden, act, slope, hlow, norm0, inv0, norm1, inv1, sems = scratch
        puts = [pltpu.make_async_copy(src, dst, sems.at[n]) for n, (src, dst) in enumerate(
            [(hlow, hlow_h), (norm0, norm0_h), (inv0, inv0_h), (act, act_h), (slope, slope_h), (norm1, norm1_h), (inv1, inv1_h)])]
        put = halves((low_a, low_b), R)

        def start(which):
            for n in which:
                puts[n].start()

        r = dict(table=table, hid=hid, pieces=[own, other], whole=whole, spec=spec, hidden=hidden, state=own, norm0=norm0, inv0=inv0,
                 hidden_low=hlow, w_in=win, w_out=wout, act=act, slope=slope, norm1=norm1, inv1=inv1, gain=gain, bias=bias,
                 b_in=b_in, b_out=b_out, chunk=CHUNK, put_state=lambda cut, value: put(cut, value.astype(bf16)),
                 wait_in=lambda: None, wait_out=lambda: None,
                 before_first=lambda: None, after_first=lambda: start((0, 1, 2)), after_ff=lambda: start((3, 4)))
        fwd_compute(0, R, scale, r)
        start((5, 6))
        for copy in puts:
            copy.wait()

    outs = [near((R // 2, D), bf16)] * 2 + [far((R, ff), bf16), far((R, ff), bf16), far((R, D), bf16),
            far((R, D), f32), far((R, 128), f32), far((R, D), f32), far((R, 128), f32)]
    scratch = [((2 * R, D), bf16), ((2 * R, D), bf16), ((R, D), f32), ((R, ff), bf16), ((R, ff), bf16), ((R, D), bf16), ((R, D), f32),
               ((R, 128), f32), ((R, D), f32), ((R, 128), f32)]
    flops = 2 * R * D * (4 * R + 2 * D + 2 * ff)
    return call(kernel, outs, scratch, [own, other, table, hid, w_in, w_out, *params], [], deps, flops, 26, 7, range(2, 9))


def forward_back_last(place, size, layer, pieces, norm_in, cot_low, cot_pieces, tables, hid, w_in, w_out, params, scale, deps=()):
    R, D = norm_in.shape
    ff = w_in.shape[2]

    def kernel(ins, outs, scratch):
        *pieces, hid, gain, bias, b_in, b_out, win_h, wout_h, norm_in_h, table_h, own_h, even_h, odd_h = ins
        local_h, final_low_h, act, hlow, branch, pre, mix, resid, small = outs
        table, cot, norm_in, final, final_low, whole, spec, norm0, inv0, norm1, inv1, win, wout, sems = scratch
        get_norm = pltpu.make_async_copy(norm_in_h, norm_in, sems.at[4])
        get_in = pltpu.make_async_copy(win_h.at[layer], win, sems.at[0])
        get_out = pltpu.make_async_copy(wout_h.at[layer], wout, sems.at[1])
        parts = [pltpu.make_async_copy(table_h.at[place.core, pl.ds(n * R, R)], table.at[pl.ds(n * R, R)], sems.at[7 + n])
                 for n in range(2)]
        for part in parts:
            part.start()
        get_norm.start()
        get_in.start()
        get_out.start()
        home = place.home
        (even_mask, odd_mask), (_, last_mask) = [p[1] for p in cot_pieces]
        at = jnp.where(home, place.s ^ even_mask, place.s ^ odd_mask) >> 1
        even = pltpu.make_async_copy(
            even_h.at[pl.ds(0, size)], cot.at[pl.ds(pl.multiple_of(at * size, size), size)], sems.at[5])
        even.start()
        at = jnp.where(home, place.s, place.s ^ last_mask) >> 1
        rest = cot.at[pl.ds(pl.multiple_of(at * size, size), size)]

        @pl.when(home)
        def _():
            pltpu.make_async_copy(own_h, rest, sems.at[6]).start()

        @pl.when(jnp.logical_not(home))
        def _():
            pltpu.make_async_copy(odd_h.at[pl.ds(0, size)], rest, sems.at[6]).start()

        gain_b, bias_b = gain[layer - 1, 1:2, :], bias[layer - 1, 1:2, :]

        class State:
            def __getitem__(self, index):
                return norm_in[index] * gain_b + bias_b

        def put_state(cut, value):
            final[cut, :] = value

        def put_mix(cut, value):
            mix[cut, :] = value

        r = dict(table=table, wait_table=lambda n: parts[n].wait(), hid=hid, pieces=pieces, whole=whole, spec=spec, hidden=resid, state=State(), norm0=norm0,
                 inv0=inv0, hidden_low=hlow, w_in=win, w_out=wout, act=act, slope=pre, norm1=norm1, inv1=inv1, gain=gain,
                 bias=bias, b_in=b_in, b_out=b_out, chunk=CHUNK, put_state=put_state, wait_in=get_in.wait,
                 wait_out=get_out.wait, resid=resid, resid_in=resid, branch_low=branch, pre_low=pre, small=small, put_mix=put_mix,
                 before_first=get_norm.wait, after_first=lambda: None, after_ff=lambda: None)
        small[...] = jnp.zeros_like(small)
        fwd_compute(layer, R, scale, r)
        block = place.row(size)
        final_low[...] = final[block, :].astype(bf16)
        puts = [pltpu.make_async_copy(final.at[block], local_h, sems.at[2]),
                pltpu.make_async_copy(final_low, final_low_h, sems.at[3])]
        for put in puts:
            put.start()
        even.wait()
        pltpu.make_async_copy(own_h, rest, sems.at[6]).wait()
        last_norm_back(layer, R, r, lambda cut: cot[cut, :].astype(f32))
        ff_back_in(R, r)
        ff_back_out(layer, R, r)
        for put in puts:
            put.wait()

    outs = [far((size, D), f32), far((size, D), bf16), near((R, ff), bf16), near((R, D), bf16), near((R, D), bf16),
            near((R, ff), bf16), near((R, D), bf16), near((R, D), f32), near((SMALL_ROWS, D), f32)]
    scratch = [((2 * R, 2 * R), bf16), ((R, D), bf16), ((R, D), f32), ((R, D), f32), ((size, D), bf16), ((2 * R, D), bf16), ((2 * R, D), bf16), ((R, D), f32), ((R, 128), f32), ((R, D), f32), ((R, 128), f32),
               ((D, ff), bf16), ((ff, D), bf16)]
    flops = 2 * R * D * (4 * R + 2 * D + 4 * ff)
    return call(kernel, outs, scratch, [*pieces, hid, *params],
                [w_in, w_out, norm_in, tables, cot_low, cot_pieces[0][0], cot_pieces[1][0]], deps, flops, 33, 9, (0, 1))


def load_back(layer, norm1, inv1, w_out, deps=()):
    def kernel(ins, outs, scratch):
        norm1_h, inv1_h, wout_h = ins
        (sems,) = scratch
        gets = [pltpu.make_async_copy(src, dst, sems.at[n]) for n, (src, dst) in enumerate(
            zip([norm1_h, inv1_h, wout_h.at[layer]], outs))]
        for get in gets:
            get.start()
        for get in gets:
            get.wait()

    outs = [near(norm1.shape, f32), near(inv1.shape, f32), near(w_out.shape[1:], bf16)]
    return call(kernel, outs, [], [], [norm1, inv1, w_out], deps, sems=3)


def back_norm(layer, own, other, resid_in, norm1, inv1, table, hid, gain, slope, scale, deps=()):
    R, D = resid_in.shape

    def kernel(ins, outs, scratch):
        own, other, resid_in, norm1, inv1, table, hid, gain, slope_h = ins
        branch, resid, small, slope = outs
        whole, spec, mixed_v, sems = scratch
        get = pltpu.make_async_copy(slope_h, slope, sems.at[0])
        get.start()
        small[...] = jnp.zeros_like(small)

        def after_mix(mixed):
            mixed_v[...] = mixed

        mix_phase(table, hid, [own, other], whole, spec, R, scale, after_mix)
        r = dict(gain=gain, resid=resid, norm1=norm1, inv1=inv1, branch_low=branch, small=small)
        last_norm_back(layer, R, r, lambda cut: resid_in[cut, :] + mixed_v[cut, :])
        get.wait()

    outs = [near((R, D), bf16), near((R, D), f32), near((SMALL_ROWS, D), f32), near(slope.shape, bf16)]
    scratch = [((2 * R, D), bf16), ((2 * R, D), bf16), ((R, D), f32)]
    flops = 2 * R * D * (4 * R + 2 * D)
    return call(kernel, outs, scratch, [own, other, resid_in, norm1, inv1, table, hid, gain], [slope], deps, flops, 8, 1)


def back_in(layer, branch, slope, w_out, small_in, w_in, norm0, inv0, deps=()):
    R, D = branch.shape
    ff = w_out.shape[0]

    def kernel(ins, outs, scratch):
        branch, slope, wout, small_in, win_h, norm0_h, inv0_h = ins
        pre, small, win, norm0, inv0 = outs
        (sems,) = scratch
        gets = [pltpu.make_async_copy(src, dst, sems.at[n]) for n, (src, dst) in enumerate(
            [(win_h.at[layer], win), (norm0_h, norm0), (inv0_h, inv0)])]
        for get in gets:
            get.start()
        small[...] = small_in[...]
        ff_back_in(R, dict(branch_low=branch, small=small, slope=slope, w_out=wout, pre_low=pre, chunk=CHUNK))
        for get in gets:
            get.wait()

    outs = [near((R, ff), bf16), near((SMALL_ROWS, D), f32), near((D, ff), bf16), near((R, D), f32), near((R, 128), f32)]
    return call(kernel, outs, [], [branch, slope, w_out, small_in], [w_in, norm0, inv0], deps, 2 * R * D * ff, 10, 3)


def back_out(layer, pre, resid_in, norm0, inv0, w_in, gain, small_in, small_upper, deps=()):
    R, D = resid_in.shape
    ff = w_in.shape[1]

    def kernel(ins, outs, scratch):
        pre, resid_in, norm0, inv0, win, gain, small_in, small_upper = ins
        mix_a, mix_b, resid, small = outs
        small[SMALL_ROWS:, :] = small_upper[...]
        small = small.at[:SMALL_ROWS]
        small[...] = small_in[...]
        ff_back_out(layer, R, dict(gain=gain, resid=resid, resid_in=resid_in, norm0=norm0, inv0=inv0, small=small, w_in=win,
                                   pre_low=pre, put_mix=halves((mix_a, mix_b), R)))

    outs = [near((R // 2, D), bf16)] * 2 + [near((R, D), f32), near((2 * SMALL_ROWS, D), f32)]
    return call(kernel, outs, [], [pre, resid_in, norm0, inv0, w_in, gain, small_in, small_upper], [], deps, 2 * R * D * ff, 6)


def mix_last(place, size, pieces, resid_in, final_low, table, hid, scale, deps=()):
    R, D = resid_in.shape

    def kernel(ins, outs, scratch):
        *pieces, resid_in, table, hid, final_low = ins
        local, low, low_final = outs
        whole, spec, grad, sems = scratch
        get = pltpu.make_async_copy(final_low, low_final, sems.at[0])
        get.start()

        def after_mix(mixed):
            grad[...] = resid_in[...] + mixed

        mix_phase(table, hid, pieces, whole, spec, R, scale, after_mix)
        cut = place.row(size)
        local[...] = grad[cut, :]
        low[...] = grad[cut, :].astype(bf16)
        get.wait()

    flops = 2 * R * D * (4 * R + 2 * D)
    return call(kernel, [near((size, D), f32)] + [near((size, D), bf16)] * 2, [((2 * R, D), bf16), ((2 * R, D), bf16), ((R, D), f32)],
                [*pieces, resid_in, table, hid], [final_low], deps, flops, 9, 1)


def gather_rows(place, block, pieces, deps=(), tables=None):
    size, D = block.shape
    R = size * place.seq_count // 2

    def kernel(ins, outs, scratch):
        rows = outs[0]
        (sems,) = scratch
        home = place.home
        if tables is not None:
            *ins, tables_h = ins
            bring = pltpu.make_async_copy(tables_h.at[place.core], outs[1], sems.at[1])
            bring.start()

        def put(ref, mask):
            rows[place.row(size, mask), :] = ref[:size, :]

        @pl.when(home)
        def _():
            own = pltpu.make_async_copy(ins[-1], rows.at[place.row(size)], sems.at[0])
            own.start()
            for ref, (home_mask, _) in zip(ins, [p[1] for p in pieces]):
                if home_mask is not None:
                    put(ref, home_mask)
            own.wait()

        @pl.when(jnp.logical_not(home))
        def _():
            for ref, (_, away_mask) in zip(ins, [p[1] for p in pieces]):
                put(ref, away_mask)

        if tables is not None:
            bring.wait()

    outs, far_args = [near((R, D), block.dtype)], [block]
    if tables is not None:
        outs.append(near(tables.shape[1:], tables.dtype))
        far_args.append(tables)
    return call(kernel, outs, [], [p[0] for p in pieces], far_args, deps, 0, 4, 2)


def send_blocks(place, block):
    odd = [m for m in range(1, place.seq_count) if parity_of(m)]
    even = [m for m in range(1, place.seq_count) if not parity_of(m)]
    pieces = []
    for n, mask in enumerate(odd):
        pairs = [((t, 1 - parity_of(t)), (t ^ mask, parity_of(t))) for t in range(place.seq_count)]
        home_mask = None
        if n < len(even):
            home_mask = even[n]
            pairs += [((t, parity_of(t)), (t ^ home_mask, parity_of(t))) for t in range(place.seq_count)]
        pieces.append((place.send(block, pairs), (home_mask, mask)))
    return pieces


class Chain:
    def __init__(self, place, grads, pieces, pad):
        self.place = place
        self.m = len(grads)
        self.masks = [g[2] for g in grads]
        self.zs = place.batch_count // 2
        self.pad = pad
        self.extra, self.more, self.z_pad = None, 0, 0
        parts = []
        for left, right, mask in grads:
            span = left.shape[1] // place.seq_count
            self.n = span // place.batch_count
            self.width = right.shape[1]
            for slot in (place.s, place.s ^ mask):
                cut = lax.dynamic_slice(left, (0, slot * span), (left.shape[0], span))
                parts.append(dot(cut, right, ((0,), (0,))).astype(bf16))
        self.parts = parts
        zs, n, D = self.zs, self.n, self.width
        self.per = 2 * self.m // pieces

        def give(ins, outs, scratch):
            core = place.core
            for i, ref in enumerate(ins):
                for z in range(zs):
                    outs[i // self.per][pl.ds((i % self.per) * zs * n + z * n, n), :] = ref[self.rows(z, 1 - core), :]

        *gives, _ = call(give, [near((self.per * zs * n, D), bf16)] * pieces, [], parts, name="give")
        self.got = [place.swap(give) for give in gives]

    def rows(self, z, core):
        return pl.ds(pl.multiple_of(z * 2 * self.n + core * self.n, 32), self.n)

    def core_done(self, deps=(), extra=None, carry=None):
        zs, n, m, D = self.zs, self.n, self.m, self.width
        place = self.place
        if extra is not None:
            self.more = extra.shape[0]
        more = self.more

        def kernel(ins, outs, scratch):
            core = place.core
            keep, *gives = outs
            if carry is not None:
                bring = pltpu.make_async_copy(ins[-1], gives.pop(), scratch[0].at[0])
                bring.start()
            if more:
                *gives, total = gives
                total[...] = ins[2 * m + len(self.got)][...]
                gives[-1][pl.ds(zs * n, more), :] = low_of(total[...])
            for i in range(2 * m):
                got = ins[2 * m + i // self.per]
                for z in range(zs):
                    cut = pl.ds(z * n, n)
                    value = ins[i][self.rows(z, core), :].astype(f32)
                    value += got[pl.ds((i % self.per) * zs * n + z * n, n), :].astype(f32)
                    if i % 2 == 0:
                        keep[i // 2, cut, :] = value
                    else:
                        gives[i // 2][cut, :] = value.astype(bf16)
            if carry is not None:
                bring.wait()

        pad = max(self.pad, more)
        outs = [near((m, zs * n, D), f32)] + [near((zs * n + pad, D), bf16)] * m
        args = self.parts + self.got
        if more:
            outs.append(near(extra.shape, f32))
            args = args + [extra]
        far_args = []
        if carry is not None:
            outs.append(near(carry.shape, carry.dtype))
            far_args = [carry]
        self.keep, *gives, self.token = call(kernel, outs, [], args, far_args, deps, 0, 4, len(far_args))
        if carry is not None:
            self.carried = gives.pop()
        if more:
            self.extra = gives.pop()
        self.got = [xor_send(give, "seq", mask) for give, mask in zip(gives, self.masks)]
        return self.token

    def seq_done(self, deps=(), carry=None):
        def read(ins):
            keep, *got = ins
            return (lambda i, cut: keep[i, cut, :] + got[i][cut, :].astype(f32)), got[-1]

        return self.z_step(0, read, [self.keep, *self.got], deps, carry)

    def z_done(self, deps=()):
        def read(ins):
            keep, got = ins
            return (lambda i, cut: keep[i, cut, :] + got[pl.ds(i * keep.shape[1] + cut.start, cut.size), :].astype(f32)), got

        return self.z_step(self.bit + 1, read, [self.keep, self.got], deps)

    def z_step(self, bit, read, args, deps, carry=None):
        m, n, D = self.m, self.n, self.width
        place = self.place
        self.bit = bit
        left = self.zs >> bit
        rows = left // 2 * n
        zs_rows = left * n if bit == 0 else m * left * n

        def kernel(ins, outs, scratch):
            keep, give = outs[:2]
            if carry is not None:
                *ins, carry_h = ins
                bring = pltpu.make_async_copy(carry_h, outs[-1], scratch[0].at[0])
                bring.start()
            if self.more:
                *ins, extra = ins
            value, last = read(ins)
            if self.more:
                total = outs[2]
                total[...] = wide_of(low_of(extra[...])) + wide_of(last[pl.ds(zs_rows, self.more), :])
                give[pl.ds(m * rows, self.more), :] = low_of(total[...])
            mine = (place.z >> bit) & 1
            for i in range(m):
                for z in range(left // 2):
                    cut = pl.ds(z * n, n)
                    keep[i, cut, :] = value(i, pl.ds(pl.multiple_of((2 * z + mine) * n, 32), n))
                    other = value(i, pl.ds(pl.multiple_of((2 * z + 1 - mine) * n, 32), n))
                    give[pl.ds(i * rows + z * n, n), :] = other.astype(bf16)
            if carry is not None:
                bring.wait()

        outs = [near((m, rows, D), f32), near((m * rows + max(self.more, self.z_pad if bit == 0 else 0), D), bf16)]
        if self.more:
            outs.append(near(self.extra.shape, f32))
            args = [*args, self.extra]
        far_args = []
        if carry is not None:
            outs.append(near(carry.shape, carry.dtype))
            far_args = [carry]
        self.keep, give, *rest, self.token = call(kernel, outs, [], args, far_args, deps, 0, 6, len(far_args))
        if carry is not None:
            self.carried = rest.pop()
        if self.more:
            self.extra = rest.pop()
        self.got = xor_send(give, "batch", 2 << bit)
        return self.token

    def last(self, deps=()):
        m, n, D = self.m, self.n, self.width

        def kernel(ins, outs, scratch):
            for i in range(m):
                outs[0][i] = ins[0][i] + ins[1][pl.ds(i * n, n), :].astype(f32)

        self.total, self.token = call(kernel, [near((m, n, D), f32)], [], [self.keep, self.got], (), deps)
        return self.token


def low_of(value):
    return value.astype(bf16)


def wide_of(parts):
    return parts.astype(f32)


def choose(place, grad_local, final_local, got, deps=()):
    def kernel(ins, outs, scratch):
        home = place.home
        outs[0][...] = jnp.where(home, ins[0][...], ins[2][...].astype(f32))
        outs[1][...] = jnp.where(home, ins[1][...], ins[3][...].astype(f32))

    return call(kernel, [result(grad_local.shape, f32)] * 2, [], [grad_local, final_local, *got], [], deps)


def last_out(chain, upper, index, deps=()):
    n, D = upper.shape[1:]

    def kernel(ins, outs, scratch):
        keep, got, upper = ins
        outs[0][0] = keep[0] + got[:n, :].astype(f32)
        outs[0][1] = upper[index]

    return call(kernel, [result((2, n, D), f32)], [], [chain.keep, chain.got, upper], (), deps)


def small_over_cores(place, values, deps=()):
    def kernel(ins, outs, scratch):
        outs[0][...] = ins[0][...] + ins[1][...]

    return call(kernel, [near(values.shape, f32)], [], [values, place.swap(values)], (), deps)


def last_out_and_small(chain, upper, index, ff, deps=()):
    n, D = upper.shape[1:]
    rows = chain.extra.shape[0]

    def kernel(ins, outs, scratch):
        keep, got, upper, mine = ins
        weight, gains, biases, bins, bouts = outs
        weight[0] = keep[0] + got[:n, :].astype(f32)
        weight[1] = upper[index]
        total = wide_of(low_of(mine[...])) + wide_of(got[pl.ds(n, rows), :])
        for layer in range(2):
            part = total[layer * SMALL_ROWS : (layer + 1) * SMALL_ROWS]
            gains[layer] = part[0:2]
            biases[layer] = part[2:4]
            bouts[layer : layer + 1, :] = part[4:5]
            for k in range(ff // D):
                bins[layer : layer + 1, k * D : (k + 1) * D] = part[5 + k : 6 + k]

    outs = [result((2, n, D), f32), result((2, 2, D), f32), result((2, 2, D), f32), result((2, ff), f32), result((2, D), f32)]
    return call(kernel, outs, [], [chain.keep, chain.got, upper, chain.extra], (), deps)


def body(tables, hid_table, inputs, norm_gain, norm_bias, w_in, b_in, w_out, b_out, cotangent):
    place = Place()
    size = inputs.shape[1]
    width = inputs.shape[2]
    length = size * place.seq_count
    scale = 1.0 / math.sqrt(length * width)
    hid = jnp.asarray(hid_table)
    tables = jnp.asarray(tables)
    span = w_in.shape[2] // (place.seq_count * place.batch_count)
    if length > 1024 or span % 32 or w_in.shape[0] != 2 or place.batch_count != 8:
        table = lax.dynamic_index_in_dim(tables, place.core, 0, keepdims=False)
        return plain_body(table, hid, inputs, norm_gain, norm_bias, w_in, b_in, w_out, b_out, cotangent)

    pieces = send_blocks(place, inputs[0])
    cot_low = cotangent[0].astype(bf16)
    cot_send = jnp.pad(cot_low, ((0, 16), (0, 0)))
    table, hid, params, win0, wout0, tok = load(place, tables, hid, (norm_gain, norm_bias, b_in, b_out), w_in, w_out)
    norm_gain = params[0]
    own, tok = gather_rows(place, inputs[0], pieces, (tok, cot_send))
    cot_pieces = send_blocks(place, cot_send)
    other = place.swap(own)
    state_a, state_b, act0, slope0, hlow0, norm00, inv00, norm01_far, inv01_far, tok = forward_first(
        own, other, table, hid, win0, wout0, params, scale, (tok,))
    others = [place.swap(half) for half in (state_a, state_b)]
    final_local, final_low, act1, hlow1, branch1, pre1, mix1, resid1, small1, tok = forward_back_last(
        place, size, 1, [state_a, state_b, *others], norm01_far, cot_low, cot_pieces, tables, hid, w_in, w_out, params, scale, (tok,))
    mix1_other = place.swap(mix1)
    grads1 = Chain(place, [(act1, branch1, 1), (pre1, hlow1, 2)], 4, 16)
    norm01, inv01, wout0, tok = load_back(0, norm01_far, inv01_far, w_out, (tok,))
    tok = grads1.core_done((tok,))
    branch0, resid0, small0, slope0, tok = back_norm(
        0, mix1, mix1_other, resid1, norm01, inv01, table, hid, norm_gain, slope0, scale, (tok,))
    out0 = Chain(place, [(act0, branch0, 1)], 2, 16)
    pre0, small0, win0, norm00, inv00, tok = back_in(0, branch0, slope0, wout0, small0, w_in, norm00, inv00, (tok,))
    mix_a, mix_b, resid0, small0, tok = back_out(0, pre0, resid0, norm00, inv00, win0, norm_gain, small0, small1, (tok,))
    others = [place.swap(half) for half in (mix_a, mix_b)]
    grads1.z_pad = 0
    tok = grads1.seq_done((tok,))
    small, tok = small_over_cores(place, small0, (tok,))
    tok = out0.core_done((tok,), small, hlow0)
    in0 = Chain(place, [(pre0, out0.carried, 2)], 2, 16)
    tok = in0.core_done((tok,))
    grad_local, low, low_final, tok = mix_last(
        place, size, [mix_a, mix_b, *others], resid0, final_low, table, hid, scale, (tok,))
    back = [place.send_back(low), place.send_back(low_final)]
    tok = grads1.z_done((tok,))
    tok = out0.seq_done((tok,))
    tok = in0.seq_done((tok,))
    tok = out0.z_done((tok,))
    tok = grads1.last((tok,))
    tok = in0.z_done((tok,))
    input_grad, outputs, tok = choose(place, grad_local, final_local, back, (tok,))
    wout, gains, biases, bin_, bout, tok = last_out_and_small(out0, grads1.total, 0, w_in.shape[2], (tok,))
    win, tok = last_out(in0, grads1.total, 1, (tok,))
    return (outputs[None], input_grad[None], gains, biases, jnp.swapaxes(win, 1, 2), bin_, wout, bout)


def solution(mesh):
    def run(inputs, norm_gain, norm_bias, w_in, b_in, w_out, b_out, cotangent):
        tables = seq_tables(inputs.shape[1], mesh.shape["seq"])
        cos_hid, sin_hid = np_tables(inputs.shape[2])
        hid_table = np.concatenate([cos_hid, -sin_hid], axis=0)

        def inner(*args):
            return body(tables, hid_table, *args)

        return jax.shard_map(
            inner,
            mesh=mesh,
            in_specs=(P("batch", "seq", None), P(), P(), P(), P(), P(), P(), P("batch", "seq", None)),
            out_specs=(
                P("batch", "seq", None),
                P("batch", "seq", None),
                P(),
                P(),
                P(None, None, ("seq", "batch")),
                P(),
                P(None, ("seq", "batch"), None),
                P(),
            ),
            check_vma=False,
        )(inputs, norm_gain, norm_bias, w_in, b_in, w_out, b_out, cotangent)

    return run
```

```python
import functools
import math

import jax
import jax.numpy as jnp
import numpy as np
from jax import lax
from jax.experimental import pallas as pl
from jax.experimental.pallas import tpu as pltpu
from jax.sharding import PartitionSpec as P

eps_norm = 1e-05
bf16 = jnp.bfloat16
f32 = jnp.float32


def parity_of(index):
    return bin(index).count("1") & 1


def np_tables(modulus):
    ids = np.arange(modulus, dtype=np.int64)
    product = (ids[:, None] * ids[None, :]) % modulus
    angles = product.astype(np.float32) * np.float32(2.0 * math.pi / modulus)
    return np.cos(angles).astype(bf16), np.sin(angles).astype(bf16)


def seq_tables(length, seq_count):
    rows = length // seq_count
    cos_t, sin_t = np_tables(length)
    ids = [
        np.concatenate([np.arange(t * rows, (t + 1) * rows) for t in range(seq_count) if parity_of(t) == c])
        for c in (0, 1)
    ]
    out = []
    for c in (0, 1):
        cols = np.concatenate([ids[c], ids[1 - c]])
        out.append(np.concatenate([t[ids[c]][:, cols] for t in (cos_t, sin_t)], axis=0))
    return np.stack(out)


class Place:
    def __init__(self):
        self.seq_count = lax.axis_size("seq")
        self.batch_count = lax.axis_size("batch")

    @property
    def s(self):
        return lax.axis_index("seq")

    @property
    def core(self):
        return lax.axis_index("batch") & 1

    @property
    def home(self):
        bits = self.s
        for shift in (4, 2, 1):
            bits = bits ^ (bits >> shift)
        return self.core == (bits & 1)

    def send(self, value, pairs):
        n = self.batch_count
        full = [
            (s0 * n + 2 * z + c0, s1 * n + 2 * z + c1)
            for (s0, c0), (s1, c1) in pairs
            for z in range(n // 2)
        ]
        return lax.ppermute(value, ("seq", "batch"), full)

    def swap(self, value):
        return xor_send(value, "batch", 1)

    @property
    def z(self):
        return lax.axis_index("batch") >> 1

    def row(self, size, mask=0):
        return pl.ds(pl.multiple_of(((self.s ^ mask) >> 1) * size, size), size)

    def send_back(self, low):
        pairs = [((t, 1 - parity_of(t)), (t ^ 1, parity_of(t))) for t in range(self.seq_count)]
        return self.send(low, pairs)

    def collect(self, block):
        odd = [m for m in range(1, self.seq_count) if parity_of(m)]
        even = [m for m in range(1, self.seq_count) if not parity_of(m)]
        size = block.shape[0]
        buffer = jnp.zeros((size * self.seq_count // 2, block.shape[1]), block.dtype)

        def put(buffer, piece, block_id):
            return lax.dynamic_update_slice(buffer, piece, ((block_id >> 1) * size, 0))

        for n, mask in enumerate(odd):
            pairs = [((t, 1 - parity_of(t)), (t ^ mask, parity_of(t))) for t in range(self.seq_count)]
            ids = self.s ^ mask
            piece = None
            if n < len(even):
                pairs += [((t, parity_of(t)), (t ^ even[n], parity_of(t))) for t in range(self.seq_count)]
                ids = jnp.where(self.home, self.s ^ even[n], ids)
                piece = self.send(block, pairs)
            else:
                ids = jnp.where(self.home, self.s, ids)
                piece = jnp.where(self.home, block, self.send(block, pairs))
            buffer = put(buffer, piece, ids)
        return buffer

    def give_back(self, rows, size):
        local = lax.dynamic_slice(rows, ((self.s >> 1) * size, 0), (size, rows.shape[1]))
        pairs = [((t, 1 - parity_of(t)), (t ^ 1, parity_of(t))) for t in range(self.seq_count)]
        got = self.send(local.astype(bf16), pairs)
        return jnp.where(self.home, local, got.astype(f32))


def xor_send(value, axis, mask):
    size = lax.axis_size(axis)
    return lax.ppermute(value, axis, [(i, i ^ mask) for i in range(size)])


def dot(a, b, dims=((1,), (0,))):
    return lax.dot_general(a, b, (dims, ((), ())), preferred_element_type=f32)


def dot_t(a, b):
    return dot(a, b, ((1,), (1,)))


def gelu_both(z):
    k = math.sqrt(2.0 / math.pi)
    z2 = z * z
    t = jnp.tanh(z * (k + (k * 0.044715) * z2))
    half = 0.5 + 0.5 * t
    act = z * half
    slope = half + act * (1.0 - half) * (2.0 * k + (6.0 * k * 0.044715) * z2)
    return act, slope


def row_loop(rows, step, fn, init=0):
    def one(i, carry):
        return fn(pl.ds(pl.multiple_of(i * step, step), step), carry)

    return lax.fori_loop(0, rows // step, one, init)


def mean_of(v):
    return jnp.mean(v, axis=-1, keepdims=True)


def norm_fwd(v):
    centered = v - mean_of(v)
    inv = lax.rsqrt(mean_of(centered * centered) + eps_norm)
    return centered * inv, inv


def norm_bwd(up, normed, inv, gain):
    scaled = up * gain
    return inv * (scaled - mean_of(scaled) - normed * mean_of(scaled * normed))


def wide(inv):
    return jnp.broadcast_to(inv, (inv.shape[0], 128))


def mix_phase(table, hid, pieces, whole, spec, rows, scale, each, wait=None):
    width = hid.shape[1]
    x, start = whole, 0
    for piece in pieces:
        count = piece.shape[0] // 128 * 128
        x[start : start + count, :] = piece[:count, :]
        start += count
    for part in range(2):
        cut = pl.ds(part * rows, rows)
        if wait is not None:
            wait(part)
        value = dot(table[cut, :], x[...])
        spec[cut, :] = (value * scale).astype(bf16)
    mixed = dot(spec[pl.ds(0, rows), :], hid[pl.ds(0, width), :])
    mixed += dot(spec[pl.ds(rows, rows), :], hid[pl.ds(width, width), :])
    each(mixed)


STEP = 512


def fwd_compute(layer, rows, scale, refs):
    r = refs
    def after_mix(mixed):
        r["hidden"][...] = mixed
    mix_phase(r["table"], r["hid"], r["pieces"], r["whole"], r["spec"], rows, scale, after_mix, r.get("wait_table"))
    gain0, bias0 = r["gain"][layer, 0:1, :], r["bias"][layer, 0:1, :]
    gain1, bias1 = r["gain"][layer, 1:2, :], r["bias"][layer, 1:2, :]

    def first(cut, carry):
        normed, inv = norm_fwd(r["state"][cut, :].astype(f32) + r["hidden"][cut, :])
        r["norm0"][cut, :] = normed
        r["inv0"][cut, :] = wide(inv)
        hidden = normed * gain0 + bias0
        r["hidden"][cut, :] = hidden
        r["hidden_low"][cut, :] = hidden.astype(bf16)
        return carry

    r["before_first"]()
    row_loop(rows, STEP, first)
    r["after_first"]()
    r["wait_in"]()
    ff = r["w_in"].shape[1]
    chunk = r["chunk"]
    r["wait_out"]()
    r["norm1"][...] = jnp.zeros_like(r["norm1"])

    def chunk_step(j, carry):
        cut = pl.ds(pl.multiple_of(j * chunk, chunk), chunk)
        z = dot(r["hidden_low"][...], r["w_in"][:, cut]) + r["b_in"][layer : layer + 1, cut]
        act, slope = gelu_both(z)
        act = act.astype(bf16)
        r["act"][:, cut] = act
        r["slope"][:, cut] = slope.astype(bf16)
        r["after_chunk"](j, cut)
        r["norm1"][...] += dot(act, r["w_out"][cut, :])
        return carry

    lax.fori_loop(0, ff // chunk, chunk_step, 0)
    r["after_ff"]()
    b_out = r["b_out"][layer : layer + 1, :]

    def second(cut, carry):
        normed, inv = norm_fwd(r["hidden"][cut, :] + (r["norm1"][cut, :] + b_out))
        r["norm1"][cut, :] = normed
        r["inv1"][cut, :] = wide(inv)
        r["put_state"](cut, normed * gain1 + bias1)
        return carry

    row_loop(rows, STEP, second)


def zero_sums(rows8):
    return tuple(jnp.zeros((8, n), f32) for n in rows8)


def fold(v):
    return jnp.sum(v.reshape(v.shape[0] // 8, 8, v.shape[1]), axis=0)


def last_norm_back(layer, rows, refs, upstream):
    r = refs
    gain1 = r["gain"][layer, 1:2, :]
    width = r["resid"].shape[1]

    def back(cut, sums):
        up, normed = upstream(cut), r["norm1"][cut, :]
        resid = norm_bwd(up, normed, r["inv1"][cut, :1], gain1)
        low = resid.astype(bf16)
        r["resid"][cut, :] = resid
        r["branch_low"][cut, :] = low
        return (sums[0] + fold(up * normed), sums[1] + fold(up), sums[2] + fold(low.astype(f32)))

    sums = row_loop(rows, STEP, back, zero_sums((width,) * 3))
    for slot, value in zip((1, 3, 4), sums):
        r["small"][slot : slot + 1, :] = jnp.sum(value, axis=0, keepdims=True)


def ff_back_in(rows, refs):
    r = refs
    ff = r["pre_low"].shape[1]
    chunk = r["chunk"]
    width = r["small"].shape[1]
    def chunk_step(j, carry):
        cut = pl.ds(pl.multiple_of(j * chunk, chunk), chunk)
        act_grad = dot_t(r["branch_low"][...], r["w_out"][cut, :])
        if "wait_slope" in r:
            r["wait_slope"](j)
        low = (act_grad * r["slope"][:, cut].astype(f32)).astype(bf16)
        r["pre_low"][:, cut] = low
        sums = jnp.sum(low.astype(f32), axis=0, keepdims=True)
        for n in range(chunk // width):
            r["small"][pl.ds(5 + j * (chunk // width) + n, 1), :] = sums[:, n * width : (n + 1) * width]
        return carry

    lax.fori_loop(0, ff // chunk, chunk_step, 0)


def ff_back_out(layer, rows, refs):
    r = refs
    width = r["resid"].shape[1]
    r["resid"][...] = r["resid_in"][...]

    def chunk_step(j, carry):
        cut = pl.ds(pl.multiple_of(j * FF_CUT, FF_CUT), FF_CUT)
        r["resid"][...] += dot_t(r["pre_low"][:, cut], r["w_in"][:, cut])
        return carry

    lax.fori_loop(0, r["pre_low"].shape[1] // FF_CUT, chunk_step, 0)
    gain0 = r["gain"][layer, 0:1, :]

    def back(cut, sums):
        up, normed = r["resid"][cut, :], r["norm0"][cut, :]
        resid = norm_bwd(up, normed, r["inv0"][cut, :1], gain0)
        r["resid"][cut, :] = resid
        r["put_mix"](cut, resid.astype(bf16))
        return (sums[0] + fold(up * normed), sums[1] + fold(up))

    sums = row_loop(rows, STEP, back, zero_sums((width,) * 2))
    for slot, value in zip((0, 2), sums):
        r["small"][slot : slot + 1, :] = jnp.sum(value, axis=0, keepdims=True)
def layer_norm(values, gain_vec, bias_vec):
    centered = values - jnp.mean(values, axis=-1, keepdims=True)
    inv_std = lax.rsqrt(jnp.mean(centered * centered, axis=-1, keepdims=True) + eps_norm)
    normed = centered * inv_std
    return (normed * gain_vec + bias_vec, normed, inv_std)


def norm_back(upstream, normed, inv_std, gain_vec):
    gain_grad = jnp.sum(upstream * normed, axis=0)
    bias_grad = jnp.sum(upstream, axis=0)
    scaled = upstream * gain_vec
    inner = (
        scaled
        - jnp.mean(scaled, axis=-1, keepdims=True)
        - normed * jnp.mean(scaled * normed, axis=-1, keepdims=True)
    )
    return (inv_std * inner, gain_grad, bias_grad)


def exchange_sum(part, axis_name, bit, dim, out_dtype):
    mine = (lax.axis_index(axis_name) >> bit) & 1
    keep = lax.dynamic_index_in_dim(part, mine, dim, keepdims=False)
    give = lax.dynamic_index_in_dim(part, 1 - mine, dim, keepdims=False)
    got = xor_send(give, axis_name, 1 << bit)
    return (keep.astype(f32) + got.astype(f32)).astype(out_dtype)


def slot_grad(place, left, right, mask):
    batch_bits = place.batch_count.bit_length() - 1
    span = left.shape[1] // place.seq_count

    def one(slot):
        cut = lax.dynamic_slice(left, (0, slot * span), (left.shape[0], span))
        return dot(cut, right, ((0,), (0,))).astype(bf16)

    part = jnp.stack([one(place.s), one(place.s ^ mask)])
    part = part.reshape((2,) + (2,) * batch_bits + (-1, right.shape[1]))
    part = exchange_sum(part, "batch", 0, batch_bits, bf16)
    part = (part[0].astype(f32) + xor_send(part[1], "seq", mask).astype(f32)).astype(bf16)
    for bit in range(1, batch_bits):
        part = exchange_sum(part, "batch", bit, batch_bits - 1 - bit, f32 if bit == batch_bits - 1 else bf16)
    return part


def all_sum(vec):
    vec = vec + xor_send(vec, "batch", 1)
    vec = vec + xor_send(vec, "seq", 1)
    for bit in range(1, lax.axis_size("batch").bit_length() - 1):
        vec = vec + xor_send(vec, "batch", 1 << bit)
    return vec


def plain_body(table, hid_table, inputs, norm_gain, norm_bias, w_in, b_in, w_out, b_out, cotangent):
    place = Place()
    size = inputs.shape[1]
    width = inputs.shape[2]
    length = size * place.seq_count
    rows = length // 2
    layers = w_in.shape[0]
    dft_scale = 1.0 / math.sqrt(length * width)

    def mix(block):
        pieces = jnp.concatenate([block, place.swap(block)], axis=0)
        spec = (dot(table, pieces) * dft_scale).astype(bf16)
        return dot(spec[:rows], hid_table[:width]) + dot(spec[rows:], hid_table[width:])

    state = place.collect(inputs[0]).astype(f32)
    stored = []
    for layer_id in range(layers):
        mixed = mix(state.astype(bf16))
        hidden, normed_mix, inv_mix = layer_norm(state + mixed, norm_gain[layer_id, 0], norm_bias[layer_id, 0])
        hidden_low = hidden.astype(bf16)
        act, slope = gelu_both(dot(hidden_low, w_in[layer_id]) + b_in[layer_id])
        act_low, slope = act.astype(bf16), slope.astype(bf16)
        branch = dot(act_low, w_out[layer_id]) + b_out[layer_id]
        state, normed_ff, inv_ff = layer_norm(hidden + branch, norm_gain[layer_id, 1], norm_bias[layer_id, 1])
        stored.append((hidden_low, slope, act_low, normed_mix, inv_mix, normed_ff, inv_ff))
    outputs = place.give_back(state, size)
    upstream = place.collect(cotangent[0].astype(bf16)).astype(f32)
    win_out, wout_out, small_out = [None] * layers, [None] * layers, [None] * layers
    for layer_id in reversed(range(layers)):
        hidden_low, slope, act_low, normed_mix, inv_mix, normed_ff, inv_ff = stored[layer_id]
        resid_ff, gain_ff, bias_ff = norm_back(upstream, normed_ff, inv_ff, norm_gain[layer_id, 1])
        branch_grad = resid_ff.astype(bf16)
        bout = jnp.sum(branch_grad.astype(f32), axis=0)
        pre_grad = (dot(branch_grad, w_out[layer_id], ((1,), (1,))) * slope.astype(f32)).astype(bf16)
        bin_ = jnp.sum(pre_grad.astype(f32), axis=0)
        hidden_grad = resid_ff + dot(pre_grad, w_in[layer_id], ((1,), (1,)))
        resid_mix, gain_mix, bias_mix = norm_back(hidden_grad, normed_mix, inv_mix, norm_gain[layer_id, 0])
        wout_out[layer_id] = slot_grad(place, act_low, branch_grad, 1)
        win_out[layer_id] = slot_grad(place, pre_grad, hidden_low, 2).T
        small_out[layer_id] = all_sum(jnp.concatenate([gain_mix, gain_ff, bias_mix, bias_ff, bout, bin_]))
        upstream = resid_mix + mix(resid_mix.astype(bf16))
    small = jnp.stack(small_out)
    gains = small[:, : 2 * width].reshape(layers, 2, width)
    biases = small[:, 2 * width : 4 * width].reshape(layers, 2, width)
    bout = small[:, 4 * width : 5 * width]
    bin_ = small[:, 5 * width :]
    input_grad = place.give_back(upstream, size)
    return (outputs[None], input_grad[None], gains, biases, jnp.stack(win_out), bin_, jnp.stack(wout_out), bout)


SMALL_ROWS = 16
CHUNK = 1536
FF_CUT = 3072


def near(shape, dtype):
    return pltpu.VMEM(shape, dtype)


def halves(refs, rows):
    half = rows // 2

    def put(cut, value):
        if value.shape[0] == rows:
            refs[0][...] = value[:half]
            refs[1][...] = value[half:]
            return
        first = cut.start < half

        @pl.when(first)
        def _():
            refs[0][cut, :] = value

        @pl.when(jnp.logical_not(first))
        def _():
            refs[1][pl.ds(pl.multiple_of(cut.start - half, STEP), STEP), :] = value

    return put


def far(shape, dtype):
    return pltpu.HBM(shape, dtype)


def result(shape, dtype):
    return jax.ShapeDtypeStruct(shape, dtype)


def sys_name(kernel):
    return kernel.__qualname__.split(".<locals>")[0].split(".")[-1]


def call(kernel, outs, scratch, args, far_args=(), deps=(), flops=0, limit=4, sems=0, far_outs=(), name=None):
    nbytes = sum(a.size * a.dtype.itemsize for a in args)
    vmem = pl.BlockSpec(memory_space=pltpu.VMEM)
    hbm = pl.BlockSpec(memory_space=pl.ANY)
    n_in, n_dep, n_out = len(args) + len(far_args), len(deps), len(outs)

    def run(*refs):
        token = refs[n_in + n_dep + n_out]
        token[...] = jnp.zeros_like(token)
        kernel(refs[:n_in], refs[n_in + n_dep : n_in + n_dep + n_out], refs[n_in + n_dep + n_out + 1 :])

    scratch_shapes = [pltpu.VMEM(s, d) for s, d in scratch]
    if sems:
        scratch_shapes.append(pltpu.SemaphoreType.DMA((sems,)))
    return pl.pallas_call(
        run,
        name=name or sys_name(kernel),
        in_specs=[vmem] * len(args) + [hbm] * (len(far_args) + n_dep),
        out_specs=[hbm if o in far_outs else vmem for o in range(n_out + 1)],
        out_shape=list(outs) + [near((8, 128), f32)],
        scratch_shapes=scratch_shapes,
        compiler_params=pltpu.CompilerParams(vmem_limit_bytes=limit << 20),
        cost_estimate=pl.CostEstimate(flops=0, bytes_accessed=0, transcendentals=0),
    )(*[pltpu.with_memory_space_constraint(a, pltpu.VMEM) for a in args],
      *[pltpu.with_memory_space_constraint(a, pltpu.HBM) for a in far_args], *deps)


def load(place, table, hid, params, w_in, w_out):
    gain, bias, b_in, b_out = params

    def kernel(ins, outs, scratch):
        (sems,) = scratch
        table_h, hid_h, gain_h, bias_h, bin_h, bout_h, win_h, wout_h = ins
        srcs = [table_h.at[place.core], hid_h, gain_h, bias_h, bin_h, bout_h, win_h.at[0], wout_h.at[0]]
        copies = [pltpu.make_async_copy(src, dst, sems.at[n]) for n, (src, dst) in enumerate(zip(srcs, outs))]
        for copy in copies:
            copy.start()
        for copy in copies:
            copy.wait()

    args = [table, hid, gain, bias, b_in, b_out, w_in, w_out]
    outs = [near(a.shape if 0 < n < 6 else a.shape[1:], a.dtype) for n, a in enumerate(args)]
    *got, token = call(kernel, outs, [], [], args, (), 0, 4, 8)
    return got[0], got[1], tuple(got[2:6]), got[6], got[7], token


def forward_first(own, other, table, hid, w_in, w_out, params, scale, deps=()):
    R, D = own.shape
    ff = w_in.shape[1]

    def kernel(ins, outs, scratch):
        own, other, table, hid, win, wout, gain, bias, b_in, b_out = ins
        low_a, low_b, act_h, slope_h, hlow_h, norm0_h, inv0_h, norm1_h, inv1_h = outs
        whole, spec, hidden, act, slope, hlow, norm0, inv0, norm1, inv1, sems = scratch
        puts = [pltpu.make_async_copy(src, dst, sems.at[n]) for n, (src, dst) in enumerate(
            [(hlow, hlow_h), (norm0, norm0_h), (inv0, inv0_h), (norm1, norm1_h), (inv1, inv1_h)])]
        chunks = ff // CHUNK

        def chunk_copies(j, cut):
            return [pltpu.make_async_copy(src.at[:, cut], dst.at[:, cut], sems.at[5 + j + chunks * n])
                    for n, (src, dst) in enumerate([(act, act_h), (slope, slope_h)])]

        def after_chunk(j, cut):
            for copy in chunk_copies(j, cut):
                copy.start()

        put = halves((low_a, low_b), R)

        def start(which):
            for n in which:
                puts[n].start()

        r = dict(table=table, hid=hid, pieces=[own, other], whole=whole, spec=spec, hidden=hidden, state=own, norm0=norm0, inv0=inv0,
                 hidden_low=hlow, w_in=win, w_out=wout, act=act, slope=slope, norm1=norm1, inv1=inv1, gain=gain, bias=bias,
                 b_in=b_in, b_out=b_out, chunk=CHUNK, put_state=lambda cut, value: put(cut, value.astype(bf16)),
                 wait_in=lambda: None, wait_out=lambda: None,
                 before_first=lambda: None, after_first=lambda: start((0, 1, 2)), after_ff=lambda: None, after_chunk=after_chunk)
        fwd_compute(0, R, scale, r)
        start((3, 4))
        for copy in puts:
            copy.wait()
        for j in range(chunks):
            for copy in chunk_copies(j, pl.ds(j * CHUNK, CHUNK)):
                copy.wait()

    outs = [near((R // 2, D), bf16)] * 2 + [far((R, ff), bf16), far((R, ff), bf16), far((R, D), bf16),
            far((R, D), f32), far((R, 128), f32), far((R, D), f32), far((R, 128), f32)]
    scratch = [((2 * R, D), bf16), ((2 * R, D), bf16), ((R, D), f32), ((R, ff), bf16), ((R, ff), bf16), ((R, D), bf16), ((R, D), f32),
               ((R, 128), f32), ((R, D), f32), ((R, 128), f32)]
    flops = 2 * R * D * (4 * R + 2 * D + 2 * ff)
    return call(kernel, outs, scratch, [own, other, table, hid, w_in, w_out, *params], [], deps, flops, 26, 5 + 2 * (ff // CHUNK), range(2, 9))


def forward_back_last(place, size, layer, pieces, norm_in, cot_low, cot_pieces, tables, hid, w_in, w_out, params, scale, deps=()):
    R, D = norm_in.shape
    ff = w_in.shape[2]

    def kernel(ins, outs, scratch):
        *pieces, hid, gain, bias, b_in, b_out, win_h, wout_h, norm_in_h, table_h, own_h, even_h, odd_h = ins
        local_h, final_low_h, act, hlow, branch, pre, mix, resid, small = outs
        table, cot, norm_in, final, final_low, whole, spec, norm0, inv0, norm1, inv1, win, wout, sems = scratch
        get_norm = pltpu.make_async_copy(norm_in_h, norm_in, sems.at[4])
        get_in = pltpu.make_async_copy(win_h.at[layer], win, sems.at[0])
        get_out = pltpu.make_async_copy(wout_h.at[layer], wout, sems.at[1])
        parts = [pltpu.make_async_copy(table_h.at[place.core, pl.ds(n * R, R)], table.at[pl.ds(n * R, R)], sems.at[7 + n])
                 for n in range(2)]
        for part in parts:
            part.start()
        get_norm.start()
        get_in.start()
        get_out.start()
        home = place.home
        (even_mask, odd_mask), (_, last_mask) = [p[1] for p in cot_pieces]
        at = jnp.where(home, place.s ^ even_mask, place.s ^ odd_mask) >> 1
        even = pltpu.make_async_copy(
            even_h.at[pl.ds(0, size)], cot.at[pl.ds(pl.multiple_of(at * size, size), size)], sems.at[5])
        even.start()
        at = jnp.where(home, place.s, place.s ^ last_mask) >> 1
        rest = cot.at[pl.ds(pl.multiple_of(at * size, size), size)]

        @pl.when(home)
        def _():
            pltpu.make_async_copy(own_h, rest, sems.at[6]).start()

        @pl.when(jnp.logical_not(home))
        def _():
            pltpu.make_async_copy(odd_h.at[pl.ds(0, size)], rest, sems.at[6]).start()

        gain_b, bias_b = gain[layer - 1, 1:2, :], bias[layer - 1, 1:2, :]

        class State:
            def __getitem__(self, index):
                return norm_in[index] * gain_b + bias_b

        def put_state(cut, value):
            final[cut, :] = value

        def put_mix(cut, value):
            mix[cut, :] = value

        r = dict(table=table, wait_table=lambda n: parts[n].wait(), hid=hid, pieces=pieces, whole=whole, spec=spec, hidden=resid, state=State(), norm0=norm0,
                 inv0=inv0, hidden_low=hlow, w_in=win, w_out=wout, act=act, slope=pre, norm1=norm1, inv1=inv1, gain=gain,
                 bias=bias, b_in=b_in, b_out=b_out, chunk=CHUNK, put_state=put_state, wait_in=get_in.wait,
                 wait_out=get_out.wait, resid=resid, resid_in=resid, branch_low=branch, pre_low=pre, small=small, put_mix=put_mix,
                 before_first=get_norm.wait, after_first=lambda: None, after_ff=lambda: None,
                 after_chunk=lambda j, cut: None)
        small[...] = jnp.zeros_like(small)
        fwd_compute(layer, R, scale, r)
        block = place.row(size)
        final_low[...] = final[block, :].astype(bf16)
        puts = [pltpu.make_async_copy(final.at[block], local_h, sems.at[2]),
                pltpu.make_async_copy(final_low, final_low_h, sems.at[3])]
        for put in puts:
            put.start()
        even.wait()
        pltpu.make_async_copy(own_h, rest, sems.at[6]).wait()
        last_norm_back(layer, R, r, lambda cut: cot[cut, :].astype(f32))
        ff_back_in(R, r)
        ff_back_out(layer, R, r)
        for put in puts:
            put.wait()

    outs = [far((size, D), f32), far((size, D), bf16), near((R, ff), bf16), near((R, D), bf16), near((R, D), bf16),
            near((R, ff), bf16), near((R, D), bf16), near((R, D), f32), near((SMALL_ROWS, D), f32)]
    scratch = [((2 * R, 2 * R), bf16), ((R, D), bf16), ((R, D), f32), ((R, D), f32), ((size, D), bf16), ((2 * R, D), bf16), ((2 * R, D), bf16), ((R, D), f32), ((R, 128), f32), ((R, D), f32), ((R, 128), f32),
               ((D, ff), bf16), ((ff, D), bf16)]
    flops = 2 * R * D * (4 * R + 2 * D + 4 * ff)
    return call(kernel, outs, scratch, [*pieces, hid, *params],
                [w_in, w_out, norm_in, tables, cot_low, cot_pieces[0][0], cot_pieces[1][0]], deps, flops, 33, 9, (0, 1))


def load_back(layer, norm1, inv1, w_out, deps=()):
    def kernel(ins, outs, scratch):
        norm1_h, inv1_h, wout_h = ins
        (sems,) = scratch
        gets = [pltpu.make_async_copy(src, dst, sems.at[n]) for n, (src, dst) in enumerate(
            zip([norm1_h, inv1_h, wout_h.at[layer]], outs))]
        for get in gets:
            get.start()
        for get in gets:
            get.wait()

    outs = [near(norm1.shape, f32), near(inv1.shape, f32), near(w_out.shape[1:], bf16)]
    return call(kernel, outs, [], [], [norm1, inv1, w_out], deps, sems=3)


def back_norm(layer, own, other, resid_in, norm1, inv1, table, hid, gain, slope, scale, deps=()):
    R, D = resid_in.shape

    def kernel(ins, outs, scratch):
        own, other, resid_in, norm1, inv1, table, hid, gain, slope_h = ins
        branch, resid, small, slope = outs
        whole, spec, mixed_v, sems = scratch
        get = pltpu.make_async_copy(slope_h, slope, sems.at[0])
        get.start()
        small[...] = jnp.zeros_like(small)

        def after_mix(mixed):
            mixed_v[...] = mixed

        mix_phase(table, hid, [own, other], whole, spec, R, scale, after_mix)
        r = dict(gain=gain, resid=resid, norm1=norm1, inv1=inv1, branch_low=branch, small=small)
        last_norm_back(layer, R, r, lambda cut: resid_in[cut, :] + mixed_v[cut, :])
        get.wait()

    outs = [near((R, D), bf16), near((R, D), f32), near((SMALL_ROWS, D), f32), near(slope.shape, bf16)]
    scratch = [((2 * R, D), bf16), ((2 * R, D), bf16), ((R, D), f32)]
    flops = 2 * R * D * (4 * R + 2 * D)
    return call(kernel, outs, scratch, [own, other, resid_in, norm1, inv1, table, hid, gain], [slope], deps, flops, 8, 1)


def back_in(layer, branch, slope, w_out, small_in, w_in, norm0, inv0, deps=()):
    R, D = branch.shape
    ff = w_out.shape[0]

    def kernel(ins, outs, scratch):
        branch, slope, wout, small_in, win_h, norm0_h, inv0_h = ins
        pre, small, win, norm0, inv0 = outs
        (sems,) = scratch
        gets = [pltpu.make_async_copy(src, dst, sems.at[n]) for n, (src, dst) in enumerate(
            [(win_h.at[layer], win), (norm0_h, norm0), (inv0_h, inv0)])]
        for get in gets:
            get.start()
        small[...] = small_in[...]
        ff_back_in(R, dict(branch_low=branch, small=small, slope=slope, w_out=wout, pre_low=pre, chunk=CHUNK))
        for get in gets:
            get.wait()

    outs = [near((R, ff), bf16), near((SMALL_ROWS, D), f32), near((D, ff), bf16), near((R, D), f32), near((R, 128), f32)]
    return call(kernel, outs, [], [branch, slope, w_out, small_in], [w_in, norm0, inv0], deps, 2 * R * D * ff, 10, 3)


def back_out(layer, pre, resid_in, norm0, inv0, w_in, gain, small_in, small_upper, deps=()):
    R, D = resid_in.shape
    ff = w_in.shape[1]

    def kernel(ins, outs, scratch):
        pre, resid_in, norm0, inv0, win, gain, small_in, small_upper = ins
        mix_a, mix_b, resid, small = outs
        small[SMALL_ROWS:, :] = small_upper[...]
        small = small.at[:SMALL_ROWS]
        small[...] = small_in[...]
        ff_back_out(layer, R, dict(gain=gain, resid=resid, resid_in=resid_in, norm0=norm0, inv0=inv0, small=small, w_in=win,
                                   pre_low=pre, put_mix=halves((mix_a, mix_b), R)))

    outs = [near((R // 2, D), bf16)] * 2 + [near((R, D), f32), near((2 * SMALL_ROWS, D), f32)]
    return call(kernel, outs, [], [pre, resid_in, norm0, inv0, w_in, gain, small_in, small_upper], [], deps, 2 * R * D * ff, 6)


def mix_last(place, size, pieces, resid_in, final_low, table, hid, scale, deps=()):
    R, D = resid_in.shape

    def kernel(ins, outs, scratch):
        *pieces, resid_in, table, hid, final_low = ins
        local, low, low_final = outs
        whole, spec, grad, sems = scratch
        get = pltpu.make_async_copy(final_low, low_final, sems.at[0])
        get.start()

        def after_mix(mixed):
            grad[...] = resid_in[...] + mixed

        mix_phase(table, hid, pieces, whole, spec, R, scale, after_mix)
        cut = place.row(size)
        local[...] = grad[cut, :]
        low[...] = grad[cut, :].astype(bf16)
        get.wait()

    flops = 2 * R * D * (4 * R + 2 * D)
    return call(kernel, [near((size, D), f32)] + [near((size, D), bf16)] * 2, [((2 * R, D), bf16), ((2 * R, D), bf16), ((R, D), f32)],
                [*pieces, resid_in, table, hid], [final_low], deps, flops, 9, 1)


def gather_rows(place, block, pieces, deps=(), tables=None):
    size, D = block.shape
    R = size * place.seq_count // 2

    def kernel(ins, outs, scratch):
        rows = outs[0]
        (sems,) = scratch
        home = place.home
        if tables is not None:
            *ins, tables_h = ins
            bring = pltpu.make_async_copy(tables_h.at[place.core], outs[1], sems.at[1])
            bring.start()

        def put(ref, mask):
            rows[place.row(size, mask), :] = ref[:size, :]

        @pl.when(home)
        def _():
            own = pltpu.make_async_copy(ins[-1], rows.at[place.row(size)], sems.at[0])
            own.start()
            for ref, (home_mask, _) in zip(ins, [p[1] for p in pieces]):
                if home_mask is not None:
                    put(ref, home_mask)
            own.wait()

        @pl.when(jnp.logical_not(home))
        def _():
            for ref, (_, away_mask) in zip(ins, [p[1] for p in pieces]):
                put(ref, away_mask)

        if tables is not None:
            bring.wait()

    outs, far_args = [near((R, D), block.dtype)], [block]
    if tables is not None:
        outs.append(near(tables.shape[1:], tables.dtype))
        far_args.append(tables)
    return call(kernel, outs, [], [p[0] for p in pieces], far_args, deps, 0, 4, 2)


def send_blocks(place, block):
    odd = [m for m in range(1, place.seq_count) if parity_of(m)]
    even = [m for m in range(1, place.seq_count) if not parity_of(m)]
    pieces = []
    for n, mask in enumerate(odd):
        pairs = [((t, 1 - parity_of(t)), (t ^ mask, parity_of(t))) for t in range(place.seq_count)]
        home_mask = None
        if n < len(even):
            home_mask = even[n]
            pairs += [((t, parity_of(t)), (t ^ home_mask, parity_of(t))) for t in range(place.seq_count)]
        pieces.append((place.send(block, pairs), (home_mask, mask)))
    return pieces


class Chain:
    def __init__(self, place, grads, pieces, pad):
        self.place = place
        self.m = len(grads)
        self.masks = [g[2] for g in grads]
        self.zs = place.batch_count // 2
        self.pad = pad
        self.extra, self.more, self.z_pad = None, 0, 0
        parts = []
        for left, right, mask in grads:
            span = left.shape[1] // place.seq_count
            self.n = span // place.batch_count
            self.width = right.shape[1]
            for slot in (place.s, place.s ^ mask):
                cut = lax.dynamic_slice(left, (0, slot * span), (left.shape[0], span))
                parts.append(dot(cut, right, ((0,), (0,))).astype(bf16))
        self.parts = parts
        zs, n, D = self.zs, self.n, self.width
        self.per = 2 * self.m // pieces

        def give(ins, outs, scratch):
            core = place.core
            for i, ref in enumerate(ins):
                for z in range(zs):
                    outs[i // self.per][pl.ds((i % self.per) * zs * n + z * n, n), :] = ref[self.rows(z, 1 - core), :]

        *gives, _ = call(give, [near((self.per * zs * n, D), bf16)] * pieces, [], parts, name="give")
        self.got = [place.swap(give) for give in gives]

    def rows(self, z, core):
        return pl.ds(pl.multiple_of(z * 2 * self.n + core * self.n, 32), self.n)

    def core_done(self, deps=(), extra=None, carry=None):
        zs, n, m, D = self.zs, self.n, self.m, self.width
        place = self.place
        if extra is not None:
            self.more = extra.shape[0]
        more = self.more

        def kernel(ins, outs, scratch):
            core = place.core
            keep, *gives = outs
            if carry is not None:
                bring = pltpu.make_async_copy(ins[-1], gives.pop(), scratch[0].at[0])
                bring.start()
            if more:
                *gives, total = gives
                total[...] = ins[2 * m + len(self.got)][...]
                gives[-1][pl.ds(zs * n, more), :] = low_of(total[...])
            for i in range(2 * m):
                got = ins[2 * m + i // self.per]
                for z in range(zs):
                    cut = pl.ds(z * n, n)
                    value = ins[i][self.rows(z, core), :].astype(f32)
                    value += got[pl.ds((i % self.per) * zs * n + z * n, n), :].astype(f32)
                    if i % 2 == 0:
                        keep[i // 2, cut, :] = value
                    else:
                        gives[i // 2][cut, :] = value.astype(bf16)
            if carry is not None:
                bring.wait()

        pad = max(self.pad, more)
        outs = [near((m, zs * n, D), f32)] + [near((zs * n + pad, D), bf16)] * m
        args = self.parts + self.got
        if more:
            outs.append(near(extra.shape, f32))
            args = args + [extra]
        far_args = []
        if carry is not None:
            outs.append(near(carry.shape, carry.dtype))
            far_args = [carry]
        self.keep, *gives, self.token = call(kernel, outs, [], args, far_args, deps, 0, 4, len(far_args))
        if carry is not None:
            self.carried = gives.pop()
        if more:
            self.extra = gives.pop()
        self.got = [xor_send(give, "seq", mask) for give, mask in zip(gives, self.masks)]
        return self.token

    def seq_done(self, deps=(), carry=None):
        def read(ins):
            keep, *got = ins
            return (lambda i, cut: keep[i, cut, :] + got[i][cut, :].astype(f32)), got[-1]

        return self.z_step(0, read, [self.keep, *self.got], deps, carry)

    def z_done(self, deps=()):
        def read(ins):
            keep, got = ins
            return (lambda i, cut: keep[i, cut, :] + got[pl.ds(i * keep.shape[1] + cut.start, cut.size), :].astype(f32)), got

        return self.z_step(self.bit + 1, read, [self.keep, self.got], deps)

    def z_step(self, bit, read, args, deps, carry=None):
        m, n, D = self.m, self.n, self.width
        place = self.place
        self.bit = bit
        left = self.zs >> bit
        rows = left // 2 * n
        zs_rows = left * n if bit == 0 else m * left * n

        def kernel(ins, outs, scratch):
            keep, give = outs[:2]
            if carry is not None:
                *ins, carry_h = ins
                bring = pltpu.make_async_copy(carry_h, outs[-1], scratch[0].at[0])
                bring.start()
            if self.more:
                *ins, extra = ins
            value, last = read(ins)
            if self.more:
                total = outs[2]
                total[...] = wide_of(low_of(extra[...])) + wide_of(last[pl.ds(zs_rows, self.more), :])
                give[pl.ds(m * rows, self.more), :] = low_of(total[...])
            mine = (place.z >> bit) & 1
            for i in range(m):
                for z in range(left // 2):
                    cut = pl.ds(z * n, n)
                    keep[i, cut, :] = value(i, pl.ds(pl.multiple_of((2 * z + mine) * n, 32), n))
                    other = value(i, pl.ds(pl.multiple_of((2 * z + 1 - mine) * n, 32), n))
                    give[pl.ds(i * rows + z * n, n), :] = other.astype(bf16)
            if carry is not None:
                bring.wait()

        outs = [near((m, rows, D), f32), near((m * rows + max(self.more, self.z_pad if bit == 0 else 0), D), bf16)]
        if self.more:
            outs.append(near(self.extra.shape, f32))
            args = [*args, self.extra]
        far_args = []
        if carry is not None:
            outs.append(near(carry.shape, carry.dtype))
            far_args = [carry]
        self.keep, give, *rest, self.token = call(kernel, outs, [], args, far_args, deps, 0, 6, len(far_args))
        if carry is not None:
            self.carried = rest.pop()
        if self.more:
            self.extra = rest.pop()
        self.got = xor_send(give, "batch", 2 << bit)
        return self.token

    def last(self, deps=()):
        m, n, D = self.m, self.n, self.width

        def kernel(ins, outs, scratch):
            for i in range(m):
                outs[0][i] = ins[0][i] + ins[1][pl.ds(i * n, n), :].astype(f32)

        self.total, self.token = call(kernel, [near((m, n, D), f32)], [], [self.keep, self.got], (), deps)
        return self.token


def low_of(value):
    return value.astype(bf16)


def wide_of(parts):
    return parts.astype(f32)


def choose(place, grad_local, final_local, got, deps=()):
    def kernel(ins, outs, scratch):
        home = place.home
        outs[0][...] = jnp.where(home, ins[0][...], ins[2][...].astype(f32))
        outs[1][...] = jnp.where(home, ins[1][...], ins[3][...].astype(f32))

    return call(kernel, [result(grad_local.shape, f32)] * 2, [], [grad_local, final_local, *got], [], deps)


def last_out(chain, upper, index, deps=()):
    n, D = upper.shape[1:]

    def kernel(ins, outs, scratch):
        keep, got, upper = ins
        outs[0][0] = keep[0] + got[:n, :].astype(f32)
        outs[0][1] = upper[index]

    return call(kernel, [result((2, n, D), f32)], [], [chain.keep, chain.got, upper], (), deps)


def small_over_cores(place, values, deps=()):
    def kernel(ins, outs, scratch):
        outs[0][...] = ins[0][...] + ins[1][...]

    return call(kernel, [near(values.shape, f32)], [], [values, place.swap(values)], (), deps)


def last_out_and_small(chain, upper, index, ff, deps=()):
    n, D = upper.shape[1:]
    rows = chain.extra.shape[0]

    def kernel(ins, outs, scratch):
        keep, got, upper, mine = ins
        weight, gains, biases, bins, bouts = outs
        weight[0] = keep[0] + got[:n, :].astype(f32)
        weight[1] = upper[index]
        total = wide_of(low_of(mine[...])) + wide_of(got[pl.ds(n, rows), :])
        for layer in range(2):
            part = total[layer * SMALL_ROWS : (layer + 1) * SMALL_ROWS]
            gains[layer] = part[0:2]
            biases[layer] = part[2:4]
            bouts[layer : layer + 1, :] = part[4:5]
            for k in range(ff // D):
                bins[layer : layer + 1, k * D : (k + 1) * D] = part[5 + k : 6 + k]

    outs = [result((2, n, D), f32), result((2, 2, D), f32), result((2, 2, D), f32), result((2, ff), f32), result((2, D), f32)]
    return call(kernel, outs, [], [chain.keep, chain.got, upper, chain.extra], (), deps)


def body(tables, hid_table, inputs, norm_gain, norm_bias, w_in, b_in, w_out, b_out, cotangent):
    place = Place()
    size = inputs.shape[1]
    width = inputs.shape[2]
    length = size * place.seq_count
    scale = 1.0 / math.sqrt(length * width)
    hid = jnp.asarray(hid_table)
    tables = jnp.asarray(tables)
    span = w_in.shape[2] // (place.seq_count * place.batch_count)
    if length != 2 * STEP or span % 32 or w_in.shape[0] != 2 or place.batch_count != 8 or w_in.shape[2] % FF_CUT:
        table = lax.dynamic_index_in_dim(tables, place.core, 0, keepdims=False)
        return plain_body(table, hid, inputs, norm_gain, norm_bias, w_in, b_in, w_out, b_out, cotangent)

    pieces = send_blocks(place, inputs[0])
    cot_low = cotangent[0].astype(bf16)
    cot_send = jnp.pad(cot_low, ((0, 16), (0, 0)))
    table, hid, params, win0, wout0, tok = load(place, tables, hid, (norm_gain, norm_bias, b_in, b_out), w_in, w_out)
    norm_gain = params[0]
    own, tok = gather_rows(place, inputs[0], pieces, (tok, cot_send))
    cot_pieces = send_blocks(place, cot_send)
    other = place.swap(own)
    state_a, state_b, act0, slope0, hlow0, norm00, inv00, norm01_far, inv01_far, tok = forward_first(
        own, other, table, hid, win0, wout0, params, scale, (tok,))
    others = [place.swap(half) for half in (state_a, state_b)]
    final_local, final_low, act1, hlow1, branch1, pre1, mix1, resid1, small1, tok = forward_back_last(
        place, size, 1, [state_a, state_b, *others], norm01_far, cot_low, cot_pieces, tables, hid, w_in, w_out, params, scale, (tok,))
    mix1_other = place.swap(mix1)
    grads1 = Chain(place, [(act1, branch1, 1), (pre1, hlow1, 2)], 4, 16)
    norm01, inv01, wout0, tok = load_back(0, norm01_far, inv01_far, w_out, (tok,))
    tok = grads1.core_done((tok,))
    branch0, resid0, small0, slope0, tok = back_norm(
        0, mix1, mix1_other, resid1, norm01, inv01, table, hid, norm_gain, slope0, scale, (tok,))
    out0 = Chain(place, [(act0, branch0, 1)], 2, 16)
    pre0, small0, win0, norm00, inv00, tok = back_in(0, branch0, slope0, wout0, small0, w_in, norm00, inv00, (tok,))
    mix_a, mix_b, resid0, small0, tok = back_out(0, pre0, resid0, norm00, inv00, win0, norm_gain, small0, small1, (tok,))
    others = [place.swap(half) for half in (mix_a, mix_b)]
    grads1.z_pad = 0
    tok = grads1.seq_done((tok,))
    small, tok = small_over_cores(place, small0, (tok,))
    tok = out0.core_done((tok,), small, hlow0)
    in0 = Chain(place, [(pre0, out0.carried, 2)], 2, 0)
    tok = in0.core_done((tok,))
    grad_local, low, low_final, tok = mix_last(
        place, size, [mix_a, mix_b, *others], resid0, final_low, table, hid, scale, (tok,))
    back = [place.send_back(low), place.send_back(low_final)]
    tok = out0.seq_done((tok,))
    tok = grads1.z_done((tok,))
    tok = in0.seq_done((tok,))
    tok = out0.z_done((tok,))
    tok = grads1.last((tok,))
    tok = in0.z_done((tok,))
    input_grad, outputs, tok = choose(place, grad_local, final_local, back, (tok,))
    wout, gains, biases, bin_, bout, tok = last_out_and_small(out0, grads1.total, 0, w_in.shape[2], (tok,))
    win, tok = last_out(in0, grads1.total, 1, (tok,))
    return (outputs[None], input_grad[None], gains, biases, jnp.swapaxes(win, 1, 2), bin_, wout, bout)


def solution(mesh):
    def run(inputs, norm_gain, norm_bias, w_in, b_in, w_out, b_out, cotangent):
        tables = seq_tables(inputs.shape[1], mesh.shape["seq"])
        cos_hid, sin_hid = np_tables(inputs.shape[2])
        hid_table = np.concatenate([cos_hid, -sin_hid], axis=0)

        def inner(*args):
            return body(tables, hid_table, *args)

        return jax.shard_map(
            inner,
            mesh=mesh,
            in_specs=(P("batch", "seq", None), P(), P(), P(), P(), P(), P(), P("batch", "seq", None)),
            out_specs=(
                P("batch", "seq", None),
                P("batch", "seq", None),
                P(),
                P(),
                P(None, None, ("seq", "batch")),
                P(),
                P(None, ("seq", "batch"), None),
                P(),
            ),
            check_vma=False,
        )(inputs, norm_gain, norm_bias, w_in, b_in, w_out, b_out, cotangent)

    return run
```

```python
import functools
import math

import jax
import jax.numpy as jnp
import numpy as np
from jax import lax
from jax.experimental import pallas as pl
from jax.experimental.pallas import tpu as pltpu
from jax.sharding import PartitionSpec as P

eps_norm = 1e-05
bf16 = jnp.bfloat16
f32 = jnp.float32


def parity_of(index):
    return bin(index).count("1") & 1


def np_tables(modulus):
    ids = np.arange(modulus, dtype=np.int64)
    product = (ids[:, None] * ids[None, :]) % modulus
    angles = product.astype(np.float32) * np.float32(2.0 * math.pi / modulus)
    return np.cos(angles).astype(bf16), np.sin(angles).astype(bf16)


def seq_tables(length, seq_count):
    rows = length // seq_count
    cos_t, sin_t = np_tables(length)
    ids = [
        np.concatenate([np.arange(t * rows, (t + 1) * rows) for t in range(seq_count) if parity_of(t) == c])
        for c in (0, 1)
    ]
    out = []
    for c in (0, 1):
        cols = np.concatenate([ids[c], ids[1 - c]])
        out.append(np.concatenate([t[ids[c]][:, cols] for t in (cos_t, sin_t)], axis=0))
    return np.stack(out)


class Place:
    def __init__(self):
        self.seq_count = lax.axis_size("seq")
        self.batch_count = lax.axis_size("batch")

    @property
    def s(self):
        return lax.axis_index("seq")

    @property
    def core(self):
        return lax.axis_index("batch") & 1

    @property
    def home(self):
        bits = self.s
        for shift in (4, 2, 1):
            bits = bits ^ (bits >> shift)
        return self.core == (bits & 1)

    def send(self, value, pairs):
        n = self.batch_count
        full = [
            (s0 * n + 2 * z + c0, s1 * n + 2 * z + c1)
            for (s0, c0), (s1, c1) in pairs
            for z in range(n // 2)
        ]
        return lax.ppermute(value, ("seq", "batch"), full)

    def swap(self, value):
        return xor_send(value, "batch", 1)

    @property
    def z(self):
        return lax.axis_index("batch") >> 1

    def row(self, size, mask=0):
        return pl.ds(pl.multiple_of(((self.s ^ mask) >> 1) * size, size), size)

    def send_back(self, low):
        pairs = [((t, 1 - parity_of(t)), (t ^ 1, parity_of(t))) for t in range(self.seq_count)]
        return self.send(low, pairs)

    def collect(self, block):
        odd = [m for m in range(1, self.seq_count) if parity_of(m)]
        even = [m for m in range(1, self.seq_count) if not parity_of(m)]
        size = block.shape[0]
        buffer = jnp.zeros((size * self.seq_count // 2, block.shape[1]), block.dtype)

        def put(buffer, piece, block_id):
            return lax.dynamic_update_slice(buffer, piece, ((block_id >> 1) * size, 0))

        for n, mask in enumerate(odd):
            pairs = [((t, 1 - parity_of(t)), (t ^ mask, parity_of(t))) for t in range(self.seq_count)]
            ids = self.s ^ mask
            piece = None
            if n < len(even):
                pairs += [((t, parity_of(t)), (t ^ even[n], parity_of(t))) for t in range(self.seq_count)]
                ids = jnp.where(self.home, self.s ^ even[n], ids)
                piece = self.send(block, pairs)
            else:
                ids = jnp.where(self.home, self.s, ids)
                piece = jnp.where(self.home, block, self.send(block, pairs))
            buffer = put(buffer, piece, ids)
        return buffer

    def give_back(self, rows, size):
        local = lax.dynamic_slice(rows, ((self.s >> 1) * size, 0), (size, rows.shape[1]))
        pairs = [((t, 1 - parity_of(t)), (t ^ 1, parity_of(t))) for t in range(self.seq_count)]
        got = self.send(local.astype(bf16), pairs)
        return jnp.where(self.home, local, got.astype(f32))


def xor_send(value, axis, mask):
    size = lax.axis_size(axis)
    return lax.ppermute(value, axis, [(i, i ^ mask) for i in range(size)])


def dot(a, b, dims=((1,), (0,))):
    return lax.dot_general(a, b, (dims, ((), ())), preferred_element_type=f32)


def dot_t(a, b):
    return dot(a, b, ((1,), (1,)))


def gelu_both(z):
    k = math.sqrt(2.0 / math.pi)
    z2 = z * z
    t = jnp.tanh(z * (k + (k * 0.044715) * z2))
    half = 0.5 + 0.5 * t
    act = z * half
    slope = half + act * (1.0 - half) * (2.0 * k + (6.0 * k * 0.044715) * z2)
    return act, slope


def row_loop(rows, step, fn, init=0):
    def one(i, carry):
        return fn(pl.ds(pl.multiple_of(i * step, step), step), carry)

    return lax.fori_loop(0, rows // step, one, init)


def mean_of(v):
    return jnp.mean(v, axis=-1, keepdims=True)


def norm_fwd(v):
    centered = v - mean_of(v)
    inv = lax.rsqrt(mean_of(centered * centered) + eps_norm)
    return centered * inv, inv


def norm_bwd(up, normed, inv, gain):
    scaled = up * gain
    return inv * (scaled - mean_of(scaled) - normed * mean_of(scaled * normed))


def wide(inv):
    return jnp.broadcast_to(inv, (inv.shape[0], 128))


def mix_phase(table, hid, pieces, whole, spec, rows, scale, each, wait=None):
    width = hid.shape[1]
    x, start = whole, 0
    for piece in pieces:
        count = piece.shape[0] // 128 * 128
        x[start : start + count, :] = piece[:count, :]
        start += count
    for part in range(2):
        cut = pl.ds(part * rows, rows)
        if wait is not None:
            wait(part)
        value = dot(table[cut, :], x[...])
        spec[cut, :] = (value * scale).astype(bf16)
    mixed = dot(spec[pl.ds(0, rows), :], hid[pl.ds(0, width), :])
    mixed += dot(spec[pl.ds(rows, rows), :], hid[pl.ds(width, width), :])
    each(mixed)


STEP = 512


def fwd_compute(layer, rows, scale, refs):
    r = refs
    def after_mix(mixed):
        r["hidden"][...] = mixed
    mix_phase(r["table"], r["hid"], r["pieces"], r["whole"], r["spec"], rows, scale, after_mix, r.get("wait_table"))
    gain0, bias0 = r["gain"][layer, 0:1, :], r["bias"][layer, 0:1, :]
    gain1, bias1 = r["gain"][layer, 1:2, :], r["bias"][layer, 1:2, :]

    def first(cut, carry):
        normed, inv = norm_fwd(r["state"][cut, :].astype(f32) + r["hidden"][cut, :])
        r["norm0"][cut, :] = normed
        r["inv0"][cut, :] = wide(inv)
        hidden = normed * gain0 + bias0
        r["hidden"][cut, :] = hidden
        r["hidden_low"][cut, :] = hidden.astype(bf16)
        return carry

    r["before_first"]()
    row_loop(rows, STEP, first)
    r["after_first"]()
    r["wait_in"]()
    ff = r["w_in"].shape[1]
    chunk = r["chunk"]
    r["wait_out"]()
    r["norm1"][...] = jnp.zeros_like(r["norm1"])

    def chunk_step(j, carry):
        cut = pl.ds(pl.multiple_of(j * chunk, chunk), chunk)
        z = dot(r["hidden_low"][...], r["w_in"][:, cut]) + r["b_in"][layer : layer + 1, cut]
        act, slope = gelu_both(z)
        act = act.astype(bf16)
        r["act"][:, cut] = act
        r["slope"][:, cut] = slope.astype(bf16)
        r["after_chunk"](j, cut)
        r["norm1"][...] += dot(act, r["w_out"][cut, :])
        return carry

    lax.fori_loop(0, ff // chunk, chunk_step, 0)
    r["after_ff"]()
    b_out = r["b_out"][layer : layer + 1, :]

    def second(cut, carry):
        normed, inv = norm_fwd(r["hidden"][cut, :] + (r["norm1"][cut, :] + b_out))
        r["norm1"][cut, :] = normed
        r["inv1"][cut, :] = wide(inv)
        r["put_state"](cut, normed * gain1 + bias1)
        return carry

    row_loop(rows, STEP, second)


def zero_sums(rows8):
    return tuple(jnp.zeros((8, n), f32) for n in rows8)


def fold(v):
    return jnp.sum(v.reshape(v.shape[0] // 8, 8, v.shape[1]), axis=0)


def last_norm_back(layer, rows, refs, upstream):
    r = refs
    gain1 = r["gain"][layer, 1:2, :]
    width = r["resid"].shape[1]

    def back(cut, sums):
        up, normed = upstream(cut), r["norm1"][cut, :]
        resid = norm_bwd(up, normed, r["inv1"][cut, :1], gain1)
        low = resid.astype(bf16)
        r["resid"][cut, :] = resid
        r["branch_low"][cut, :] = low
        return (sums[0] + fold(up * normed), sums[1] + fold(up), sums[2] + fold(low.astype(f32)))

    sums = row_loop(rows, STEP, back, zero_sums((width,) * 3))
    for slot, value in zip((1, 3, 4), sums):
        r["small"][slot : slot + 1, :] = jnp.sum(value, axis=0, keepdims=True)


def ff_back_in(rows, refs):
    r = refs
    ff = r["pre_low"].shape[1]
    chunk = r["chunk"]
    width = r["small"].shape[1]
    def chunk_step(j, carry):
        cut = pl.ds(pl.multiple_of(j * chunk, chunk), chunk)
        act_grad = dot_t(r["branch_low"][...], r["w_out"][cut, :])
        if "wait_slope" in r:
            r["wait_slope"](j)
        low = (act_grad * r["slope"][:, cut].astype(f32)).astype(bf16)
        r["pre_low"][:, cut] = low
        sums = jnp.sum(low.astype(f32), axis=0, keepdims=True)
        for n in range(chunk // width):
            r["small"][pl.ds(5 + j * (chunk // width) + n, 1), :] = sums[:, n * width : (n + 1) * width]
        return carry

    lax.fori_loop(0, ff // chunk, chunk_step, 0)


def ff_back_out(layer, rows, refs):
    r = refs
    width = r["resid"].shape[1]
    r["resid"][...] = r["resid_in"][...]

    def chunk_step(j, carry):
        cut = pl.ds(pl.multiple_of(j * FF_CUT, FF_CUT), FF_CUT)
        r["resid"][...] += dot_t(r["pre_low"][:, cut], r["w_in"][:, cut])
        return carry

    lax.fori_loop(0, r["pre_low"].shape[1] // FF_CUT, chunk_step, 0)
    gain0 = r["gain"][layer, 0:1, :]

    def back(cut, sums):
        up, normed = r["resid"][cut, :], r["norm0"][cut, :]
        resid = norm_bwd(up, normed, r["inv0"][cut, :1], gain0)
        r["resid"][cut, :] = resid
        r["put_mix"](cut, resid.astype(bf16))
        return (sums[0] + fold(up * normed), sums[1] + fold(up))

    sums = row_loop(rows, STEP, back, zero_sums((width,) * 2))
    for slot, value in zip((0, 2), sums):
        r["small"][slot : slot + 1, :] = jnp.sum(value, axis=0, keepdims=True)
def layer_norm(values, gain_vec, bias_vec):
    centered = values - jnp.mean(values, axis=-1, keepdims=True)
    inv_std = lax.rsqrt(jnp.mean(centered * centered, axis=-1, keepdims=True) + eps_norm)
    normed = centered * inv_std
    return (normed * gain_vec + bias_vec, normed, inv_std)


def norm_back(upstream, normed, inv_std, gain_vec):
    gain_grad = jnp.sum(upstream * normed, axis=0)
    bias_grad = jnp.sum(upstream, axis=0)
    scaled = upstream * gain_vec
    inner = (
        scaled
        - jnp.mean(scaled, axis=-1, keepdims=True)
        - normed * jnp.mean(scaled * normed, axis=-1, keepdims=True)
    )
    return (inv_std * inner, gain_grad, bias_grad)


def exchange_sum(part, axis_name, bit, dim, out_dtype):
    mine = (lax.axis_index(axis_name) >> bit) & 1
    keep = lax.dynamic_index_in_dim(part, mine, dim, keepdims=False)
    give = lax.dynamic_index_in_dim(part, 1 - mine, dim, keepdims=False)
    got = xor_send(give, axis_name, 1 << bit)
    return (keep.astype(f32) + got.astype(f32)).astype(out_dtype)


def slot_grad(place, left, right, mask):
    batch_bits = place.batch_count.bit_length() - 1
    span = left.shape[1] // place.seq_count

    def one(slot):
        cut = lax.dynamic_slice(left, (0, slot * span), (left.shape[0], span))
        return dot(cut, right, ((0,), (0,))).astype(bf16)

    part = jnp.stack([one(place.s), one(place.s ^ mask)])
    part = part.reshape((2,) + (2,) * batch_bits + (-1, right.shape[1]))
    part = exchange_sum(part, "batch", 0, batch_bits, bf16)
    part = (part[0].astype(f32) + xor_send(part[1], "seq", mask).astype(f32)).astype(bf16)
    for bit in range(1, batch_bits):
        part = exchange_sum(part, "batch", bit, batch_bits - 1 - bit, f32 if bit == batch_bits - 1 else bf16)
    return part


def all_sum(vec):
    vec = vec + xor_send(vec, "batch", 1)
    vec = vec + xor_send(vec, "seq", 1)
    for bit in range(1, lax.axis_size("batch").bit_length() - 1):
        vec = vec + xor_send(vec, "batch", 1 << bit)
    return vec


def plain_body(table, hid_table, inputs, norm_gain, norm_bias, w_in, b_in, w_out, b_out, cotangent):
    place = Place()
    size = inputs.shape[1]
    width = inputs.shape[2]
    length = size * place.seq_count
    rows = length // 2
    layers = w_in.shape[0]
    dft_scale = 1.0 / math.sqrt(length * width)

    def mix(block):
        pieces = jnp.concatenate([block, place.swap(block)], axis=0)
        spec = (dot(table, pieces) * dft_scale).astype(bf16)
        return dot(spec[:rows], hid_table[:width]) + dot(spec[rows:], hid_table[width:])

    state = place.collect(inputs[0]).astype(f32)
    stored = []
    for layer_id in range(layers):
        mixed = mix(state.astype(bf16))
        hidden, normed_mix, inv_mix = layer_norm(state + mixed, norm_gain[layer_id, 0], norm_bias[layer_id, 0])
        hidden_low = hidden.astype(bf16)
        act, slope = gelu_both(dot(hidden_low, w_in[layer_id]) + b_in[layer_id])
        act_low, slope = act.astype(bf16), slope.astype(bf16)
        branch = dot(act_low, w_out[layer_id]) + b_out[layer_id]
        state, normed_ff, inv_ff = layer_norm(hidden + branch, norm_gain[layer_id, 1], norm_bias[layer_id, 1])
        stored.append((hidden_low, slope, act_low, normed_mix, inv_mix, normed_ff, inv_ff))
    outputs = place.give_back(state, size)
    upstream = place.collect(cotangent[0].astype(bf16)).astype(f32)
    win_out, wout_out, small_out = [None] * layers, [None] * layers, [None] * layers
    for layer_id in reversed(range(layers)):
        hidden_low, slope, act_low, normed_mix, inv_mix, normed_ff, inv_ff = stored[layer_id]
        resid_ff, gain_ff, bias_ff = norm_back(upstream, normed_ff, inv_ff, norm_gain[layer_id, 1])
        branch_grad = resid_ff.astype(bf16)
        bout = jnp.sum(branch_grad.astype(f32), axis=0)
        pre_grad = (dot(branch_grad, w_out[layer_id], ((1,), (1,))) * slope.astype(f32)).astype(bf16)
        bin_ = jnp.sum(pre_grad.astype(f32), axis=0)
        hidden_grad = resid_ff + dot(pre_grad, w_in[layer_id], ((1,), (1,)))
        resid_mix, gain_mix, bias_mix = norm_back(hidden_grad, normed_mix, inv_mix, norm_gain[layer_id, 0])
        wout_out[layer_id] = slot_grad(place, act_low, branch_grad, 1)
        win_out[layer_id] = slot_grad(place, pre_grad, hidden_low, 2).T
        small_out[layer_id] = all_sum(jnp.concatenate([gain_mix, gain_ff, bias_mix, bias_ff, bout, bin_]))
        upstream = resid_mix + mix(resid_mix.astype(bf16))
    small = jnp.stack(small_out)
    gains = small[:, : 2 * width].reshape(layers, 2, width)
    biases = small[:, 2 * width : 4 * width].reshape(layers, 2, width)
    bout = small[:, 4 * width : 5 * width]
    bin_ = small[:, 5 * width :]
    input_grad = place.give_back(upstream, size)
    return (outputs[None], input_grad[None], gains, biases, jnp.stack(win_out), bin_, jnp.stack(wout_out), bout)


SMALL_ROWS = 16
CHUNK = 1536
FF_CUT = 3072


def near(shape, dtype):
    return pltpu.VMEM(shape, dtype)


def halves(refs, rows):
    half = rows // 2

    def put(cut, value):
        if value.shape[0] == rows:
            refs[0][...] = value[:half]
            refs[1][...] = value[half:]
            return
        first = cut.start < half

        @pl.when(first)
        def _():
            refs[0][cut, :] = value

        @pl.when(jnp.logical_not(first))
        def _():
            refs[1][pl.ds(pl.multiple_of(cut.start - half, STEP), STEP), :] = value

    return put


def far(shape, dtype):
    return pltpu.HBM(shape, dtype)


def result(shape, dtype):
    return jax.ShapeDtypeStruct(shape, dtype)


def sys_name(kernel):
    return kernel.__qualname__.split(".<locals>")[0].split(".")[-1]


def call(kernel, outs, scratch, args, far_args=(), deps=(), flops=0, limit=4, sems=0, far_outs=(), name=None):
    nbytes = sum(a.size * a.dtype.itemsize for a in args)
    vmem = pl.BlockSpec(memory_space=pltpu.VMEM)
    hbm = pl.BlockSpec(memory_space=pl.ANY)
    n_in, n_dep, n_out = len(args) + len(far_args), len(deps), len(outs)

    def run(*refs):
        token = refs[n_in + n_dep + n_out]
        token[...] = jnp.zeros_like(token)
        kernel(refs[:n_in], refs[n_in + n_dep : n_in + n_dep + n_out], refs[n_in + n_dep + n_out + 1 :])

    scratch_shapes = [pltpu.VMEM(s, d) for s, d in scratch]
    if sems:
        scratch_shapes.append(pltpu.SemaphoreType.DMA((sems,)))
    return pl.pallas_call(
        run,
        name=name or sys_name(kernel),
        in_specs=[vmem] * len(args) + [hbm] * (len(far_args) + n_dep),
        out_specs=[hbm if o in far_outs else vmem for o in range(n_out + 1)],
        out_shape=list(outs) + [near((8, 128), f32)],
        scratch_shapes=scratch_shapes,
        compiler_params=pltpu.CompilerParams(vmem_limit_bytes=limit << 20),
        cost_estimate=pl.CostEstimate(flops=0, bytes_accessed=0, transcendentals=0),
    )(*[pltpu.with_memory_space_constraint(a, pltpu.VMEM) for a in args],
      *[pltpu.with_memory_space_constraint(a, pltpu.HBM) for a in far_args], *deps)


def load(place, table, hid, params, w_in, w_out):
    gain, bias, b_in, b_out = params

    def kernel(ins, outs, scratch):
        (sems,) = scratch
        table_h, hid_h, gain_h, bias_h, bin_h, bout_h, win_h, wout_h = ins
        srcs = [table_h.at[place.core], hid_h, gain_h, bias_h, bin_h, bout_h, win_h.at[0], wout_h.at[0]]
        copies = [pltpu.make_async_copy(src, dst, sems.at[n]) for n, (src, dst) in enumerate(zip(srcs, outs))]
        for copy in copies:
            copy.start()
        for copy in copies:
            copy.wait()

    args = [table, hid, gain, bias, b_in, b_out, w_in, w_out]
    outs = [near(a.shape if 0 < n < 6 else a.shape[1:], a.dtype) for n, a in enumerate(args)]
    *got, token = call(kernel, outs, [], [], args, (), 0, 4, 8)
    return got[0], got[1], tuple(got[2:6]), got[6], got[7], token


def forward_first(own, other, table, hid, w_in, w_out, params, scale, deps=()):
    R, D = own.shape
    ff = w_in.shape[1]

    def kernel(ins, outs, scratch):
        own, other, table, hid, win, wout, gain, bias, b_in, b_out = ins
        low_a, low_b, act_h, slope_h, hlow_h, norm0_h, inv0_h, norm1_h, inv1_h = outs
        whole, spec, hidden, act, slope, hlow, norm0, inv0, norm1, inv1, sems = scratch
        puts = [pltpu.make_async_copy(src, dst, sems.at[n]) for n, (src, dst) in enumerate(
            [(hlow, hlow_h), (norm0, norm0_h), (inv0, inv0_h), (norm1, norm1_h), (inv1, inv1_h)])]
        chunks = ff // CHUNK

        def chunk_copies(j, cut):
            return [pltpu.make_async_copy(src.at[:, cut], dst.at[:, cut], sems.at[5 + j + chunks * n])
                    for n, (src, dst) in enumerate([(act, act_h), (slope, slope_h)])]

        def after_chunk(j, cut):
            for copy in chunk_copies(j, cut):
                copy.start()

        put = halves((low_a, low_b), R)

        def start(which):
            for n in which:
                puts[n].start()

        r = dict(table=table, hid=hid, pieces=[own, other], whole=whole, spec=spec, hidden=hidden, state=own, norm0=norm0, inv0=inv0,
                 hidden_low=hlow, w_in=win, w_out=wout, act=act, slope=slope, norm1=norm1, inv1=inv1, gain=gain, bias=bias,
                 b_in=b_in, b_out=b_out, chunk=CHUNK, put_state=lambda cut, value: put(cut, value.astype(bf16)),
                 wait_in=lambda: None, wait_out=lambda: None,
                 before_first=lambda: None, after_first=lambda: start((0, 1, 2)), after_ff=lambda: None, after_chunk=after_chunk)
        fwd_compute(0, R, scale, r)
        start((3, 4))
        for copy in puts:
            copy.wait()
        for j in range(chunks):
            for copy in chunk_copies(j, pl.ds(j * CHUNK, CHUNK)):
                copy.wait()

    outs = [near((R // 2, D), bf16)] * 2 + [far((R, ff), bf16), far((R, ff), bf16), far((R, D), bf16),
            far((R, D), f32), far((R, 128), f32), far((R, D), f32), far((R, 128), f32)]
    scratch = [((2 * R, D), bf16), ((2 * R, D), bf16), ((R, D), f32), ((R, ff), bf16), ((R, ff), bf16), ((R, D), bf16), ((R, D), f32),
               ((R, 128), f32), ((R, D), f32), ((R, 128), f32)]
    flops = 2 * R * D * (4 * R + 2 * D + 2 * ff)
    return call(kernel, outs, scratch, [own, other, table, hid, w_in, w_out, *params], [], deps, flops, 26, 5 + 2 * (ff // CHUNK), range(2, 9))


def forward_back_last(place, size, layer, pieces, norm_in, cot_low, cot_pieces, tables, hid, w_in, w_out, params, scale, deps=()):
    R, D = norm_in.shape
    ff = w_in.shape[2]

    def kernel(ins, outs, scratch):
        *pieces, hid, gain, bias, b_in, b_out, win_h, wout_h, norm_in_h, table_h, own_h, even_h, odd_h = ins
        local_h, final_low_h, act, hlow, branch, pre, mix, resid, small = outs
        table, cot, norm_in, final, final_low, whole, spec, norm0, inv0, norm1, inv1, win, wout, sems = scratch
        get_norm = pltpu.make_async_copy(norm_in_h, norm_in, sems.at[4])
        get_in = pltpu.make_async_copy(win_h.at[layer], win, sems.at[0])
        get_out = pltpu.make_async_copy(wout_h.at[layer], wout, sems.at[1])
        parts = [pltpu.make_async_copy(table_h.at[place.core, pl.ds(n * R, R)], table.at[pl.ds(n * R, R)], sems.at[7 + n])
                 for n in range(2)]
        for part in parts:
            part.start()
        get_norm.start()
        get_in.start()
        get_out.start()
        home = place.home
        (even_mask, odd_mask), (_, last_mask) = [p[1] for p in cot_pieces]
        at = jnp.where(home, place.s ^ even_mask, place.s ^ odd_mask) >> 1
        even = pltpu.make_async_copy(
            even_h.at[pl.ds(0, size)], cot.at[pl.ds(pl.multiple_of(at * size, size), size)], sems.at[5])
        even.start()
        at = jnp.where(home, place.s, place.s ^ last_mask) >> 1
        rest = cot.at[pl.ds(pl.multiple_of(at * size, size), size)]

        @pl.when(home)
        def _():
            pltpu.make_async_copy(own_h, rest, sems.at[6]).start()

        @pl.when(jnp.logical_not(home))
        def _():
            pltpu.make_async_copy(odd_h.at[pl.ds(0, size)], rest, sems.at[6]).start()

        gain_b, bias_b = gain[layer - 1, 1:2, :], bias[layer - 1, 1:2, :]

        class State:
            def __getitem__(self, index):
                return norm_in[index] * gain_b + bias_b

        def put_state(cut, value):
            final[cut, :] = value

        def put_mix(cut, value):
            mix[cut, :] = value

        r = dict(table=table, wait_table=lambda n: parts[n].wait(), hid=hid, pieces=pieces, whole=whole, spec=spec, hidden=resid, state=State(), norm0=norm0,
                 inv0=inv0, hidden_low=hlow, w_in=win, w_out=wout, act=act, slope=pre, norm1=norm1, inv1=inv1, gain=gain,
                 bias=bias, b_in=b_in, b_out=b_out, chunk=CHUNK, put_state=put_state, wait_in=get_in.wait,
                 wait_out=get_out.wait, resid=resid, resid_in=resid, branch_low=branch, pre_low=pre, small=small, put_mix=put_mix,
                 before_first=get_norm.wait, after_first=lambda: None, after_ff=lambda: None,
                 after_chunk=lambda j, cut: None)
        small[...] = jnp.zeros_like(small)
        fwd_compute(layer, R, scale, r)
        block = place.row(size)
        final_low[...] = final[block, :].astype(bf16)
        puts = [pltpu.make_async_copy(final.at[block], local_h, sems.at[2]),
                pltpu.make_async_copy(final_low, final_low_h, sems.at[3])]
        for put in puts:
            put.start()
        even.wait()
        pltpu.make_async_copy(own_h, rest, sems.at[6]).wait()
        last_norm_back(layer, R, r, lambda cut: cot[cut, :].astype(f32))
        ff_back_in(R, r)
        ff_back_out(layer, R, r)
        for put in puts:
            put.wait()

    outs = [far((size, D), f32), far((size, D), bf16), near((R, ff), bf16), near((R, D), bf16), near((R, D), bf16),
            near((R, ff), bf16), near((R, D), bf16), near((R, D), f32), near((SMALL_ROWS, D), f32)]
    scratch = [((2 * R, 2 * R), bf16), ((R, D), bf16), ((R, D), f32), ((R, D), f32), ((size, D), bf16), ((2 * R, D), bf16), ((2 * R, D), bf16), ((R, D), f32), ((R, 128), f32), ((R, D), f32), ((R, 128), f32),
               ((D, ff), bf16), ((ff, D), bf16)]
    flops = 2 * R * D * (4 * R + 2 * D + 4 * ff)
    return call(kernel, outs, scratch, [*pieces, hid, *params],
                [w_in, w_out, norm_in, tables, cot_low, cot_pieces[0][0], cot_pieces[1][0]], deps, flops, 33, 9, (0, 1))


def load_back(layer, norm1, inv1, w_out, deps=()):
    def kernel(ins, outs, scratch):
        norm1_h, inv1_h, wout_h = ins
        (sems,) = scratch
        gets = [pltpu.make_async_copy(src, dst, sems.at[n]) for n, (src, dst) in enumerate(
            zip([norm1_h, inv1_h, wout_h.at[layer]], outs))]
        for get in gets:
            get.start()
        for get in gets:
            get.wait()

    outs = [near(norm1.shape, f32), near(inv1.shape, f32), near(w_out.shape[1:], bf16)]
    return call(kernel, outs, [], [], [norm1, inv1, w_out], deps, sems=3)


def back_norm(layer, own, other, resid_in, norm1, inv1, table, hid, gain, slope, scale, deps=()):
    R, D = resid_in.shape

    def kernel(ins, outs, scratch):
        own, other, resid_in, norm1, inv1, table, hid, gain, slope_h = ins
        branch, resid, small, slope = outs
        whole, spec, mixed_v, sems = scratch
        get = pltpu.make_async_copy(slope_h, slope, sems.at[0])
        get.start()
        small[...] = jnp.zeros_like(small)

        def after_mix(mixed):
            mixed_v[...] = mixed

        mix_phase(table, hid, [own, other], whole, spec, R, scale, after_mix)
        r = dict(gain=gain, resid=resid, norm1=norm1, inv1=inv1, branch_low=branch, small=small)
        last_norm_back(layer, R, r, lambda cut: resid_in[cut, :] + mixed_v[cut, :])
        get.wait()

    outs = [near((R, D), bf16), near((R, D), f32), near((SMALL_ROWS, D), f32), near(slope.shape, bf16)]
    scratch = [((2 * R, D), bf16), ((2 * R, D), bf16), ((R, D), f32)]
    flops = 2 * R * D * (4 * R + 2 * D)
    return call(kernel, outs, scratch, [own, other, resid_in, norm1, inv1, table, hid, gain], [slope], deps, flops, 8, 1)


def back_in(layer, branch, slope, w_out, small_in, w_in, norm0, inv0, deps=()):
    R, D = branch.shape
    ff = w_out.shape[0]

    def kernel(ins, outs, scratch):
        branch, slope, wout, small_in, win_h, norm0_h, inv0_h = ins
        pre, small, win, norm0, inv0 = outs
        (sems,) = scratch
        gets = [pltpu.make_async_copy(src, dst, sems.at[n]) for n, (src, dst) in enumerate(
            [(win_h.at[layer], win), (norm0_h, norm0), (inv0_h, inv0)])]
        for get in gets:
            get.start()
        small[...] = small_in[...]
        ff_back_in(R, dict(branch_low=branch, small=small, slope=slope, w_out=wout, pre_low=pre, chunk=CHUNK))
        for get in gets:
            get.wait()

    outs = [near((R, ff), bf16), near((SMALL_ROWS, D), f32), near((D, ff), bf16), near((R, D), f32), near((R, 128), f32)]
    return call(kernel, outs, [], [branch, slope, w_out, small_in], [w_in, norm0, inv0], deps, 2 * R * D * ff, 10, 3)


def back_out(layer, pre, resid_in, norm0, inv0, w_in, gain, small_in, small_upper, deps=()):
    R, D = resid_in.shape
    ff = w_in.shape[1]

    def kernel(ins, outs, scratch):
        pre, resid_in, norm0, inv0, win, gain, small_in, small_upper = ins
        mix_a, mix_b, resid, small = outs
        small[SMALL_ROWS:, :] = small_upper[...]
        small = small.at[:SMALL_ROWS]
        small[...] = small_in[...]
        ff_back_out(layer, R, dict(gain=gain, resid=resid, resid_in=resid_in, norm0=norm0, inv0=inv0, small=small, w_in=win,
                                   pre_low=pre, put_mix=halves((mix_a, mix_b), R)))

    outs = [near((R // 2, D), bf16)] * 2 + [near((R, D), f32), near((2 * SMALL_ROWS, D), f32)]
    return call(kernel, outs, [], [pre, resid_in, norm0, inv0, w_in, gain, small_in, small_upper], [], deps, 2 * R * D * ff, 6)


def mix_last(place, size, pieces, resid_in, final_low, table, hid, scale, deps=()):
    R, D = resid_in.shape

    def kernel(ins, outs, scratch):
        *pieces, resid_in, table, hid, final_low = ins
        local, low, low_final = outs
        whole, spec, grad, sems = scratch
        get = pltpu.make_async_copy(final_low, low_final, sems.at[0])
        get.start()

        def after_mix(mixed):
            grad[...] = resid_in[...] + mixed

        mix_phase(table, hid, pieces, whole, spec, R, scale, after_mix)
        cut = place.row(size)
        local[...] = grad[cut, :]
        low[...] = grad[cut, :].astype(bf16)
        get.wait()

    flops = 2 * R * D * (4 * R + 2 * D)
    return call(kernel, [near((size, D), f32)] + [near((size, D), bf16)] * 2, [((2 * R, D), bf16), ((2 * R, D), bf16), ((R, D), f32)],
                [*pieces, resid_in, table, hid], [final_low], deps, flops, 9, 1)


def gather_rows(place, block, pieces, deps=(), tables=None):
    size, D = block.shape
    R = size * place.seq_count // 2

    def kernel(ins, outs, scratch):
        rows = outs[0]
        (sems,) = scratch
        home = place.home
        if tables is not None:
            *ins, tables_h = ins
            bring = pltpu.make_async_copy(tables_h.at[place.core], outs[1], sems.at[1])
            bring.start()

        def put(ref, mask):
            rows[place.row(size, mask), :] = ref[:size, :]

        @pl.when(home)
        def _():
            own = pltpu.make_async_copy(ins[-1], rows.at[place.row(size)], sems.at[0])
            own.start()
            for ref, (home_mask, _) in zip(ins, [p[1] for p in pieces]):
                if home_mask is not None:
                    put(ref, home_mask)
            own.wait()

        @pl.when(jnp.logical_not(home))
        def _():
            for ref, (_, away_mask) in zip(ins, [p[1] for p in pieces]):
                put(ref, away_mask)

        if tables is not None:
            bring.wait()

    outs, far_args = [near((R, D), block.dtype)], [block]
    if tables is not None:
        outs.append(near(tables.shape[1:], tables.dtype))
        far_args.append(tables)
    return call(kernel, outs, [], [p[0] for p in pieces], far_args, deps, 0, 4, 2)


def send_blocks(place, block):
    odd = [m for m in range(1, place.seq_count) if parity_of(m)]
    even = [m for m in range(1, place.seq_count) if not parity_of(m)]
    pieces = []
    for n, mask in enumerate(odd):
        pairs = [((t, 1 - parity_of(t)), (t ^ mask, parity_of(t))) for t in range(place.seq_count)]
        home_mask = None
        if n < len(even):
            home_mask = even[n]
            pairs += [((t, parity_of(t)), (t ^ home_mask, parity_of(t))) for t in range(place.seq_count)]
        pieces.append((place.send(block, pairs), (home_mask, mask)))
    return pieces


class Chain:
    def __init__(self, place, grads, pieces, pad):
        self.place = place
        self.m = len(grads)
        self.masks = [g[2] for g in grads]
        self.zs = place.batch_count // 2
        self.pad = pad
        self.extra, self.more, self.z_pad = None, 0, 0
        parts = []
        for left, right, mask in grads:
            span = left.shape[1] // place.seq_count
            self.n = span // place.batch_count
            self.width = right.shape[1]
            for slot in (place.s, place.s ^ mask):
                cut = lax.dynamic_slice(left, (0, slot * span), (left.shape[0], span))
                parts.append(dot(cut, right, ((0,), (0,))).astype(bf16))
        self.parts = parts
        zs, n, D = self.zs, self.n, self.width
        self.per = 2 * self.m // pieces

        def give(ins, outs, scratch):
            core = place.core
            for i, ref in enumerate(ins):
                for z in range(zs):
                    outs[i // self.per][pl.ds((i % self.per) * zs * n + z * n, n), :] = ref[self.rows(z, 1 - core), :]

        *gives, _ = call(give, [near((self.per * zs * n, D), bf16)] * pieces, [], parts, name="give")
        self.got = [place.swap(give) for give in gives]

    def rows(self, z, core):
        return pl.ds(pl.multiple_of(z * 2 * self.n + core * self.n, 32), self.n)

    def core_done(self, deps=(), extra=None, carry=None):
        zs, n, m, D = self.zs, self.n, self.m, self.width
        place = self.place
        if extra is not None:
            self.more = extra.shape[0]
        more = self.more

        def kernel(ins, outs, scratch):
            core = place.core
            keep, *gives = outs
            if carry is not None:
                bring = pltpu.make_async_copy(ins[-1], gives.pop(), scratch[0].at[0])
                bring.start()
            if more:
                *gives, total = gives
                total[...] = ins[2 * m + len(self.got)][...]
                gives[-1][pl.ds(zs * n, more), :] = low_of(total[...])
            for i in range(2 * m):
                got = ins[2 * m + i // self.per]
                for z in range(zs):
                    cut = pl.ds(z * n, n)
                    value = ins[i][self.rows(z, core), :].astype(f32)
                    value += got[pl.ds((i % self.per) * zs * n + z * n, n), :].astype(f32)
                    if i % 2 == 0:
                        keep[i // 2, cut, :] = value
                    else:
                        gives[i // 2][cut, :] = value.astype(bf16)
            if carry is not None:
                bring.wait()

        pad = max(self.pad, more)
        outs = [near((m, zs * n, D), f32)] + [near((zs * n + pad, D), bf16)] * m
        args = self.parts + self.got
        if more:
            outs.append(near(extra.shape, f32))
            args = args + [extra]
        far_args = []
        if carry is not None:
            outs.append(near(carry.shape, carry.dtype))
            far_args = [carry]
        self.keep, *gives, self.token = call(kernel, outs, [], args, far_args, deps, 0, 4, len(far_args))
        if carry is not None:
            self.carried = gives.pop()
        if more:
            self.extra = gives.pop()
        self.got = [xor_send(give, "seq", mask) for give, mask in zip(gives, self.masks)]
        return self.token

    def seq_done(self, deps=(), carry=None):
        def read(ins):
            keep, *got = ins
            return (lambda i, cut: keep[i, cut, :] + got[i][cut, :].astype(f32)), got[-1]

        return self.z_step(0, read, [self.keep, *self.got], deps, carry)

    def z_done(self, deps=()):
        def read(ins):
            keep, got = ins
            return (lambda i, cut: keep[i, cut, :] + got[pl.ds(i * keep.shape[1] + cut.start, cut.size), :].astype(f32)), got

        return self.z_step(self.bit + 1, read, [self.keep, self.got], deps)

    def z_step(self, bit, read, args, deps, carry=None):
        m, n, D = self.m, self.n, self.width
        place = self.place
        self.bit = bit
        left = self.zs >> bit
        rows = left // 2 * n
        zs_rows = left * n if bit == 0 else m * left * n

        def kernel(ins, outs, scratch):
            keep, give = outs[:2]
            if carry is not None:
                *ins, carry_h = ins
                bring = pltpu.make_async_copy(carry_h, outs[-1], scratch[0].at[0])
                bring.start()
            if self.more:
                *ins, extra = ins
            value, last = read(ins)
            if self.more:
                total = outs[2]
                total[...] = wide_of(low_of(extra[...])) + wide_of(last[pl.ds(zs_rows, self.more), :])
                give[pl.ds(m * rows, self.more), :] = low_of(total[...])
            mine = (place.z >> bit) & 1
            for i in range(m):
                for z in range(left // 2):
                    cut = pl.ds(z * n, n)
                    keep[i, cut, :] = value(i, pl.ds(pl.multiple_of((2 * z + mine) * n, 32), n))
                    other = value(i, pl.ds(pl.multiple_of((2 * z + 1 - mine) * n, 32), n))
                    give[pl.ds(i * rows + z * n, n), :] = other.astype(bf16)
            if carry is not None:
                bring.wait()

        outs = [near((m, rows, D), f32), near((m * rows + max(self.more, self.z_pad if bit == 0 else 0), D), bf16)]
        if self.more:
            outs.append(near(self.extra.shape, f32))
            args = [*args, self.extra]
        far_args = []
        if carry is not None:
            outs.append(near(carry.shape, carry.dtype))
            far_args = [carry]
        self.keep, give, *rest, self.token = call(kernel, outs, [], args, far_args, deps, 0, 6, len(far_args))
        if carry is not None:
            self.carried = rest.pop()
        if self.more:
            self.extra = rest.pop()
        self.got = xor_send(give, "batch", 2 << bit)
        return self.token

    def last(self, deps=()):
        m, n, D = self.m, self.n, self.width

        def kernel(ins, outs, scratch):
            for i in range(m):
                outs[0][i] = ins[0][i] + ins[1][pl.ds(i * n, n), :].astype(f32)

        self.total, self.token = call(kernel, [near((m, n, D), f32)], [], [self.keep, self.got], (), deps)
        return self.token


def low_of(value):
    return value.astype(bf16)


def wide_of(parts):
    return parts.astype(f32)


def choose(place, grad_local, final_local, got, deps=()):
    def kernel(ins, outs, scratch):
        home = place.home
        outs[0][...] = jnp.where(home, ins[0][...], ins[2][...].astype(f32))
        outs[1][...] = jnp.where(home, ins[1][...], ins[3][...].astype(f32))

    return call(kernel, [result(grad_local.shape, f32)] * 2, [], [grad_local, final_local, *got], [], deps)


def last_out(chain, upper, index, deps=()):
    n, D = upper.shape[1:]

    def kernel(ins, outs, scratch):
        keep, got, upper = ins
        outs[0][0] = keep[0] + got[:n, :].astype(f32)
        outs[0][1] = upper[index]

    return call(kernel, [result((2, n, D), f32)], [], [chain.keep, chain.got, upper], (), deps)


def small_over_cores(place, values, deps=()):
    def kernel(ins, outs, scratch):
        outs[0][...] = ins[0][...] + ins[1][...]

    return call(kernel, [near(values.shape, f32)], [], [values, place.swap(values)], (), deps)


def last_out_and_small(chain, upper, index, ff, deps=()):
    n, D = upper.shape[1:]
    rows = chain.extra.shape[0]

    def kernel(ins, outs, scratch):
        keep, got, upper, mine = ins
        weight, gains, biases, bins, bouts = outs
        weight[0] = keep[0] + got[:n, :].astype(f32)
        weight[1] = upper[index]
        total = wide_of(low_of(mine[...])) + wide_of(got[pl.ds(n, rows), :])
        for layer in range(2):
            part = total[layer * SMALL_ROWS : (layer + 1) * SMALL_ROWS]
            gains[layer] = part[0:2]
            biases[layer] = part[2:4]
            bouts[layer : layer + 1, :] = part[4:5]
            for k in range(ff // D):
                bins[layer : layer + 1, k * D : (k + 1) * D] = part[5 + k : 6 + k]

    outs = [result((2, n, D), f32), result((2, 2, D), f32), result((2, 2, D), f32), result((2, ff), f32), result((2, D), f32)]
    return call(kernel, outs, [], [chain.keep, chain.got, upper, chain.extra], (), deps)


def body(tables, hid_table, inputs, norm_gain, norm_bias, w_in, b_in, w_out, b_out, cotangent):
    place = Place()
    size = inputs.shape[1]
    width = inputs.shape[2]
    length = size * place.seq_count
    scale = 1.0 / math.sqrt(length * width)
    hid = jnp.asarray(hid_table)
    tables = jnp.asarray(tables)
    span = w_in.shape[2] // (place.seq_count * place.batch_count)
    if length != 2 * STEP or span % 32 or w_in.shape[0] != 2 or place.batch_count != 8 or w_in.shape[2] % FF_CUT:
        table = lax.dynamic_index_in_dim(tables, place.core, 0, keepdims=False)
        return plain_body(table, hid, inputs, norm_gain, norm_bias, w_in, b_in, w_out, b_out, cotangent)

    pieces = send_blocks(place, inputs[0])
    cot_low = cotangent[0].astype(bf16)
    cot_send = jnp.pad(cot_low, ((0, 16), (0, 0)))
    table, hid, params, win0, wout0, tok = load(place, tables, hid, (norm_gain, norm_bias, b_in, b_out), w_in, w_out)
    norm_gain = params[0]
    own, tok = gather_rows(place, inputs[0], pieces, (tok, cot_send))
    cot_pieces = send_blocks(place, cot_send)
    other = place.swap(own)
    state_a, state_b, act0, slope0, hlow0, norm00, inv00, norm01_far, inv01_far, tok = forward_first(
        own, other, table, hid, win0, wout0, params, scale, (tok,))
    others = [place.swap(half) for half in (state_a, state_b)]
    final_local, final_low, act1, hlow1, branch1, pre1, mix1, resid1, small1, tok = forward_back_last(
        place, size, 1, [state_a, state_b, *others], norm01_far, cot_low, cot_pieces, tables, hid, w_in, w_out, params, scale, (tok,))
    mix1_other = place.swap(mix1)
    grads1 = Chain(place, [(act1, branch1, 1), (pre1, hlow1, 2)], 4, 0)
    norm01, inv01, wout0, tok = load_back(0, norm01_far, inv01_far, w_out, (tok,))
    tok = grads1.core_done((tok,))
    branch0, resid0, small0, slope0, tok = back_norm(
        0, mix1, mix1_other, resid1, norm01, inv01, table, hid, norm_gain, slope0, scale, (tok,))
    out0 = Chain(place, [(act0, branch0, 1)], 2, 16)
    pre0, small0, win0, norm00, inv00, tok = back_in(0, branch0, slope0, wout0, small0, w_in, norm00, inv00, (tok,))
    mix_a, mix_b, resid0, small0, tok = back_out(0, pre0, resid0, norm00, inv00, win0, norm_gain, small0, small1, (tok,))
    others = [place.swap(half) for half in (mix_a, mix_b)]
    grads1.z_pad = 0
    tok = grads1.seq_done((tok,))
    small, tok = small_over_cores(place, small0, (tok,))
    tok = out0.core_done((tok,), small, hlow0)
    in0 = Chain(place, [(pre0, out0.carried, 2)], 2, 0)
    tok = in0.core_done((tok,))
    grad_local, low, low_final, tok = mix_last(
        place, size, [mix_a, mix_b, *others], resid0, final_low, table, hid, scale, (tok,))
    back = [place.send_back(low), place.send_back(low_final)]
    tok = out0.seq_done((tok,))
    tok = grads1.z_done((tok,))
    tok = in0.seq_done((tok,))
    tok = out0.z_done((tok,))
    tok = grads1.last((tok,))
    tok = in0.z_done((tok,))
    input_grad, outputs, tok = choose(place, grad_local, final_local, back, (tok,))
    wout, gains, biases, bin_, bout, tok = last_out_and_small(out0, grads1.total, 0, w_in.shape[2], (tok,))
    win, tok = last_out(in0, grads1.total, 1, (tok,))
    return (outputs[None], input_grad[None], gains, biases, jnp.swapaxes(win, 1, 2), bin_, wout, bout)


def solution(mesh):
    def run(inputs, norm_gain, norm_bias, w_in, b_in, w_out, b_out, cotangent):
        tables = seq_tables(inputs.shape[1], mesh.shape["seq"])
        cos_hid, sin_hid = np_tables(inputs.shape[2])
        hid_table = np.concatenate([cos_hid, -sin_hid], axis=0)

        def inner(*args):
            return body(tables, hid_table, *args)

        return jax.shard_map(
            inner,
            mesh=mesh,
            in_specs=(P("batch", "seq", None), P(), P(), P(), P(), P(), P(), P("batch", "seq", None)),
            out_specs=(
                P("batch", "seq", None),
                P("batch", "seq", None),
                P(),
                P(),
                P(None, None, ("seq", "batch")),
                P(),
                P(None, ("seq", "batch"), None),
                P(),
            ),
            check_vma=False,
        )(inputs, norm_gain, norm_bias, w_in, b_in, w_out, b_out, cotangent)

    return run
```
